128 devices in a mesh: band: 64 (over z, y, x), head: 2 (over core).
Axes of the slice: x: 4, y: 4, z: 4, core: 2. Of those that a mesh axis runs over, the one named last changes fastest.
Arguments:
- grid_in: bfloat16 [262144, 128], P('band'), may hold values from -6 to 6
- mesh_in: bfloat16 [16384, 1024], P('band'), may hold values from -6 to 6
- counts: int32 [64], replicated, may hold values from 1 to 256, 12288 in all
- enc_edges: int32 [12, 16384], P(None, 'band'), may hold values from 0 to 262143, as said below
- enc_bias: float32 [12, 16, 16384], P(None, 'head', 'band'), may hold values from -90 to 160
- proc_bias: float32 [257, 16, 16384], P(None, 'head', 'band'), may hold values from -90 to 160
- w_embed: bfloat16 [128, 1024], replicated, may hold values from -0.5 to 0.5
- enc_query: bfloat16 [1024, 1024], P(None, 'head'), may hold values from -0.1875 to 0.1875
- enc_key: bfloat16 [1024, 1024], P(None, 'head'), may hold values from -0.1875 to 0.1875
- enc_value: bfloat16 [1024, 1024], P(None, 'head'), may hold values from -0.1875 to 0.1875
- enc_out: bfloat16 [1024, 1024], replicated, may hold values from -0.1875 to 0.1875
- proc_query: bfloat16 [1024, 1024], P(None, 'head'), may hold values from -0.1875 to 0.1875
- proc_key: bfloat16 [1024, 1024], P(None, 'head'), may hold values from -0.1875 to 0.1875
- proc_value: bfloat16 [1024, 1024], P(None, 'head'), may hold values from -0.1875 to 0.1875
- proc_out: bfloat16 [1024, 1024], P('head'), may hold values from -0.1875 to 0.1875
- mlp_gate: bfloat16 [1024, 4096], P(None, 'head'), may hold values from -0.1875 to 0.1875
- mlp_up: bfloat16 [1024, 4096], P(None, 'head'), may hold values from -0.1875 to 0.1875
- mlp_down: bfloat16 [4096, 1024], P('head'), may hold values from -0.09375 to 0.09375
Outputs:
- mesh_out: bfloat16 [16384, 1024], P('band')
The draws below stay inside these ranges and needn't reach their ends.
Inputs may be any that keep to these rules, and one draw needn't show every extreme that they name: The live mesh nodes of band b are its first counts[b] slots; some band is full. `enc_edges`: A node of band b = n // 256 has its grid neighbours among grid points (b - 1) * 4096 to (b + 2) * 4096 - 1; in every band some edge reaches each end of that range that lies inside the grid.
All inputs are finite; a program needn't handle non-finite values.
Results may differ from the reference program's by a relative error of at most 0.02.
Values may be sent and summed in bfloat16 or wider, within the bound.
A program may use at most 192 MiB of HBM per device.

```python
import math
import jax
import jax.numpy as jnp
import numpy as np
from jax import lax

D = 1024
HEADS = 16
HDIM = 64
FF = 4096
C_IN = 128
K_ENC = 12
W = 128
M_DEV = 256
G_DEV = 4096
BANDS = 64
MESH = 16384
GRID = 262144
WIN = 257
N_HEAD = 2


def draw_enc_edges(key, part):
    key = jax.random.fold_in(key, 11)
    node_index = jnp.arange(MESH, dtype=jnp.int32)
    band_index = node_index // M_DEV
    slot_index = node_index % M_DEV
    centre = band_index * G_DEV + slot_index * (G_DEV - 1) // max(M_DEV - 1, 1)
    offsets = jax.random.randint(key, (K_ENC, MESH), -G_DEV, G_DEV + 1, dtype=jnp.int32)
    first_row = jnp.where(slot_index == 0, -G_DEV, offsets[0])
    second_row = jnp.where(slot_index == M_DEV - 1, G_DEV, offsets[1])
    offsets = jnp.concatenate([first_row[None], second_row[None], offsets[2:]], 0)
    return jnp.clip(centre[None, :] + offsets, 0, GRID - 1).astype(jnp.int32)


def draw_enc_bias(key, part):
    key = jax.random.fold_in(key, 23)
    array_dims = (K_ENC, HEADS, MESH)
    return jnp.clip(jax.random.normal(key, array_dims, jnp.float32), -4.0, 4.0)


def draw_proc_bias(key, part):
    key = jax.random.fold_in(key, 37)
    array_dims = (WIN, HEADS, MESH)
    return jnp.clip(jax.random.normal(key, array_dims, jnp.float32), -4.0, 4.0)


def block_levels(own_key, shape, cuts, low, top_value):
    gain, own = 1.0, jax.random.fold_in(own_key, 6)
    for dim, parts in cuts:
        steps = jnp.exp(jax.random.uniform(jax.random.fold_in(own, dim), (parts,), jnp.float32, low / len(cuts), top_value / len(cuts)))
        gain = gain * jnp.repeat(steps, shape[dim] // parts).reshape([-1 if axis == dim else 1 for axis in range(len(shape))])
    return gain


def length_profile(amount, total, bound, skew):
    loads = [(1 << 20) // math.isqrt(rank ** skew) + 1 for rank in range(2, amount + 1)]
    rest, given = total - bound - (amount - 1), [1] * (amount - 1)
    while rest > 0:
        movable = [i for i in range(amount - 1) if given[i] < bound]
        whole, left = sum([loads[i] for i in movable]), rest
        for i in movable:
            extra = min(bound - given[i], max(1, left * loads[i] // whole), rest)
            given[i] = given[i] + extra
            rest = rest - extra
    return np.array([bound] + given)


def uneven(key, count, total, bound, skew):
    if count == 2:
        one = jax.random.randint(key, (), max(1, total - bound), min(bound, total - 1) + 1)
        return jnp.stack([one, total - one])
    lengths = jnp.asarray(length_profile(count, total, bound, skew), jnp.int32)
    twos = (count - 1) // 2
    giver, taker = lengths[1:1 + 2 * twos:2], lengths[2:2 + 2 * twos:2]
    margin = jnp.minimum(giver - 1, bound - taker)
    shifted = jax.random.randint(jax.random.fold_in(key, 1), (twos,), 0, 1 << 20) % (margin + 1)
    lengths = lengths.at[1:1 + 2 * twos:2].set(giver - shifted).at[2:2 + 2 * twos:2].set(taker + shifted)
    return lengths[jax.random.permutation(jax.random.fold_in(key, 2), count)]


def scatter_about(rng, dims, width, bound, cuts=(), held_as=jnp.bfloat16):
    drawn = width * jax.random.normal(rng, dims, jnp.float32)
    if cuts:
        drawn = drawn * block_levels(rng, dims, cuts, -0.22, 0.18)
    return jnp.clip(drawn, -bound, bound).astype(held_as)


def setup_inputs(seed: int = 0) -> dict:
    arg_keys = jax.random.split(jax.random.key(seed), 19)
    return {
        "grid_in": scatter_about(arg_keys[0], (GRID, C_IN), 1.0, 6.0, ((0, 64),)),
        "mesh_in": scatter_about(arg_keys[1], (MESH, D), 1.0, 6.0, ((0, 64),)),
        "counts": uneven(arg_keys[2], BANDS, 3 * BANDS * M_DEV // 4, M_DEV, 2).astype(jnp.int32),
        "enc_edges": draw_enc_edges(jax.random.fold_in(arg_keys[18], 71), 0),
        "enc_bias": draw_enc_bias(jax.random.fold_in(arg_keys[18], 71), 0),
        "proc_bias": draw_proc_bias(jax.random.fold_in(arg_keys[18], 71), 0),
        "w_embed": scatter_about(arg_keys[6], (C_IN, D), C_IN ** -0.5, 0.5),
        "enc_query": scatter_about(arg_keys[7], (D, D), D ** -0.5, 0.1875, ((1, 2),)),
        "enc_key": scatter_about(arg_keys[8], (D, D), D ** -0.5, 0.1875, ((1, 2),)),
        "enc_value": scatter_about(arg_keys[9], (D, D), D ** -0.5, 0.1875, ((1, 2),)),
        "enc_out": scatter_about(arg_keys[10], (D, D), D ** -0.5, 0.1875),
        "proc_query": scatter_about(arg_keys[11], (D, D), D ** -0.5, 0.1875, ((1, 2),)),
        "proc_key": scatter_about(arg_keys[12], (D, D), D ** -0.5, 0.1875, ((1, 2),)),
        "proc_value": scatter_about(arg_keys[13], (D, D), D ** -0.5, 0.1875, ((1, 2),)),
        "proc_out": scatter_about(arg_keys[14], (D, D), D ** -0.5, 0.1875, ((0, 2),)),
        "mlp_gate": scatter_about(arg_keys[15], (D, FF), D ** -0.5, 0.1875, ((1, 2),)),
        "mlp_up": scatter_about(arg_keys[16], (D, FF), D ** -0.5, 0.1875, ((1, 2),)),
        "mlp_down": scatter_about(arg_keys[17], (FF, D), FF ** -0.5, 0.09375, ((0, 2),)),
    }


EPSILON = 1e-05
NEGATIVE = -1e+30

def normalize(source_rows):
    values_f = source_rows.astype(jnp.float32)
    centred = values_f - lax.optimization_barrier(jnp.mean(values_f, -1, keepdims=True))
    variance = lax.optimization_barrier(jnp.mean(centred * centred, -1, keepdims=True))
    return (centred * lax.rsqrt(variance + EPSILON)).astype(jnp.bfloat16)

def soft_weights(scores, usable, axis_index):
    masked = jnp.where(usable, scores, NEGATIVE)
    row_peak = lax.optimization_barrier(jnp.max(masked, axis_index, keepdims=True))
    exponent = jnp.where(usable, jnp.exp(masked - row_peak), 0.0)
    return (exponent / lax.optimization_barrier(jnp.sum(exponent, axis_index, keepdims=True))).astype(jnp.bfloat16)

def grouped_sum(pairs):
    total = jnp.zeros((pairs[0][0].shape[0], pairs[0][1].shape[1]), jnp.float32)
    for group in range(N_HEAD):
        partial_value = jnp.zeros_like(total)
        for left_part, right_part in pairs:
            share = left_part.shape[1] // N_HEAD
            partial_value = partial_value + jnp.dot(left_part[:, group * share:(group + 1) * share], right_part[group * share:(group + 1) * share], preferred_element_type=jnp.float32)
        rounded = lax.optimization_barrier(partial_value.astype(jnp.bfloat16))
        total = total + rounded.astype(jnp.float32)
    return total

def to_band(dense_scores, band_width):
    lead_dims = dense_scores.shape[:-2]
    row_count, col_count = dense_scores.shape[-2:]
    flattened = dense_scores.reshape(lead_dims + (row_count * col_count,))
    flattened = jnp.pad(flattened, [(0, 0)] * len(lead_dims) + [(0, row_count)])
    return flattened.reshape(lead_dims + (row_count, col_count + 1))[..., :band_width]

def from_band(banded, col_count):
    lead_dims = banded.shape[:-2]
    row_count, band_width = banded.shape[-2:]
    padded = jnp.pad(banded, [(0, 0)] * len(lead_dims) + [(0, 0), (0, col_count + 1 - band_width)])
    flattened = padded.reshape(lead_dims + (row_count * (col_count + 1),))[..., :row_count * col_count]
    return flattened.reshape(lead_dims + (row_count, col_count))

def reference(grid_in, mesh_in, counts, enc_edges, enc_bias, proc_bias, w_embed, enc_query, enc_key, enc_value, enc_out, proc_query, proc_key, proc_value, proc_out, mlp_gate, mlp_up, mlp_down):
    score_scale = HDIM ** (-0.5)
    embedded = jnp.dot(grid_in, w_embed, preferred_element_type=jnp.float32).astype(jnp.bfloat16)
    grid_keys = jnp.dot(embedded, enc_key, preferred_element_type=jnp.float32).astype(jnp.bfloat16)
    grid_values = jnp.dot(embedded, enc_value, preferred_element_type=jnp.float32).astype(jnp.bfloat16)
    mesh_query = jnp.dot(normalize(mesh_in), enc_query, preferred_element_type=jnp.float32).astype(jnp.bfloat16)
    mesh_query = mesh_query.reshape(MESH, HEADS, HDIM)
    near_keys = grid_keys[enc_edges].reshape(K_ENC, MESH, HEADS, HDIM)
    near_values = grid_values[enc_edges].reshape(K_ENC, MESH, HEADS, HDIM)
    scores = jnp.einsum('knhc,nhc->khn', near_keys.astype(jnp.float32), mesh_query.astype(jnp.float32))
    scores = scores * score_scale + enc_bias
    weights = soft_weights(scores, jnp.ones(scores.shape, jnp.bool_), 0)
    attended = jnp.einsum('khn,knhc->nhc', weights.astype(jnp.float32), near_values.astype(jnp.float32))
    attended = attended.astype(jnp.bfloat16).reshape(MESH, D)
    latent = (mesh_in.astype(jnp.float32) + grouped_sum(((attended, enc_out),))).astype(jnp.bfloat16)
    normed = normalize(latent)
    win_query = jnp.dot(normed, proc_query, preferred_element_type=jnp.float32).astype(jnp.bfloat16)
    win_key = jnp.dot(normed, proc_key, preferred_element_type=jnp.float32).astype(jnp.bfloat16)
    win_value = jnp.dot(normed, proc_value, preferred_element_type=jnp.float32).astype(jnp.bfloat16)
    node_index = jnp.arange(MESH, dtype=jnp.int32)
    node_live = node_index % M_DEV < counts[node_index // M_DEV]
    keys_padded = jnp.pad(win_key, ((W, W), (0, 0)))
    values_padded = jnp.pad(win_value, ((W, W), (0, 0)))

    def window_block(block_index):
        block_start = (block_index * M_DEV).astype(jnp.int32)
        block_query = lax.dynamic_slice_in_dim(win_query, block_start, M_DEV, 0).reshape(M_DEV, HEADS, HDIM)
        block_keys = lax.dynamic_slice_in_dim(keys_padded, block_start, M_DEV + 2 * W, 0)
        block_values = lax.dynamic_slice_in_dim(values_padded, block_start, M_DEV + 2 * W, 0)
        block_keys = block_keys.reshape(M_DEV + 2 * W, HEADS, HDIM)
        block_values = block_values.reshape(M_DEV + 2 * W, HEADS, HDIM)
        block_bias = lax.dynamic_slice_in_dim(proc_bias, block_start, M_DEV, 2)
        dense_scores = jnp.einsum('mhc,ehc->hme', block_query.astype(jnp.float32), block_keys.astype(jnp.float32))
        banded = to_band(dense_scores * score_scale, WIN) + jnp.transpose(block_bias, (1, 2, 0))
        key_offset = jnp.arange(WIN, dtype=jnp.int32)[None, :] - W
        key_position = block_start + jnp.arange(M_DEV, dtype=jnp.int32)[:, None] + key_offset
        inside = (key_position >= 0) & (key_position < MESH)
        clipped = jnp.clip(key_position, 0, MESH - 1)
        key_live = clipped % M_DEV < counts[clipped // M_DEV]
        usable = inside & (key_live | (key_offset == 0))
        block_weights = soft_weights(banded, usable[None], 2)
        dense_weights = from_band(block_weights, M_DEV + 2 * W)
        result = jnp.einsum('hme,ehc->mhc', dense_weights.astype(jnp.float32), block_values.astype(jnp.float32))
        return result.astype(jnp.bfloat16).reshape(M_DEV, D)
    window_out = lax.map(window_block, jnp.arange(MESH // M_DEV, dtype=jnp.int32)).reshape(MESH, D)
    gate_acts = jnp.dot(normed, mlp_gate, preferred_element_type=jnp.float32)
    up_acts = jnp.dot(normed, mlp_up, preferred_element_type=jnp.float32)
    hidden = (jax.nn.silu(gate_acts) * up_acts).astype(jnp.bfloat16)
    summed = grouped_sum(((window_out, proc_out), (hidden, mlp_down)))
    live_scale = node_live[:, None].astype(jnp.float32)
    return ((latent.astype(jnp.float32) + summed) * live_scale).astype(jnp.bfloat16)
```

```python
import jax
import jax.numpy as jnp
from jax import lax
from jax.experimental import pallas as pl
from jax.experimental.pallas import tpu as pltpu
from jax.sharding import PartitionSpec as P

HDIM = 64
EPSILON = 1e-05
NEGATIVE = -1e30
F32 = jnp.float32
BF16 = jnp.bfloat16
LANES = 128
BLOCK = 16
CHUNKS = 4
VMEM_BYTES = 60 * 1024 * 1024


def nn(left, right):
    return lax.dot_general(left, right, (((1,), (0,)), ((), ())), preferred_element_type=F32)


def nt(left, right):
    return lax.dot_general(left, right, (((1,), (1,)), ((), ())), preferred_element_type=F32)


def iota(shape, dim):
    return lax.broadcasted_iota(jnp.int32, shape, dim)


def normalize(rows):
    centred = rows - jnp.mean(rows, -1, keepdims=True)
    variance = jnp.mean(centred * centred, -1, keepdims=True)
    return (centred * lax.rsqrt(variance + EPSILON)).astype(BF16)


def kernel(
    edge_s, count_s, grid, mesh_in, enc_bias, proc_bias, w_embed,
    enc_query, enc_key, enc_value, enc_out,
    proc_query, proc_key, proc_value, proc_out, mlp_gate, mlp_up, mlp_down,
    out,
    ext, extf, mesh_v, we_v, eq_v, ek_v, ev_v, eo_v, pq_v, pk_v, pv_v, po_v,
    gate_v, up_v, down_v, eb_v, pb_v, bd, qk, wv, g, u_s, lat, nx, q_s, k_s, v_s,
    hid, part, wo, psend, precv, ob,
    load_sem, gs_sem, gr_sem, fs_sem, fr_sem, xs_sem, xr_sem, ls_sem, lr_sem,
    hs_sem, hr_sem, ps_sem, pr_sem, os_sem,
):
    band, core = lax.axis_index("band"), lax.axis_index("head")
    bands = lax.axis_size("band")
    other = 1 - core
    left = lax.rem(band + bands - 1, bands)
    right = lax.rem(band + 1, bands)
    toward = jnp.where(core == 1, right, left)
    grid_rows = grid.shape[0]
    nodes = mesh_in.shape[0]
    half = nodes // 2
    width = mesh_in.shape[1]
    local_width = enc_query.shape[1]
    local_heads = local_width // HDIM
    pairs = local_heads // 2
    edges = edge_s.shape[0]

    def mesh_id(b, h):
        return {"band": b, "head": h}

    own = pl.ds(pl.multiple_of(core * local_width, LANES), local_width)
    theirs = pl.ds(pl.multiple_of(other * local_width, LANES), local_width)
    bias_rows = enc_bias.shape[0]
    sources = [
        (mesh_in, mesh_v),
        (enc_query, eq_v),
        (w_embed, we_v),
        (enc_key, ek_v),
        (enc_value, ev_v),
        (enc_bias.at[:, pl.ds(0, half)], eb_v.at[0, pl.ds(0, bias_rows)]),
        (enc_bias.at[:, pl.ds(half, half)], eb_v.at[1, pl.ds(0, bias_rows)]),
        (proc_bias.at[:, pl.ds(0, half)], pb_v.at[0]),
        (proc_bias.at[:, pl.ds(half, half)], pb_v.at[1]),
        (grid, ext.at[pl.ds(grid_rows, grid_rows)]),
        (enc_out.at[own], eo_v.at[pl.ds(0, local_width)]),
        (enc_out.at[theirs], eo_v.at[pl.ds(local_width, local_width)]),
        (mlp_gate, gate_v),
        (mlp_up, up_v),
        (proc_query, pq_v),
        (proc_key, pk_v),
        (proc_value, pv_v),
        (mlp_down, down_v),
        (proc_out, po_v),
    ]
    loads = [
        pltpu.make_async_copy(src, dst, load_sem.at[i]) for i, (src, dst) in enumerate(sources)
    ]
    (
        l_mesh, l_eq, l_we, l_ek, l_ev, l_eb0, l_eb1, l_pb0, l_pb1, l_grid, l_eo0, l_eo1,
        l_gate, l_up, l_pq, l_pk, l_pv, l_down, l_po,
    ) = loads
    for load in loads[:9]:
        load.start()

    barrier = pltpu.get_barrier_semaphore()
    for partner in (
        mesh_id(band, other), mesh_id(left, core), mesh_id(right, core), mesh_id(toward, other)
    ):
        pl.semaphore_signal(
            barrier, inc=1, device_id=partner, device_id_type=pl.DeviceIdType.MESH
        )
    pl.semaphore_wait(barrier, 4)

    def remote(src, dst, send, recv, device):
        return pltpu.make_async_remote_copy(
            src_ref=src, dst_ref=dst, send_sem=send, recv_sem=recv,
            device_id=device, device_id_type=pl.DeviceIdType.MESH,
        )

    piece = grid_rows // 2 // CHUNKS
    halo = []
    passed = []
    for k in range(CHUNKS):
        src_row = pl.multiple_of(core * (grid_rows // 2) + k * piece, piece)
        far_row = pl.multiple_of(other * (grid_rows // 2) + k * piece, piece)
        for d, device in ((0, right), (1, left)):
            start = 2 * grid_rows * d
            slot = d * CHUNKS + k
            halo.append(
                remote(
                    grid.at[pl.ds(src_row, piece)],
                    ext.at[pl.ds(pl.multiple_of(start + src_row, piece), piece)],
                    gs_sem.at[slot], gr_sem.at[slot], mesh_id(device, core),
                )
            )
            here = ext.at[pl.ds(pl.multiple_of(start + src_row, piece), piece)]
            passed.append(
                remote(here, here, fs_sem.at[slot], fr_sem.at[slot], mesh_id(band, other))
            )
    for copy in halo:
        copy.start()
    for load in loads[9:]:
        load.start()

    padding = eb_v.shape[1] - bias_rows
    eb_v[:, pl.ds(bias_rows, padding), :] = jnp.zeros((2, padding, half), F32)
    l_mesh.wait()
    normed_mesh = normalize(mesh_v[...].astype(F32))
    l_eq.wait()
    queries = nn(normed_mesh, eq_v[...]).astype(BF16)
    queries = (queries.astype(F32) * HDIM**-0.5).astype(BF16)
    l_we.wait()
    l_ek.wait()
    key_map = nn(we_v[...], ek_v[...]).astype(BF16)
    l_ev.wait()
    wv[0] = nn(we_v[...], ev_v[...]).astype(BF16)
    l_eb0.wait()
    l_eb1.wait()
    low_half = iota((nodes, LANES), 1) < HDIM
    for h in range(local_heads):
        columns = slice(h // 2 * LANES, (h // 2 + 1) * LANES)
        keep = low_half if h % 2 == 0 else jnp.logical_not(low_half)
        masked = jnp.where(keep, queries[:, columns].astype(F32), 0.0).astype(BF16)
        mapped = nt(masked, key_map[:, columns]).astype(BF16)
        for n in range(2):
            bias = eb_v[n, pl.ds(h, 16, stride=local_heads), :]
            high = bias.astype(BF16).astype(F32)
            middle = (bias - high).astype(BF16).astype(F32)
            low = (bias - high) - middle
            lanes = jnp.concatenate([high, middle, low, jnp.zeros((LANES - 48, half), F32)], 0)
            slot = lax.rem(core + n, 2)
            qk[slot, h, :, 0:LANES] = mapped[n * half : (n + 1) * half]
            qk[slot, h, :, LANES : 2 * LANES] = lanes.T.astype(BF16)
    exchange = [
        remote(qk.at[1], qk.at[2], xs_sem.at[0], xr_sem.at[0], mesh_id(band, other)),
        remote(wv.at[0], wv.at[1], xs_sem.at[1], xr_sem.at[1], mesh_id(band, other)),
    ]
    for copy in exchange:
        copy.start()

    reach = half
    span = nodes + 2 * reach
    window = 3 * half
    own_count = count_s[band]
    lower_count = jnp.where(band > 0, count_s[left], 0)
    upper_count = jnp.where(band < bands - 1, count_s[right], 0)
    key_slot = iota((1, span), 1)
    before, after = key_slot < reach, key_slot >= reach + nodes
    limit = jnp.where(before, lower_count, jnp.where(after, upper_count, own_count))
    place = key_slot - jnp.where(before, reach - nodes, jnp.where(after, reach + nodes, reach))
    live = jnp.where(place < limit, 1, 0)
    offset = iota((half, window), 1) - iota((half, window), 0)
    in_window = (offset >= 0) & (offset <= 2 * reach)
    l_pb0.wait()
    l_pb1.wait()
    last = [pb_v[i, pl.ds(2 * reach * local_heads, local_heads), :].T for i in range(2)]

    def window_bias(h):
        for i in range(2):
            turned = pb_v[i, pl.ds(h, 2 * reach, stride=local_heads), :].T
            wide = jnp.concatenate([turned, jnp.zeros((half, window - 2 * reach), F32)], 1)
            skewed = pltpu.roll(wide, 0, 1, stride=1, stride_axis=0)
            final = last[i][:, h : h + 1]
            skewed = jnp.where(offset == 2 * reach, final, skewed)
            usable = in_window & (
                (live[:, i * half : i * half + window] > 0) | (offset == reach)
            )
            bd[h, i] = jnp.where(usable, skewed, NEGATIVE)

    def widen(k, d, which):
        start = pl.multiple_of(
            2 * grid_rows * d + which * (grid_rows // 2) + k * piece, piece
        )
        rows = pl.ds(start, piece)
        extf[rows, :] = ext[rows, :].astype(F32)

    v_s[...] = jnp.ones(v_s.shape, BF16)
    g[...] = jnp.zeros(g.shape, F32)
    l_grid.wait()
    for k in range(CHUNKS):
        for h in range(k * local_heads // CHUNKS, (k + 1) * local_heads // CHUNKS):
            window_bias(h)
        own_rows = pl.ds(grid_rows + k * 2 * piece, 2 * piece)
        extf[own_rows, :] = ext[own_rows, :].astype(F32)
        for d in range(2):
            halo[2 * k + d].wait_recv()
            passed[2 * k + d].start()
        for d in range(2):
            widen(k, d, core)
        if k > 0:
            for d in range(2):
                passed[2 * (k - 1) + d].wait_recv()
                widen(k - 1, d, other)
    for d in range(2):
        passed[2 * (CHUNKS - 1) + d].wait_recv()
        widen(CHUNKS - 1, d, other)

    base = (band - 1) * grid_rows
    blocks = half // BLOCK
    block_rows = 16 * BLOCK

    def gather(i, carry):
        block, edge = i // edges, lax.rem(i, edges)
        for n in range(BLOCK):
            row = jnp.maximum(edge_s[edge, core * half + block * BLOCK + n] - base, 0)
            g[pl.ds(block * block_rows + edge * BLOCK + n, 1), :] = extf[pl.ds(row, 1), :]
        return carry

    lax.fori_loop(0, blocks * edges, gather, 0)

    for copy in exchange:
        copy.wait()
    lane = iota((block_rows, LANES), 1)
    edge_of_row = iota((block_rows, LANES), 0) // BLOCK
    marks = (lane < 48) & (lax.rem(lane, 16) == edge_of_row)
    marks = marks.astype(F32).astype(BF16)
    ones = jnp.ones((block_rows, LANES), BF16)
    row = iota((block_rows, block_rows), 0)
    column = iota((block_rows, block_rows), 1)
    same = (lax.rem(row, BLOCK) == lax.rem(column, BLOCK)) & (column < edges * BLOCK)
    for block in range(blocks):
        rows = slice(block * BLOCK, (block + 1) * BLOCK)
        near = g[block * block_rows : (block + 1) * block_rows, :].astype(BF16)
        asked = jnp.concatenate(
            [qk[s, :, rows, :].reshape(local_heads * BLOCK, 2 * LANES) for s in (0, 2)], 0
        )
        scores = jnp.where(same, nt(asked, jnp.concatenate([near, marks], 1)), NEGATIVE)
        peak = jnp.max(scores, 1, keepdims=True)
        weights = jnp.exp(scores - peak).astype(BF16)
        mixed = nn(weights, jnp.concatenate([near, ones], 1))
        mixed = (mixed[:, :LANES] / mixed[:, LANES:]).astype(BF16)
        for h in range(2 * local_heads):
            u_s[rows, h * LANES : (h + 1) * LANES] = mixed[h * BLOCK : (h + 1) * BLOCK]
    low_lanes = iota((LANES, LANES), 1) < HDIM
    attended = []
    for pair in range(2 * pairs):
        value_map = wv[pair // pairs, :, pair % pairs * LANES : (pair % pairs + 1) * LANES]
        value_map = value_map.astype(F32)
        value_map = jnp.concatenate(
            [jnp.where(low_lanes, value_map, 0.0), jnp.where(low_lanes, 0.0, value_map)], 0
        ).astype(BF16)
        attended.append(nn(u_s[:, pair * 2 * LANES : (pair + 1) * 2 * LANES], value_map))
    attended = jnp.concatenate(attended, 1).astype(BF16)
    l_eo0.wait()
    l_eo1.wait()
    own_mesh = mesh_v[pl.ds(pl.multiple_of(core * half, half), half), :].astype(F32)
    latent = (own_mesh + nn(attended, eo_v[...])).astype(BF16)
    lat[core] = latent
    to_sibling = remote(lat.at[core], lat.at[core], ls_sem.at[0], lr_sem.at[0], mesh_id(band, other))
    to_sibling.start()
    nx[1 + core] = normalize(latent.astype(F32))
    slot = 3 * other
    sends = [
        remote(nx.at[1 + core], nx.at[slot], hs_sem.at[0], hr_sem.at[slot], mesh_id(toward, core)),
        remote(nx.at[1 + core], nx.at[slot], hs_sem.at[1], hr_sem.at[slot], mesh_id(toward, other)),
    ]
    for copy in sends:
        copy.start()
    to_sibling.wait_recv()
    nx[2 - core] = normalize(lat[other].astype(F32))
    normed = nx[1:3].reshape(nodes, width)

    l_gate.wait()
    l_up.wait()
    step = 512
    for ch in range(gate_v.shape[1] // step):
        columns = slice(ch * step, (ch + 1) * step)
        gated = nn(normed, gate_v[:, columns])
        raised = nn(normed, up_v[:, columns])
        hid[:, columns] = (0.5 * gated * (1.0 + jnp.tanh(0.5 * gated)) * raised).astype(BF16)
    l_pq.wait()
    win_query = nn(normed, pq_v[...]).astype(BF16)
    q_s[...] = (win_query.astype(F32) * HDIM**-0.5).astype(BF16)
    l_pk.wait()
    l_pv.wait()

    def keys_values(rows, source):
        k_s[rows, :] = nn(source, pk_v[...]).astype(BF16)
        values = nn(source, pv_v[...]).astype(BF16)
        for pair in range(pairs):
            v_s[rows, pair * 2 * LANES : pair * 2 * LANES + LANES] = values[
                :, pair * LANES : (pair + 1) * LANES
            ]

    keys_values(slice(reach, reach + nodes), normed)
    l_down.wait()
    for ch in range(width // step):
        columns = slice(ch * step, (ch + 1) * step)
        part[:, columns] = nn(hid[...], down_v[:, columns])

    for s, at in ((0, 0), (3, reach + nodes)):
        remote(
            nx.at[s], nx.at[s], hs_sem.at[0], hr_sem.at[s], mesh_id(toward, core)
        ).wait_recv()
        keys_values(slice(at, at + reach), nx[s])

    l_po.wait()
    results = []
    first_head = iota((half, LANES), 1) < HDIM
    for i in range(2):
        rows = slice(i * half, (i + 1) * half)
        seen = slice(i * half, i * half + window)
        for pair in range(pairs):
            columns = slice(pair * LANES, (pair + 1) * LANES)
            asked = q_s[rows, columns].astype(F32)
            keys = k_s[seen, columns]
            values = v_s[seen, pair * 2 * LANES : (pair + 1) * 2 * LANES]
            outs = []
            for h in range(2):
                keep = first_head if h == 0 else jnp.logical_not(first_head)
                masked = jnp.where(keep, asked, 0.0).astype(BF16)
                scores = nt(masked, keys) + bd[pair * 2 + h, i]
                peak = jnp.max(scores, 1, keepdims=True)
                weights = jnp.exp(scores - peak).astype(BF16)
                mixed = nn(weights, values)
                outs.append(mixed[:, :LANES] / mixed[:, LANES:])
            wo[rows, columns] = jnp.where(first_head, outs[0], outs[1]).astype(BF16)
        psend[i] = (part[rows, :] + nn(wo[rows, :], po_v[...])).astype(BF16)
        result = remote(
            psend.at[i], precv.at[i], ps_sem.at[i], pr_sem.at[i], mesh_id(band, other)
        )
        result.start()
        results.append(result)
    stores = []
    for i in range(2):
        results[i].wait_recv()
        summed = psend[i].astype(F32) + precv[i].astype(F32)
        node = iota((half, width), 0) + i * half
        scale = (node < own_count).astype(F32)
        ob[i] = ((lat[i].astype(F32) + summed) * scale).astype(BF16)
        store = pltpu.make_async_copy(ob.at[i], out.at[pl.ds(i * half, half)], os_sem.at[i])
        store.start()
        stores.append(store)
    for copy in halo + passed + [to_sibling] + sends + results:
        copy.wait_send()
    for store in stores:
        store.wait()


def local(
    grid_in, mesh_in, counts, enc_edges, enc_bias, proc_bias, w_embed, enc_query, enc_key,
    enc_value, enc_out, proc_query, proc_key, proc_value, proc_out, mlp_gate, mlp_up, mlp_down,
):
    grid_rows, channels = grid_in.shape
    nodes, width = mesh_in.shape
    local_width = enc_query.shape[1]
    heads = local_width // HDIM
    hidden = mlp_gate.shape[1]
    half = nodes // 2
    edges = enc_edges.shape[0]
    enc_bias = enc_bias.reshape(edges * heads, nodes)
    proc_bias = proc_bias.reshape(-1, nodes)
    anywhere = pl.BlockSpec(memory_space=pl.ANY)
    in_scalar = pl.BlockSpec(memory_space=pltpu.SMEM)
    dma = pltpu.SemaphoreType.DMA
    vmem = pltpu.VMEM
    scratch = [
        vmem((3 * grid_rows, channels), BF16),
        vmem((3 * grid_rows, channels), F32),
        vmem((nodes, width), BF16),
        vmem((channels, width), BF16),
        vmem((width, local_width), BF16),
        vmem((width, local_width), BF16),
        vmem((width, local_width), BF16),
        vmem((width, width), BF16),
        vmem((width, local_width), BF16),
        vmem((width, local_width), BF16),
        vmem((width, local_width), BF16),
        vmem((local_width, width), BF16),
        vmem((width, hidden), BF16),
        vmem((width, hidden), BF16),
        vmem((hidden, width), BF16),
        vmem((2, 16 * heads, half), F32),
        vmem((2, proc_bias.shape[0], half), F32),
        vmem((heads, 2, half, 3 * half), F32),
        vmem((3, heads, half, 2 * LANES), BF16),
        vmem((2, channels, local_width), BF16),
        vmem((half * 16, channels), F32),
        vmem((half, 2 * heads * channels), BF16),
        vmem((2, half, width), BF16),
        vmem((4, half, width), BF16),
        vmem((nodes, local_width), BF16),
        vmem((2 * nodes, local_width), BF16),
        vmem((2 * nodes, 2 * local_width), BF16),
        vmem((nodes, hidden), BF16),
        vmem((nodes, width), F32),
        vmem((nodes, local_width), BF16),
        vmem((2, half, width), BF16),
        vmem((2, half, width), BF16),
        vmem((2, half, width), BF16),
        dma((19,)),
        dma((2 * CHUNKS,)),
        dma((2 * CHUNKS,)),
        dma((2 * CHUNKS,)),
        dma((2 * CHUNKS,)),
        dma((2,)),
        dma((2,)),
        dma((1,)),
        dma((1,)),
        dma((2,)),
        dma((4,)),
        dma((2,)),
        dma((2,)),
        dma((2,)),
    ]
    return pl.pallas_call(
        kernel,
        out_shape=jax.ShapeDtypeStruct((nodes, width), BF16),
        in_specs=[in_scalar, in_scalar] + [anywhere] * 16,
        out_specs=anywhere,
        scratch_shapes=scratch,
        compiler_params=pltpu.CompilerParams(
            collective_id=0, has_side_effects=True, vmem_limit_bytes=VMEM_BYTES
        ),
        name="encoder_processor",
    )(
        enc_edges, counts, grid_in, mesh_in, enc_bias, proc_bias, w_embed, enc_query, enc_key,
        enc_value, enc_out, proc_query, proc_key, proc_value, proc_out, mlp_gate, mlp_up, mlp_down,
    )


def solution(mesh):
    heads = P(None, "head")
    in_specs = (
        P("band", None), P("band", None), P(), P(None, "band"), P(None, "head", "band"),
        P(None, "head", "band"), P(), heads, heads, heads, P(), heads, heads, heads,
        P("head", None), heads, heads, P("head", None),
    )
    return jax.shard_map(
        local, mesh=mesh, in_specs=in_specs, out_specs=P("band", None), check_vma=False
    )
```

```python
import jax
import jax.numpy as jnp
from jax import lax
from jax.experimental import pallas as pl
from jax.experimental.pallas import tpu as pltpu
from jax.sharding import PartitionSpec as P

HDIM = 64
EPSILON = 1e-05
NEGATIVE = -1e30
F32 = jnp.float32
BF16 = jnp.bfloat16
LANES = 128
BLOCK = 16
CHUNKS = 8
RING = 4
VMEM_BYTES = 60 * 1024 * 1024


def nn(left, right):
    return lax.dot_general(left, right, (((1,), (0,)), ((), ())), preferred_element_type=F32)


def nt(left, right):
    return lax.dot_general(left, right, (((1,), (1,)), ((), ())), preferred_element_type=F32)


def iota(shape, dim):
    return lax.broadcasted_iota(jnp.int32, shape, dim)


def normalize(rows):
    centred = rows - jnp.mean(rows, -1, keepdims=True)
    variance = jnp.mean(centred * centred, -1, keepdims=True)
    return (centred * lax.rsqrt(variance + EPSILON)).astype(BF16)


def kernel(
    count_s, enc_edges, grid, mesh_in, enc_bias, proc_bias, w_embed,
    enc_query, enc_key, enc_value, enc_out,
    proc_query, proc_key, proc_value, proc_out, mlp_gate, mlp_up, mlp_down,
    out,
    edge_s, ext, extf, mesh_v, we_v, eq_v, ek_v, ev_v, eo_v, pq_v, pk_v, pv_v, po_v,
    gate_v, up_v, down_v, eb_v, pb_v, bd, qk, vmap, apart, marks, g, u_s, lat, nx, q_s, k_s, v_s,
    hid, part, wo, psend, precv, ob,
    load_sem, gs_sem, gr_sem, fs_sem, fr_sem, xs_sem, xr_sem, ls_sem, lr_sem,
    hs_sem, hr_sem, ks_sem, kr_sem, ps_sem, pr_sem, os_sem,
):
    band, core = lax.axis_index("band"), lax.axis_index("head")
    bands = lax.axis_size("band")
    other = 1 - core
    has_left, has_right = band > 0, band < bands - 1
    left, right = jnp.maximum(band - 1, 0), jnp.minimum(band + 1, bands - 1)
    toward = jnp.where(core == 1, right, left)
    has_toward = band != toward
    grid_rows = grid.shape[0]
    nodes = mesh_in.shape[0]
    half = nodes // 2
    width = mesh_in.shape[1]
    local_width = enc_query.shape[1]
    local_heads = local_width // HDIM
    pairs = local_heads // 2
    edges = edge_s.shape[0]

    def when(condition, action):
        pl.when(condition)(action)

    def mesh_id(b, h):
        return {"band": b, "head": h}

    def ring_rows(b, start, size):
        first = lax.rem(b, RING) * grid_rows + start
        return pl.ds(pl.multiple_of(first, grid_rows // 2 // CHUNKS), size)

    own = pl.ds(pl.multiple_of(core * local_width, LANES), local_width)
    theirs = pl.ds(pl.multiple_of(other * local_width, LANES), local_width)
    bias_rows = enc_bias.shape[0]
    sources = [
        (mesh_in, mesh_v),
        (enc_edges.at[:, pl.ds(pl.multiple_of(core * half, LANES), half)], edge_s),
        (enc_query, eq_v),
        (w_embed, we_v),
        (enc_key, ek_v),
        (enc_value, ev_v),
        (enc_bias.at[:, pl.ds(0, half)], eb_v.at[0, pl.ds(0, bias_rows)]),
        (enc_bias.at[:, pl.ds(half, half)], eb_v.at[1, pl.ds(0, bias_rows)]),
        (proc_bias.at[:, pl.ds(0, half)], pb_v.at[0]),
        (proc_bias.at[:, pl.ds(half, half)], pb_v.at[1]),
        (grid, ext.at[ring_rows(band, 0, grid_rows)]),
        (enc_out.at[own], eo_v.at[pl.ds(0, local_width)]),
        (enc_out.at[theirs], eo_v.at[pl.ds(local_width, local_width)]),
        (mlp_gate, gate_v),
        (mlp_up, up_v),
        (proc_query, pq_v),
        (proc_key, pk_v),
        (proc_value, pv_v),
        (mlp_down, down_v),
        (proc_out, po_v),
    ]
    loads = [
        pltpu.make_async_copy(src, dst, load_sem.at[i]) for i, (src, dst) in enumerate(sources)
    ]
    (
        l_mesh, l_edge, l_eq, l_we, l_ek, l_ev, l_eb0, l_eb1, l_pb0, l_pb1, l_grid, l_eo0, l_eo1,
        l_gate, l_up, l_pq, l_pk, l_pv, l_down, l_po,
    ) = loads
    for load in loads[:10]:
        load.start()

    barrier = pltpu.get_barrier_semaphore()
    def greet(device):
        pl.semaphore_signal(barrier, inc=1, device_id=device, device_id_type=pl.DeviceIdType.MESH)

    greet(mesh_id(band, other))
    when(has_left, lambda: greet(mesh_id(left, core)))
    when(has_right, lambda: greet(mesh_id(right, core)))
    when(has_toward, lambda: greet(mesh_id(toward, other)))
    met = 1 + sum(jnp.where(flag, 1, 0) for flag in (has_left, has_right, has_toward))
    pl.semaphore_wait(barrier, met)

    def remote(src, dst, send, recv, device):
        return pltpu.make_async_remote_copy(
            src_ref=src, dst_ref=dst, send_sem=send, recv_sem=recv,
            device_id=device, device_id_type=pl.DeviceIdType.MESH,
        )

    piece = grid_rows // 2 // CHUNKS
    halo = []
    passed = []
    for k in range(CHUNKS):
        start = core * (grid_rows // 2) + k * piece
        for d, (target, source) in enumerate(((right, left), (left, right))):
            slot = d * CHUNKS + k
            halo.append(
                remote(
                    grid.at[pl.ds(pl.multiple_of(start, piece), piece)],
                    ext.at[ring_rows(band, start, piece)],
                    gs_sem.at[slot], gr_sem.at[slot], mesh_id(target, core),
                )
            )
            here = ext.at[ring_rows(source, start, piece)]
            passed.append(
                remote(here, here, fs_sem.at[slot], fr_sem.at[slot], mesh_id(band, other))
            )
    sides = (has_left, has_right)

    def start_all(copies):
        for copy in copies:
            copy.start()

    when(has_right, lambda: start_all(halo[0::2]))
    when(has_left, lambda: start_all(halo[1::2]))
    for load in loads[10:]:
        load.start()

    padding = eb_v.shape[1] - bias_rows
    eb_v[:, pl.ds(bias_rows, padding), :] = jnp.zeros((2, padding, half), F32)
    l_mesh.wait()
    normed_mesh = normalize(mesh_v[...].astype(F32))
    l_eq.wait()
    queries = nn(normed_mesh, eq_v[...]).astype(BF16)
    queries = (queries.astype(F32) * HDIM**-0.5).astype(BF16)
    l_we.wait()
    l_ek.wait()
    key_map = nn(we_v[...], ek_v[...]).astype(BF16)
    l_ev.wait()
    value_map = nn(we_v[...], ev_v[...])
    low_lanes = iota((LANES, LANES), 1) < HDIM
    for pair in range(pairs):
        both = value_map[:, pair * LANES : (pair + 1) * LANES]
        vmap[pair, 0:LANES, :] = jnp.where(low_lanes, both, 0.0).astype(BF16)
        vmap[pair, LANES : 2 * LANES, :] = jnp.where(low_lanes, 0.0, both).astype(BF16)
    l_eb0.wait()
    l_eb1.wait()
    low_half = iota((nodes, LANES), 1) < HDIM
    for h in range(local_heads):
        columns = slice(h // 2 * LANES, (h // 2 + 1) * LANES)
        keep = low_half if h % 2 == 0 else jnp.logical_not(low_half)
        masked = jnp.where(keep, queries[:, columns].astype(F32), 0.0).astype(BF16)
        mapped = nt(masked, key_map[:, columns]).astype(BF16)
        for n in range(2):
            bias = eb_v[n, pl.ds(h, 16, stride=local_heads), :]
            high = bias.astype(BF16).astype(F32)
            middle = (bias - high).astype(BF16).astype(F32)
            low = (bias - high) - middle
            lanes = jnp.concatenate([high, middle, low, jnp.zeros((LANES - 48, half), F32)], 0)
            slot = lax.rem(core + n, 2)
            qk[slot, h, :, 0:LANES] = mapped[n * half : (n + 1) * half]
            qk[slot, h, :, LANES : 2 * LANES] = lanes.T.astype(BF16)
    exchange = [
        remote(qk.at[1], qk.at[2], xs_sem.at[0], xr_sem.at[0], mesh_id(band, other)),
        remote(vmap.at[0:pairs], vmap.at[pairs : 2 * pairs], xs_sem.at[1], xr_sem.at[1], mesh_id(band, other)),
    ]
    for copy in exchange:
        copy.start()

    reach = half
    span = nodes + 2 * reach
    window = 3 * half
    own_count = count_s[band]
    lower_count = jnp.where(has_left, count_s[left], 0)
    upper_count = jnp.where(has_right, count_s[right], 0)
    key_slot = iota((1, span), 1)
    before, after = key_slot < reach, key_slot >= reach + nodes
    limit = jnp.where(before, lower_count, jnp.where(after, upper_count, own_count))
    place = key_slot - jnp.where(before, reach - nodes, jnp.where(after, reach + nodes, reach))
    live = jnp.where(place < limit, 1, 0)
    offset = iota((half, window), 1) - iota((half, window), 0)
    in_window = (offset >= 0) & (offset <= 2 * reach)
    l_pb0.wait()
    l_pb1.wait()
    last = [pb_v[i, pl.ds(2 * reach * local_heads, local_heads), :].T for i in range(2)]

    def window_bias(h):
        for i in range(2):
            turned = pb_v[i, pl.ds(h, 2 * reach, stride=local_heads), :].T
            wide = jnp.concatenate([turned, jnp.zeros((half, window - 2 * reach), F32)], 1)
            skewed = pltpu.roll(wide, 0, 1, stride=1, stride_axis=0)
            final = last[i][:, h : h + 1]
            skewed = jnp.where(offset == 2 * reach, final, skewed)
            usable = in_window & (
                (live[:, i * half : i * half + window] > 0) | (offset == reach)
            )
            bd[h, i] = jnp.where(usable, skewed, NEGATIVE)

    def widen(rows):
        extf[rows, :] = ext[rows, :].astype(F32)

    def arrive(k, d):
        halo[2 * k + d].wait_recv()
        passed[2 * k + d].start()
        widen(ring_rows((left, right)[d], core * (grid_rows // 2) + k * piece, piece))

    def arrive_passed(k, d):
        passed[2 * k + d].wait_recv()
        widen(ring_rows((left, right)[d], other * (grid_rows // 2) + k * piece, piece))

    blocks = half // BLOCK
    block_rows = 16 * BLOCK
    row = iota((block_rows, block_rows), 0)
    column = iota((block_rows, block_rows), 1)
    same = ((row & (BLOCK - 1)) == (column & (BLOCK - 1))) & (column < edges * BLOCK)
    apart[...] = jnp.where(same, 0.0, NEGATIVE)
    lane = iota((block_rows, LANES), 1)
    edge_of_row = iota((block_rows, LANES), 0) >> 4
    mark = (lane < 48) & ((lane & 15) == edge_of_row)
    marks[...] = jnp.where(mark, 1.0, 0.0).astype(BF16)
    v_s[...] = jnp.ones(v_s.shape, BF16)
    for block in range(blocks):
        unused = slice(block * block_rows + edges * BLOCK, (block + 1) * block_rows)
        g[unused, :] = jnp.zeros((block_rows - edges * BLOCK, LANES), F32)
    l_edge.wait()
    l_grid.wait()
    for h in range(local_heads):
        window_bias(h)
    for k in range(CHUNKS):
        widen(ring_rows(band, 2 * k * piece, 2 * piece))
        for d in range(2):
            when(sides[d], lambda k=k, d=d: arrive(k, d))
        if k > 0:
            for d in range(2):
                when(sides[d], lambda k=k, d=d: arrive_passed(k - 1, d))
    for copy in exchange:
        copy.wait()
    for d in range(2):
        when(sides[d], lambda d=d: arrive_passed(CHUNKS - 1, d))

    def gather(block):
        for edge in range(edges):
            found = []
            for n in range(BLOCK):
                row = edge_s[edge, block * BLOCK + n] & (RING * grid_rows - 1)
                found.append(extf[pl.ds(row, 1), :])
            for n in range(BLOCK):
                g[pl.ds(block * block_rows + edge * BLOCK + n, 1), :] = found[n]

    ones = jnp.ones((block_rows, LANES), BF16)
    gather(0)
    for block in range(blocks):
        if block + 1 < blocks:
            gather(block + 1)
        rows = slice(block * BLOCK, (block + 1) * BLOCK)
        near = g[block * block_rows : (block + 1) * block_rows, :].astype(BF16)
        asked = jnp.concatenate(
            [qk[s, :, rows, :].reshape(local_heads * BLOCK, 2 * LANES) for s in (0, 2)], 0
        )
        scores = nt(asked, jnp.concatenate([near, marks[...]], 1)) + apart[...]
        peak = jnp.max(scores, 1, keepdims=True)
        weights = jnp.exp(scores - peak).astype(BF16)
        mixed = nn(weights, jnp.concatenate([near, ones], 1))
        mixed = (mixed[:, :LANES] / mixed[:, LANES:]).astype(BF16)
        for h in range(2 * local_heads):
            u_s[rows, h * LANES : (h + 1) * LANES] = mixed[h * BLOCK : (h + 1) * BLOCK]
    attended = []
    for pair in range(2 * pairs):
        attended.append(nn(u_s[:, pair * 2 * LANES : (pair + 1) * 2 * LANES], vmap[pair]))
    attended = jnp.concatenate(attended, 1).astype(BF16)
    l_eo0.wait()
    l_eo1.wait()
    own_mesh = mesh_v[pl.ds(pl.multiple_of(core * half, half), half), :].astype(F32)
    latent = (own_mesh + nn(attended, eo_v[...])).astype(BF16)
    lat[core] = latent
    to_sibling = remote(lat.at[core], lat.at[core], ls_sem.at[0], lr_sem.at[0], mesh_id(band, other))
    to_sibling.start()
    nx[1 + core] = normalize(latent.astype(F32))

    quarter = half // 2

    def part_of(slot, which):
        return nx.at[slot, pl.ds(pl.multiple_of(which * quarter, quarter), quarter)]

    sends = [
        remote(
            part_of(1 + core, which), part_of(3 * other, which),
            hs_sem.at[i], hr_sem.at[3 * other], mesh_id(toward, which),
        )
        for i, which in enumerate((core, other))
    ]
    when(has_toward, lambda: start_all(sends))
    handed = [
        remote(
            part_of(s, core), part_of(s, core),
            ks_sem.at[d], kr_sem.at[d], mesh_id(band, other),
        )
        for d, s in enumerate((0, 3))
    ]

    def hand(d):
        s = 3 * d
        remote(
            part_of(s, core), part_of(s, core), hs_sem.at[0], hr_sem.at[s], mesh_id(toward, core)
        ).wait_recv()
        handed[d].start()

    def clear(s):
        nx[s] = jnp.zeros((half, width), BF16)

    when(jnp.logical_not(has_left), lambda: clear(0))
    when(jnp.logical_not(has_right), lambda: clear(3))
    to_sibling.wait_recv()
    nx[2 - core] = normalize(lat[other].astype(F32))
    normed = nx[1:3].reshape(nodes, width)

    l_gate.wait()
    l_up.wait()
    step = 512
    for ch in range(gate_v.shape[1] // step):
        columns = slice(ch * step, (ch + 1) * step)
        gated = nn(normed, gate_v[:, columns])
        raised = nn(normed, up_v[:, columns])
        hid[:, columns] = (0.5 * gated * (1.0 + jnp.tanh(0.5 * gated)) * raised).astype(BF16)
    for d in range(2):
        when(sides[d], lambda d=d: hand(d))
    l_pq.wait()
    win_query = nn(normed, pq_v[...]).astype(BF16)
    q_s[...] = (win_query.astype(F32) * HDIM**-0.5).astype(BF16)
    l_pk.wait()
    l_pv.wait()

    def keys_values(rows, source):
        k_s[rows, :] = nn(source, pk_v[...]).astype(BF16)
        values = nn(source, pv_v[...]).astype(BF16)
        for pair in range(pairs):
            v_s[rows, pair * 2 * LANES : pair * 2 * LANES + LANES] = values[
                :, pair * LANES : (pair + 1) * LANES
            ]

    keys_values(slice(reach, reach + nodes), normed)
    l_down.wait()
    for ch in range(width // step):
        columns = slice(ch * step, (ch + 1) * step)
        part[:, columns] = nn(hid[...], down_v[:, columns])

    for d in range(2):
        when(sides[d], handed[d].wait_recv)
    outer = jnp.concatenate([nx[0], nx[3]], 0)
    outer_keys = nn(outer, pk_v[...]).astype(BF16)
    outer_values = nn(outer, pv_v[...]).astype(BF16)
    for s, rows in ((0, slice(0, reach)), (1, slice(reach + nodes, span))):
        k_s[rows, :] = outer_keys[s * reach : (s + 1) * reach]
        for pair in range(pairs):
            v_s[rows, pair * 2 * LANES : pair * 2 * LANES + LANES] = outer_values[
                s * reach : (s + 1) * reach, pair * LANES : (pair + 1) * LANES
            ]

    l_po.wait()
    results = []
    first_head = iota((half, LANES), 1) < HDIM
    for i in range(2):
        rows = slice(i * half, (i + 1) * half)
        seen = slice(i * half, i * half + window)
        for pair in range(pairs):
            columns = slice(pair * LANES, (pair + 1) * LANES)
            asked = q_s[rows, columns].astype(F32)
            keys = k_s[seen, columns]
            values = v_s[seen, pair * 2 * LANES : (pair + 1) * 2 * LANES]
            outs = []
            for h in range(2):
                keep = first_head if h == 0 else jnp.logical_not(first_head)
                masked = jnp.where(keep, asked, 0.0).astype(BF16)
                scores = nt(masked, keys) + bd[pair * 2 + h, i]
                peak = jnp.max(scores, 1, keepdims=True)
                weights = jnp.exp(scores - peak).astype(BF16)
                mixed = nn(weights, values)
                outs.append(mixed[:, :LANES] / mixed[:, LANES:])
            wo[rows, columns] = jnp.where(first_head, outs[0], outs[1]).astype(BF16)
        psend[i] = (part[rows, :] + nn(wo[rows, :], po_v[...])).astype(BF16)
        result = remote(
            psend.at[i], precv.at[i], ps_sem.at[i], pr_sem.at[i], mesh_id(band, other)
        )
        result.start()
        results.append(result)
    stores = []
    for i in range(2):
        results[i].wait_recv()
        summed = psend[i].astype(F32) + precv[i].astype(F32)
        node = iota((half, width), 0) + i * half
        scale = (node < own_count).astype(F32)
        ob[i] = ((lat[i].astype(F32) + summed) * scale).astype(BF16)
        store = pltpu.make_async_copy(ob.at[i], out.at[pl.ds(i * half, half)], os_sem.at[i])
        store.start()
        stores.append(store)

    def sent(copies):
        for copy in copies:
            copy.wait_send()

    when(has_right, lambda: sent(halo[0::2] + passed[1::2] + handed[1:]))
    when(has_left, lambda: sent(halo[1::2] + passed[0::2] + handed[:1]))
    when(has_toward, lambda: sent(sends))
    sent([to_sibling] + results)
    for store in stores:
        store.wait()


def local(
    grid_in, mesh_in, counts, enc_edges, enc_bias, proc_bias, w_embed, enc_query, enc_key,
    enc_value, enc_out, proc_query, proc_key, proc_value, proc_out, mlp_gate, mlp_up, mlp_down,
):
    grid_rows, channels = grid_in.shape
    nodes, width = mesh_in.shape
    local_width = enc_query.shape[1]
    heads = local_width // HDIM
    hidden = mlp_gate.shape[1]
    half = nodes // 2
    edges = enc_edges.shape[0]
    enc_bias = enc_bias.reshape(edges * heads, nodes)
    proc_bias = proc_bias.reshape(-1, nodes)
    anywhere = pl.BlockSpec(memory_space=pl.ANY)
    in_scalar = pl.BlockSpec(memory_space=pltpu.SMEM)
    dma = pltpu.SemaphoreType.DMA
    vmem = pltpu.VMEM
    scratch = [
        pltpu.SMEM((edges, half), jnp.int32),
        vmem((RING * grid_rows, channels), BF16),
        vmem((RING * grid_rows, channels), F32),
        vmem((nodes, width), BF16),
        vmem((channels, width), BF16),
        vmem((width, local_width), BF16),
        vmem((width, local_width), BF16),
        vmem((width, local_width), BF16),
        vmem((width, width), BF16),
        vmem((width, local_width), BF16),
        vmem((width, local_width), BF16),
        vmem((width, local_width), BF16),
        vmem((local_width, width), BF16),
        vmem((width, hidden), BF16),
        vmem((width, hidden), BF16),
        vmem((hidden, width), BF16),
        vmem((2, 16 * heads, half), F32),
        vmem((2, proc_bias.shape[0], half), F32),
        vmem((heads, 2, half, 3 * half), F32),
        vmem((3, heads, half, 2 * LANES), BF16),
        vmem((heads, 2 * LANES, LANES), BF16),
        vmem((16 * BLOCK, 16 * BLOCK), F32),
        vmem((16 * BLOCK, LANES), BF16),
        vmem((half * 16, channels), F32),
        vmem((half, 2 * heads * channels), BF16),
        vmem((2, half, width), BF16),
        vmem((4, half, width), BF16),
        vmem((nodes, local_width), BF16),
        vmem((2 * nodes, local_width), BF16),
        vmem((2 * nodes, 2 * local_width), BF16),
        vmem((nodes, hidden), BF16),
        vmem((nodes, width), F32),
        vmem((nodes, local_width), BF16),
        vmem((2, half, width), BF16),
        vmem((2, half, width), BF16),
        vmem((2, half, width), BF16),
        dma((20,)),
        dma((2 * CHUNKS,)),
        dma((2 * CHUNKS,)),
        dma((2 * CHUNKS,)),
        dma((2 * CHUNKS,)),
        dma((2,)),
        dma((2,)),
        dma((1,)),
        dma((1,)),
        dma((2,)),
        dma((4,)),
        dma((2,)),
        dma((2,)),
        dma((2,)),
        dma((2,)),
        dma((2,)),
    ]
    return pl.pallas_call(
        kernel,
        out_shape=jax.ShapeDtypeStruct((nodes, width), BF16),
        in_specs=[in_scalar] + [anywhere] * 17,
        out_specs=anywhere,
        scratch_shapes=scratch,
        compiler_params=pltpu.CompilerParams(
            collective_id=0, has_side_effects=True, vmem_limit_bytes=VMEM_BYTES
        ),
        name="encoder_processor",
    )(
        counts, enc_edges, grid_in, mesh_in, enc_bias, proc_bias, w_embed, enc_query, enc_key,
        enc_value, enc_out, proc_query, proc_key, proc_value, proc_out, mlp_gate, mlp_up, mlp_down,
    )


def solution(mesh):
    heads = P(None, "head")
    in_specs = (
        P("band", None), P("band", None), P(), P(None, "band"), P(None, "head", "band"),
        P(None, "head", "band"), P(), heads, heads, heads, P(), heads, heads, heads,
        P("head", None), heads, heads, P("head", None),
    )
    return jax.shard_map(
        local, mesh=mesh, in_specs=in_specs, out_specs=P("band", None), check_vma=False
    )
```

```python
import jax
import jax.numpy as jnp
from jax import lax
from jax.experimental import pallas as pl
from jax.experimental.pallas import tpu as pltpu
from jax.sharding import PartitionSpec as P

HDIM = 64
EPSILON = 1e-05
NEGATIVE = -1e30
F32 = jnp.float32
BF16 = jnp.bfloat16
LANES = 128
BLOCK = 16
CHUNKS = 8
RING = 4
VMEM_BYTES = 60 * 1024 * 1024


def nn(left, right):
    return lax.dot_general(left, right, (((1,), (0,)), ((), ())), preferred_element_type=F32)


def nt(left, right):
    return lax.dot_general(left, right, (((1,), (1,)), ((), ())), preferred_element_type=F32)


def iota(shape, dim):
    return lax.broadcasted_iota(jnp.int32, shape, dim)


def normalize(rows):
    centred = rows - jnp.mean(rows, -1, keepdims=True)
    variance = jnp.mean(centred * centred, -1, keepdims=True)
    return (centred * lax.rsqrt(variance + EPSILON)).astype(BF16)


def kernel(
    count_s, enc_edges, grid, mesh_in, enc_bias, proc_bias, w_embed,
    enc_query, enc_key, enc_value, enc_out,
    proc_query, proc_key, proc_value, proc_out, mlp_gate, mlp_up, mlp_down,
    out,
    edge_s, ext, extf, mesh_v, we_v, eq_v, ek_v, ev_v, eo_v, pq_v, pk_v, pv_v, po_v,
    gate_v, up_v, down_v, eb_v, pb_v, bd, qk, vmap, apart, marks, g, u_s, lat, nx, q_s, k_s, v_s,
    hid, part, wo, psend, precv,
    load_sem, gs_sem, gr_sem, fs_sem, fr_sem, xs_sem, xr_sem, ls_sem, lr_sem,
    hs_sem, hr_sem, ks_sem, kr_sem, ps_sem, pr_sem,
):
    band, core = lax.axis_index("band"), lax.axis_index("head")
    bands = lax.axis_size("band")
    other = 1 - core
    has_left, has_right = band > 0, band < bands - 1
    left, right = jnp.maximum(band - 1, 0), jnp.minimum(band + 1, bands - 1)
    toward = jnp.where(core == 1, right, left)
    has_toward = band != toward
    grid_rows = grid.shape[0]
    nodes = mesh_in.shape[0]
    half = nodes // 2
    width = mesh_in.shape[1]
    local_width = enc_query.shape[1]
    local_heads = local_width // HDIM
    pairs = local_heads // 2
    edges = edge_s.shape[0]

    def when(condition, action):
        pl.when(condition)(action)

    def mesh_id(b, h):
        return {"band": b, "head": h}

    def ring_rows(b, start, size):
        first = lax.rem(b, RING) * grid_rows + start
        return pl.ds(pl.multiple_of(first, grid_rows // 2 // CHUNKS), size)

    own = pl.ds(pl.multiple_of(core * local_width, LANES), local_width)
    theirs = pl.ds(pl.multiple_of(other * local_width, LANES), local_width)
    bias_rows = enc_bias.shape[0]
    sources = [
        (mesh_in, mesh_v),
        (enc_edges.at[:, pl.ds(pl.multiple_of(core * half, LANES), half)], edge_s),
        (enc_query, eq_v),
        (w_embed, we_v),
        (enc_key, ek_v),
        (enc_value, ev_v),
        (enc_bias.at[:, pl.ds(0, half)], eb_v.at[0, pl.ds(0, bias_rows)]),
        (enc_bias.at[:, pl.ds(half, half)], eb_v.at[1, pl.ds(0, bias_rows)]),
        (proc_bias.at[:, pl.ds(0, half)], pb_v.at[0]),
        (proc_bias.at[:, pl.ds(half, half)], pb_v.at[1]),
        (grid, ext.at[ring_rows(band, 0, grid_rows)]),
        (enc_out.at[own], eo_v.at[pl.ds(0, local_width)]),
        (enc_out.at[theirs], eo_v.at[pl.ds(local_width, local_width)]),
        (mlp_gate, gate_v),
        (mlp_up, up_v),
        (proc_query, pq_v),
        (proc_key, pk_v),
        (proc_value, pv_v),
        (mlp_down, down_v),
        (proc_out, po_v),
    ]
    loads = [
        pltpu.make_async_copy(src, dst, load_sem.at[i]) for i, (src, dst) in enumerate(sources)
    ]
    (
        l_mesh, l_edge, l_eq, l_we, l_ek, l_ev, l_eb0, l_eb1, l_pb0, l_pb1, l_grid, l_eo0, l_eo1,
        l_gate, l_up, l_pq, l_pk, l_pv, l_down, l_po,
    ) = loads
    for load in loads[:10]:
        load.start()

    barrier = pltpu.get_barrier_semaphore()
    def greet(device):
        pl.semaphore_signal(barrier, inc=1, device_id=device, device_id_type=pl.DeviceIdType.MESH)

    greet(mesh_id(band, other))
    when(has_left, lambda: greet(mesh_id(left, core)))
    when(has_right, lambda: greet(mesh_id(right, core)))
    when(has_toward, lambda: greet(mesh_id(toward, other)))
    met = 1 + sum(jnp.where(flag, 1, 0) for flag in (has_left, has_right, has_toward))
    pl.semaphore_wait(barrier, met)

    def remote(src, dst, send, recv, device):
        return pltpu.make_async_remote_copy(
            src_ref=src, dst_ref=dst, send_sem=send, recv_sem=recv,
            device_id=device, device_id_type=pl.DeviceIdType.MESH,
        )

    piece = grid_rows // 2 // CHUNKS
    halo = []
    passed = []
    for k in range(CHUNKS):
        start = core * (grid_rows // 2) + k * piece
        for d, (target, source) in enumerate(((right, left), (left, right))):
            slot = d * CHUNKS + k
            halo.append(
                remote(
                    grid.at[pl.ds(pl.multiple_of(start, piece), piece)],
                    ext.at[ring_rows(band, start, piece)],
                    gs_sem.at[slot], gr_sem.at[slot], mesh_id(target, core),
                )
            )
            here = ext.at[ring_rows(source, start, piece)]
            passed.append(
                remote(here, here, fs_sem.at[slot], fr_sem.at[slot], mesh_id(band, other))
            )
    sides = (has_left, has_right)

    def start_all(copies):
        for copy in copies:
            copy.start()

    when(has_right, lambda: start_all(halo[0::2]))
    when(has_left, lambda: start_all(halo[1::2]))
    for load in loads[10:]:
        load.start()

    padding = eb_v.shape[1] - bias_rows
    eb_v[:, pl.ds(bias_rows, padding), :] = jnp.zeros((2, padding, half), F32)
    l_mesh.wait()
    normed_mesh = normalize(mesh_v[...].astype(F32))
    l_eq.wait()
    queries = nn(normed_mesh, eq_v[...]).astype(BF16)
    queries = (queries.astype(F32) * HDIM**-0.5).astype(BF16)
    l_we.wait()
    l_ek.wait()
    key_map = nn(we_v[...], ek_v[...]).astype(BF16)
    l_ev.wait()
    value_map = nn(we_v[...], ev_v[...])
    low_lanes = iota((LANES, LANES), 1) < HDIM
    for pair in range(pairs):
        both = value_map[:, pair * LANES : (pair + 1) * LANES]
        vmap[pair, 0:LANES, :] = jnp.where(low_lanes, both, 0.0).astype(BF16)
        vmap[pair, LANES : 2 * LANES, :] = jnp.where(low_lanes, 0.0, both).astype(BF16)
    l_eb0.wait()
    l_eb1.wait()
    low_half = iota((nodes, LANES), 1) < HDIM
    for h in range(local_heads):
        columns = slice(h // 2 * LANES, (h // 2 + 1) * LANES)
        keep = low_half if h % 2 == 0 else jnp.logical_not(low_half)
        masked = jnp.where(keep, queries[:, columns].astype(F32), 0.0).astype(BF16)
        mapped = nt(masked, key_map[:, columns]).astype(BF16)
        for n in range(2):
            bias = eb_v[n, pl.ds(h, 16, stride=local_heads), :]
            high = bias.astype(BF16).astype(F32)
            middle = (bias - high).astype(BF16).astype(F32)
            low = (bias - high) - middle
            lanes = jnp.concatenate([high, middle, low, jnp.zeros((LANES - 48, half), F32)], 0)
            slot = lax.rem(core + n, 2)
            qk[slot, h, :, 0:LANES] = mapped[n * half : (n + 1) * half]
            qk[slot, h, :, LANES : 2 * LANES] = lanes.T.astype(BF16)
    exchange = [
        remote(qk.at[1], qk.at[2], xs_sem.at[0], xr_sem.at[0], mesh_id(band, other)),
        remote(vmap.at[0:pairs], vmap.at[pairs : 2 * pairs], xs_sem.at[1], xr_sem.at[1], mesh_id(band, other)),
    ]
    for copy in exchange:
        copy.start()

    reach = half
    span = nodes + 2 * reach
    window = 3 * half
    own_count = count_s[band]
    lower_count = jnp.where(has_left, count_s[left], 0)
    upper_count = jnp.where(has_right, count_s[right], 0)
    key_slot = iota((1, span), 1)
    before, after = key_slot < reach, key_slot >= reach + nodes
    limit = jnp.where(before, lower_count, jnp.where(after, upper_count, own_count))
    place = key_slot - jnp.where(before, reach - nodes, jnp.where(after, reach + nodes, reach))
    live = jnp.where(place < limit, 1, 0)
    offset = iota((half, window), 1) - iota((half, window), 0)
    in_window = (offset >= 0) & (offset <= 2 * reach)
    l_pb0.wait()
    l_pb1.wait()
    last = [pb_v[i, pl.ds(2 * reach * local_heads, local_heads), :].T for i in range(2)]

    def window_bias(h):
        for i in range(2):
            turned = pb_v[i, pl.ds(h, 2 * reach, stride=local_heads), :].T
            wide = jnp.concatenate([turned, jnp.zeros((half, window - 2 * reach), F32)], 1)
            skewed = pltpu.roll(wide, 0, 1, stride=1, stride_axis=0)
            final = last[i][:, h : h + 1]
            skewed = jnp.where(offset == 2 * reach, final, skewed)
            usable = in_window & (
                (live[:, i * half : i * half + window] > 0) | (offset == reach)
            )
            bd[h // 2, i, h % 2 * half : (h % 2 + 1) * half] = jnp.where(usable, skewed, NEGATIVE)

    def widen(rows):
        extf[rows, :] = ext[rows, :].astype(F32)

    def arrive(k, d):
        halo[2 * k + d].wait_recv()
        passed[2 * k + d].start()
        widen(ring_rows((left, right)[d], core * (grid_rows // 2) + k * piece, piece))

    def arrive_passed(k, d):
        passed[2 * k + d].wait_recv()
        widen(ring_rows((left, right)[d], other * (grid_rows // 2) + k * piece, piece))

    blocks = half // BLOCK
    block_rows = 16 * BLOCK
    row = iota((block_rows, block_rows), 0)
    column = iota((block_rows, block_rows), 1)
    same = ((row & (BLOCK - 1)) == (column & (BLOCK - 1))) & (column < edges * BLOCK)
    apart[...] = jnp.where(same, 0.0, NEGATIVE)
    lane = iota((block_rows, LANES), 1)
    edge_of_row = iota((block_rows, LANES), 0) >> 4
    mark = (lane < 48) & ((lane & 15) == edge_of_row)
    marks[...] = jnp.where(mark, 1.0, 0.0).astype(BF16)
    v_s[...] = jnp.ones(v_s.shape, BF16)
    for block in range(blocks):
        unused = slice(block * block_rows + edges * BLOCK, (block + 1) * block_rows)
        g[unused, :] = jnp.zeros((block_rows - edges * BLOCK, LANES), F32)
    l_edge.wait()
    l_grid.wait()
    for h in range(local_heads):
        window_bias(h)
    for k in range(CHUNKS):
        widen(ring_rows(band, 2 * k * piece, 2 * piece))
        for d in range(2):
            when(sides[d], lambda k=k, d=d: arrive(k, d))
        if k > 0:
            for d in range(2):
                when(sides[d], lambda k=k, d=d: arrive_passed(k - 1, d))
    for copy in exchange:
        copy.wait()
    for d in range(2):
        when(sides[d], lambda d=d: arrive_passed(CHUNKS - 1, d))

    def gather(block):
        for edge in range(edges):
            found = []
            for n in range(BLOCK):
                row = edge_s[edge, block * BLOCK + n] & (RING * grid_rows - 1)
                found.append(extf[pl.ds(row, 1), :])
            for n in range(BLOCK):
                g[pl.ds(block * block_rows + edge * BLOCK + n, 1), :] = found[n]

    ones = jnp.ones((block_rows, LANES), BF16)
    gather(0)
    for block in range(blocks):
        if block + 1 < blocks:
            gather(block + 1)
        rows = slice(block * BLOCK, (block + 1) * BLOCK)
        near = g[block * block_rows : (block + 1) * block_rows, :].astype(BF16)
        asked = jnp.concatenate(
            [qk[s, :, rows, :].reshape(local_heads * BLOCK, 2 * LANES) for s in (0, 2)], 0
        )
        scores = nt(asked, jnp.concatenate([near, marks[...]], 1)) + apart[...]
        peak = jnp.max(scores, 1, keepdims=True)
        weights = jnp.exp(scores - peak).astype(BF16)
        mixed = nn(weights, jnp.concatenate([near, ones], 1))
        mixed = (mixed[:, :LANES] / mixed[:, LANES:]).astype(BF16)
        for h in range(2 * local_heads):
            u_s[rows, h * LANES : (h + 1) * LANES] = mixed[h * BLOCK : (h + 1) * BLOCK]
    attended = []
    for pair in range(2 * pairs):
        attended.append(nn(u_s[:, pair * 2 * LANES : (pair + 1) * 2 * LANES], vmap[pair]))
    attended = jnp.concatenate(attended, 1).astype(BF16)
    l_eo0.wait()
    l_eo1.wait()
    own_mesh = mesh_v[pl.ds(pl.multiple_of(core * half, half), half), :].astype(F32)
    latent = (own_mesh + nn(attended, eo_v[...])).astype(BF16)
    lat[core] = latent
    to_sibling = remote(lat.at[core], lat.at[core], ls_sem.at[0], lr_sem.at[0], mesh_id(band, other))
    to_sibling.start()
    nx[1 + core] = normalize(latent.astype(F32))

    quarter = half // 2

    def part_of(slot, which):
        return nx.at[slot, pl.ds(pl.multiple_of(which * quarter, quarter), quarter)]

    sends = [
        remote(
            part_of(1 + core, which), part_of(3 * other, which),
            hs_sem.at[i], hr_sem.at[3 * other], mesh_id(toward, which),
        )
        for i, which in enumerate((core, other))
    ]
    when(has_toward, lambda: start_all(sends))
    handed = [
        remote(
            part_of(s, core), part_of(s, core),
            ks_sem.at[d], kr_sem.at[d], mesh_id(band, other),
        )
        for d, s in enumerate((0, 3))
    ]

    def hand(d):
        s = 3 * d
        remote(
            part_of(s, core), part_of(s, core), hs_sem.at[0], hr_sem.at[s], mesh_id(toward, core)
        ).wait_recv()
        handed[d].start()

    def clear(s):
        nx[s] = jnp.zeros((half, width), BF16)

    when(jnp.logical_not(has_left), lambda: clear(0))
    when(jnp.logical_not(has_right), lambda: clear(3))
    to_sibling.wait_recv()
    nx[2 - core] = normalize(lat[other].astype(F32))
    normed = nx[1:3].reshape(nodes, width)

    l_pq.wait()
    win_query = nn(normed, pq_v[...]).astype(BF16)
    win_query = win_query.astype(F32) * HDIM**-0.5
    first_head = iota((half, LANES), 1) < HDIM
    for i in range(2):
        for pair in range(pairs):
            both = win_query[i * half : (i + 1) * half, pair * LANES : (pair + 1) * LANES]
            q_s[i, pair, 0:half, :] = jnp.where(first_head, both, 0.0).astype(BF16)
            q_s[i, pair, half:nodes, :] = jnp.where(first_head, 0.0, both).astype(BF16)
    l_pk.wait()
    l_pv.wait()

    def keys_values(source, places):
        keys = nn(source, pk_v[...]).astype(BF16)
        values = nn(source, pv_v[...]).astype(BF16)
        for n, rows in enumerate(places):
            have = slice(n * half, (n + 1) * half)
            k_s[rows, :] = keys[have]
            for pair in range(pairs):
                v_s[rows, pair * 2 * LANES : pair * 2 * LANES + LANES] = values[
                    have, pair * LANES : (pair + 1) * LANES
                ]

    keys_values(normed, (slice(half, 2 * half), slice(2 * half, 3 * half)))
    l_gate.wait()
    l_up.wait()
    step = 512
    steps = gate_v.shape[1] // step
    for ch in range(steps):
        if ch == steps // 2:
            for d in range(2):
                when(sides[d], lambda d=d: hand(d))
        columns = slice(ch * step, (ch + 1) * step)
        gated = nn(normed, gate_v[:, columns])
        raised = nn(normed, up_v[:, columns])
        hid[:, columns] = (0.5 * gated * (1.0 + jnp.tanh(0.5 * gated)) * raised).astype(BF16)
    l_down.wait()
    l_po.wait()
    for d in range(2):
        when(sides[d], handed[d].wait_recv)
    outer = jnp.concatenate([nx[0], nx[3]], 0)
    keys_values(outer, (slice(0, half), slice(3 * half, 4 * half)))
    results = []
    for i in range(2):
        rows = slice(i * half, (i + 1) * half)
        seen = slice(i * half, i * half + window)
        for pair in range(pairs):
            if i == 0:
                columns = slice(pair * width // pairs, (pair + 1) * width // pairs)
                part[:, columns] = nn(hid[...], down_v[:, columns])
            columns = slice(pair * LANES, (pair + 1) * LANES)
            scores = nt(q_s[i, pair], k_s[seen, columns]) + bd[pair, i]
            peak = jnp.max(scores, 1, keepdims=True)
            weights = jnp.exp(scores - peak).astype(BF16)
            mixed = nn(weights, v_s[seen, pair * 2 * LANES : (pair + 1) * 2 * LANES])
            mixed = mixed[:, :LANES] / mixed[:, LANES:]
            wo[rows, columns] = jnp.where(first_head, mixed[:half], mixed[half:]).astype(BF16)
        psend[i] = (part[rows, :] + nn(wo[rows, :], po_v[...])).astype(BF16)
        result = remote(
            psend.at[i], precv.at[i], ps_sem.at[i], pr_sem.at[i], mesh_id(band, other)
        )
        result.start()
        results.append(result)
    for i in range(2):
        results[i].wait_recv()
        summed = psend[i].astype(F32) + precv[i].astype(F32)
        node = iota((half, width), 0) + i * half
        scale = (node < own_count).astype(F32)
        out[i * half : (i + 1) * half, :] = ((lat[i].astype(F32) + summed) * scale).astype(BF16)

    def sent(copies):
        for copy in copies:
            copy.wait_send()

    when(has_right, lambda: sent(halo[0::2] + passed[1::2] + handed[1:]))
    when(has_left, lambda: sent(halo[1::2] + passed[0::2] + handed[:1]))
    when(has_toward, lambda: sent(sends))
    sent([to_sibling] + results)


def local(
    grid_in, mesh_in, counts, enc_edges, enc_bias, proc_bias, w_embed, enc_query, enc_key,
    enc_value, enc_out, proc_query, proc_key, proc_value, proc_out, mlp_gate, mlp_up, mlp_down,
):
    grid_rows, channels = grid_in.shape
    nodes, width = mesh_in.shape
    local_width = enc_query.shape[1]
    heads = local_width // HDIM
    hidden = mlp_gate.shape[1]
    half = nodes // 2
    edges = enc_edges.shape[0]
    enc_bias = enc_bias.reshape(edges * heads, nodes)
    proc_bias = proc_bias.reshape(-1, nodes)
    anywhere = pl.BlockSpec(memory_space=pl.ANY)
    in_scalar = pl.BlockSpec(memory_space=pltpu.SMEM)
    dma = pltpu.SemaphoreType.DMA
    vmem = pltpu.VMEM
    scratch = [
        pltpu.SMEM((edges, half), jnp.int32),
        vmem((RING * grid_rows, channels), BF16),
        vmem((RING * grid_rows, channels), F32),
        vmem((nodes, width), BF16),
        vmem((channels, width), BF16),
        vmem((width, local_width), BF16),
        vmem((width, local_width), BF16),
        vmem((width, local_width), BF16),
        vmem((width, width), BF16),
        vmem((width, local_width), BF16),
        vmem((width, local_width), BF16),
        vmem((width, local_width), BF16),
        vmem((local_width, width), BF16),
        vmem((width, hidden), BF16),
        vmem((width, hidden), BF16),
        vmem((hidden, width), BF16),
        vmem((2, 16 * heads, half), F32),
        vmem((2, proc_bias.shape[0], half), F32),
        vmem((heads // 2, 2, 2 * half, 3 * half), F32),
        vmem((3, heads, half, 2 * LANES), BF16),
        vmem((heads, 2 * LANES, LANES), BF16),
        vmem((16 * BLOCK, 16 * BLOCK), F32),
        vmem((16 * BLOCK, LANES), BF16),
        vmem((half * 16, channels), F32),
        vmem((half, 2 * heads * channels), BF16),
        vmem((2, half, width), BF16),
        vmem((4, half, width), BF16),
        vmem((2, heads // 2, nodes, LANES), BF16),
        vmem((2 * nodes, local_width), BF16),
        vmem((2 * nodes, 2 * local_width), BF16),
        vmem((nodes, hidden), BF16),
        vmem((nodes, width), F32),
        vmem((nodes, local_width), BF16),
        vmem((2, half, width), BF16),
        vmem((2, half, width), BF16),
        dma((20,)),
        dma((2 * CHUNKS,)),
        dma((2 * CHUNKS,)),
        dma((2 * CHUNKS,)),
        dma((2 * CHUNKS,)),
        dma((2,)),
        dma((2,)),
        dma((1,)),
        dma((1,)),
        dma((2,)),
        dma((4,)),
        dma((2,)),
        dma((2,)),
        dma((2,)),
        dma((2,)),
    ]
    return pl.pallas_call(
        kernel,
        out_shape=pltpu.VMEM((nodes, width), BF16),
        in_specs=[in_scalar] + [anywhere] * 17,
        out_specs=pl.BlockSpec(memory_space=pltpu.VMEM),
        scratch_shapes=scratch,
        compiler_params=pltpu.CompilerParams(
            collective_id=0, has_side_effects=True, vmem_limit_bytes=VMEM_BYTES
        ),
        name="encoder_processor",
    )(
        counts, enc_edges, grid_in, mesh_in, enc_bias, proc_bias, w_embed, enc_query, enc_key,
        enc_value, enc_out, proc_query, proc_key, proc_value, proc_out, mlp_gate, mlp_up, mlp_down,
    )


def solution(mesh):
    heads = P(None, "head")
    in_specs = (
        P("band", None), P("band", None), P(), P(None, "band"), P(None, "head", "band"),
        P(None, "head", "band"), P(), heads, heads, heads, P(), heads, heads, heads,
        P("head", None), heads, heads, P("head", None),
    )
    return jax.shard_map(
        local, mesh=mesh, in_specs=in_specs, out_specs=P("band", None), check_vma=False
    )
```

```python
import jax
import jax.numpy as jnp
from jax import lax
from jax.experimental import pallas as pl
from jax.experimental.pallas import tpu as pltpu
from jax.sharding import PartitionSpec as P

HDIM = 64
EPSILON = 1e-05
NEGATIVE = -1e30
F32 = jnp.float32
BF16 = jnp.bfloat16
LANES = 128
BLOCK = 16
CHUNKS = 8
RING = 4
VMEM_BYTES = 60 * 1024 * 1024


def nn(left, right):
    return lax.dot_general(left, right, (((1,), (0,)), ((), ())), preferred_element_type=F32)


def nt(left, right):
    return lax.dot_general(left, right, (((1,), (1,)), ((), ())), preferred_element_type=F32)


def iota(shape, dim):
    return lax.broadcasted_iota(jnp.int32, shape, dim)


def normalize(rows):
    centred = rows - jnp.mean(rows, -1, keepdims=True)
    variance = jnp.mean(centred * centred, -1, keepdims=True)
    return (centred * lax.rsqrt(variance + EPSILON)).astype(BF16)


def kernel(
    count_s, enc_edges, grid, mesh_in, enc_bias, proc_bias, w_embed,
    enc_query, enc_key, enc_value, enc_out,
    proc_query, proc_key, proc_value, proc_out, mlp_gate, mlp_up, mlp_down,
    out,
    edge_s, ext, extf, mesh_v, we_v, eq_v, ek_v, ev_v, eo_v, pq_v, pk_v, pv_v, po_v,
    gate_v, up_v, down_v, eb_v, pb_v, bd, qk, vmap, apart, marks, g, u_s, lat, nx, q_s, k_s, v_s,
    hid, part, peaks, sums, wo, psend, precv,
    load_sem, gs_sem, gr_sem, fs_sem, fr_sem, ds_sem, dr_sem, xs_sem, xr_sem, ls_sem, lr_sem,
    hs_sem, hr_sem, ks_sem, kr_sem, ps_sem, pr_sem,
):
    band, core = lax.axis_index("band"), lax.axis_index("head")
    bands = lax.axis_size("band")
    other = 1 - core
    has_left, has_right = band > 0, band < bands - 1
    left, right = jnp.maximum(band - 1, 0), jnp.minimum(band + 1, bands - 1)
    toward = jnp.where(core == 1, right, left)
    has_toward = band != toward
    grid_rows = grid.shape[0]
    nodes = mesh_in.shape[0]
    half = nodes // 2
    width = mesh_in.shape[1]
    local_width = enc_query.shape[1]
    local_heads = local_width // HDIM
    pairs = local_heads // 2
    edges = edge_s.shape[0]

    def when(condition, action):
        pl.when(condition)(action)

    def mesh_id(b, h):
        return {"band": b, "head": h}

    def ring_rows(b, start, size):
        first = lax.rem(b, RING) * grid_rows + start
        return pl.ds(pl.multiple_of(first, LANES), size)

    own = pl.ds(pl.multiple_of(core * local_width, LANES), local_width)
    theirs = pl.ds(pl.multiple_of(other * local_width, LANES), local_width)
    bias_rows = enc_bias.shape[0]
    sources = [
        (mesh_in, mesh_v),
        (enc_edges.at[:, pl.ds(pl.multiple_of(core * half, LANES), half)], edge_s),
        (enc_query, eq_v),
        (w_embed, we_v),
        (enc_key, ek_v),
        (enc_value, ev_v),
        (enc_bias.at[:, pl.ds(0, half)], eb_v.at[0, pl.ds(0, bias_rows)]),
        (enc_bias.at[:, pl.ds(half, half)], eb_v.at[1, pl.ds(0, bias_rows)]),
        (proc_bias.at[:, pl.ds(0, half)], pb_v.at[0]),
        (proc_bias.at[:, pl.ds(half, half)], pb_v.at[1]),
        (grid, ext.at[ring_rows(band, 0, grid_rows)]),
        (enc_out.at[own], eo_v.at[pl.ds(0, local_width)]),
        (enc_out.at[theirs], eo_v.at[pl.ds(local_width, local_width)]),
        (mlp_gate, gate_v),
        (mlp_up, up_v),
        (proc_query, pq_v),
        (proc_key, pk_v),
        (proc_value, pv_v),
        (mlp_down, down_v),
        (proc_out, po_v),
    ]
    loads = [
        pltpu.make_async_copy(src, dst, load_sem.at[i]) for i, (src, dst) in enumerate(sources)
    ]
    (
        l_mesh, l_edge, l_eq, l_we, l_ek, l_ev, l_eb0, l_eb1, l_pb0, l_pb1, l_grid, l_eo0, l_eo1,
        l_gate, l_up, l_pq, l_pk, l_pv, l_down, l_po,
    ) = loads
    for load in loads[:10]:
        load.start()

    barrier = pltpu.get_barrier_semaphore()
    def greet(device):
        pl.semaphore_signal(barrier, inc=1, device_id=device, device_id_type=pl.DeviceIdType.MESH)

    greet(mesh_id(band, other))

    def greet_band(b):
        greet(mesh_id(b, core))
        greet(mesh_id(b, other))

    when(has_left, lambda: greet_band(left))
    when(has_right, lambda: greet_band(right))
    pl.semaphore_wait(barrier, 1 + jnp.where(has_left, 2, 0) + jnp.where(has_right, 2, 0))

    def remote(src, dst, send, recv, device):
        return pltpu.make_async_remote_copy(
            src_ref=src, dst_ref=dst, send_sem=send, recv_sem=recv,
            device_id=device, device_id_type=pl.DeviceIdType.MESH,
        )

    piece = grid_rows // 2 // CHUNKS
    last_piece = piece // 2
    sizes = [piece] * (CHUNKS - 1) + [piece - last_piece]
    halo = []
    passed = []
    direct = []
    landing = []
    for k, size in enumerate(sizes):
        start = core * (grid_rows // 2) + k * piece
        for d, (target, source) in enumerate(((right, left), (left, right))):
            slot = d * CHUNKS + k
            halo.append(
                remote(
                    grid.at[pl.ds(pl.multiple_of(start, LANES), size)],
                    ext.at[ring_rows(band, start, size)],
                    gs_sem.at[slot], gr_sem.at[slot], mesh_id(target, core),
                )
            )
            here = ext.at[ring_rows(source, start, size)]
            passed.append(
                remote(here, here, fs_sem.at[slot], fr_sem.at[slot], mesh_id(band, other))
            )

    def direct_start(which):
        return which * (grid_rows // 2) + grid_rows // 2 - last_piece

    for n, peer in enumerate((core, other)):
        for d, (target, source) in enumerate(((right, left), (left, right))):
            mine = pl.ds(pl.multiple_of(direct_start(core), LANES), last_piece)
            direct.append(
                remote(
                    grid.at[mine], ext.at[ring_rows(band, direct_start(core), last_piece)],
                    ds_sem.at[2 * n + d], dr_sem.at[2 * n + d], mesh_id(target, peer),
                )
            )
            here = ext.at[ring_rows(source, direct_start(peer), last_piece)]
            landing.append(
                remote(
                    here, here, ds_sem.at[2 * n + d], dr_sem.at[2 * n + d], mesh_id(target, peer)
                )
            )
    sides = (has_left, has_right)

    def start_all(copies):
        for copy in copies:
            copy.start()

    when(has_right, lambda: start_all(halo[0::2] + direct[0::2]))
    when(has_left, lambda: start_all(halo[1::2] + direct[1::2]))
    for load in loads[10:]:
        load.start()

    padding = eb_v.shape[1] - bias_rows
    eb_v[:, pl.ds(bias_rows, padding), :] = jnp.zeros((2, padding, half), F32)
    l_mesh.wait()
    normed_mesh = normalize(mesh_v[...].astype(F32))
    l_eq.wait()
    queries = nn(normed_mesh, eq_v[...]).astype(BF16)
    queries = (queries.astype(F32) * HDIM**-0.5).astype(BF16)
    l_we.wait()
    l_ek.wait()
    key_map = nn(we_v[...], ek_v[...]).astype(BF16)
    l_ev.wait()
    value_map = nn(we_v[...], ev_v[...])
    low_lanes = iota((LANES, LANES), 1) < HDIM
    for pair in range(pairs):
        both = value_map[:, pair * LANES : (pair + 1) * LANES]
        vmap[pair, 0:LANES, :] = jnp.where(low_lanes, both, 0.0).astype(BF16)
        vmap[pair, LANES : 2 * LANES, :] = jnp.where(low_lanes, 0.0, both).astype(BF16)
    l_eb0.wait()
    l_eb1.wait()
    low_half = iota((nodes, LANES), 1) < HDIM
    for h in range(local_heads):
        columns = slice(h // 2 * LANES, (h // 2 + 1) * LANES)
        keep = low_half if h % 2 == 0 else jnp.logical_not(low_half)
        masked = jnp.where(keep, queries[:, columns].astype(F32), 0.0).astype(BF16)
        mapped = nt(masked, key_map[:, columns]).astype(BF16)
        for n in range(2):
            bias = eb_v[n, pl.ds(h, 16, stride=local_heads), :]
            high = bias.astype(BF16).astype(F32)
            middle = (bias - high).astype(BF16).astype(F32)
            low = (bias - high) - middle
            lanes = jnp.concatenate([high, middle, low, jnp.zeros((LANES - 48, half), F32)], 0)
            slot = lax.rem(core + n, 2)
            qk[slot, h, :, 0:LANES] = mapped[n * half : (n + 1) * half]
            qk[slot, h, :, LANES : 2 * LANES] = lanes.T.astype(BF16)
    exchange = [
        remote(qk.at[1], qk.at[2], xs_sem.at[0], xr_sem.at[0], mesh_id(band, other)),
        remote(vmap.at[0:pairs], vmap.at[pairs : 2 * pairs], xs_sem.at[1], xr_sem.at[1], mesh_id(band, other)),
    ]
    for copy in exchange:
        copy.start()

    reach = half
    span = nodes + 2 * reach
    window = 3 * half
    own_count = count_s[band]
    lower_count = jnp.where(has_left, count_s[left], 0)
    upper_count = jnp.where(has_right, count_s[right], 0)
    key_slot = iota((1, span), 1)
    before, after = key_slot < reach, key_slot >= reach + nodes
    limit = jnp.where(before, lower_count, jnp.where(after, upper_count, own_count))
    place = key_slot - jnp.where(before, reach - nodes, jnp.where(after, reach + nodes, reach))
    live = jnp.where(place < limit, 1, 0)
    offset = iota((half, window), 1) - iota((half, window), 0)
    in_window = (offset >= 0) & (offset <= 2 * reach)
    l_pb0.wait()
    l_pb1.wait()
    last = [pb_v[i, pl.ds(2 * reach * local_heads, local_heads), :].T for i in range(2)]

    def window_bias(h):
        for i in range(2):
            turned = pb_v[i, pl.ds(h, 2 * reach, stride=local_heads), :].T
            wide = jnp.concatenate([turned, jnp.zeros((half, window - 2 * reach), F32)], 1)
            skewed = pltpu.roll(wide, 0, 1, stride=1, stride_axis=0)
            final = last[i][:, h : h + 1]
            skewed = jnp.where(offset == 2 * reach, final, skewed)
            usable = in_window & (
                (live[:, i * half : i * half + window] > 0) | (offset == reach)
            )
            bd[h // 2, i, h % 2 * half : (h % 2 + 1) * half] = jnp.where(usable, skewed, NEGATIVE)

    def widen(rows):
        extf[rows, :] = ext[rows, :].astype(F32)

    def arrive(k, d):
        halo[2 * k + d].wait_recv()
        passed[2 * k + d].start()
        widen(ring_rows((left, right)[d], core * (grid_rows // 2) + k * piece, sizes[k]))

    def arrive_passed(k, d):
        passed[2 * k + d].wait_recv()
        widen(ring_rows((left, right)[d], other * (grid_rows // 2) + k * piece, sizes[k]))

    def arrive_direct(d):
        for n, peer in enumerate((core, other)):
            landing[2 * n + d].wait_recv()
            widen(ring_rows((left, right)[d], direct_start(peer), last_piece))

    blocks = half // BLOCK
    block_rows = 16 * BLOCK
    row = iota((block_rows, block_rows), 0)
    column = iota((block_rows, block_rows), 1)
    same = ((row & (BLOCK - 1)) == (column & (BLOCK - 1))) & (column < edges * BLOCK)
    apart[...] = jnp.where(same, 0.0, NEGATIVE)
    lane = iota((block_rows, LANES), 1)
    edge_of_row = iota((block_rows, LANES), 0) >> 4
    mark = (lane < 48) & ((lane & 15) == edge_of_row)
    marks[...] = jnp.where(mark, 1.0, 0.0).astype(BF16)
    v_s[...] = jnp.ones(v_s.shape, BF16)
    for block in range(blocks):
        unused = slice(block * block_rows + edges * BLOCK, (block + 1) * block_rows)
        g[unused, :] = jnp.zeros((block_rows - edges * BLOCK, LANES), F32)
    l_edge.wait()
    l_grid.wait()
    for h in range(local_heads):
        window_bias(h)
    for k in range(CHUNKS):
        widen(ring_rows(band, 2 * k * piece, 2 * piece))
        for d in range(2):
            when(sides[d], lambda k=k, d=d: arrive(k, d))
        if k > 0:
            for d in range(2):
                when(sides[d], lambda k=k, d=d: arrive_passed(k - 1, d))
    for copy in exchange:
        copy.wait()
    for d in range(2):
        when(sides[d], lambda d=d: arrive_direct(d))
    for d in range(2):
        when(sides[d], lambda d=d: arrive_passed(CHUNKS - 1, d))

    def gather(block):
        for edge in range(edges):
            found = []
            for n in range(BLOCK):
                row = edge_s[edge, block * BLOCK + n] & (RING * grid_rows - 1)
                found.append(extf[pl.ds(row, 1), :])
            for n in range(BLOCK):
                g[pl.ds(block * block_rows + edge * BLOCK + n, 1), :] = found[n]

    ones = jnp.ones((block_rows, LANES), BF16)
    gather(0)
    for block in range(blocks):
        if block + 1 < blocks:
            gather(block + 1)
        rows = slice(block * BLOCK, (block + 1) * BLOCK)
        near = g[block * block_rows : (block + 1) * block_rows, :].astype(BF16)
        asked = jnp.concatenate(
            [qk[s, :, rows, :].reshape(local_heads * BLOCK, 2 * LANES) for s in (0, 2)], 0
        )
        scores = nt(asked, jnp.concatenate([near, marks[...]], 1)) + apart[...]
        peak = jnp.max(scores, 1, keepdims=True)
        weights = jnp.exp(scores - peak).astype(BF16)
        mixed = nn(weights, jnp.concatenate([near, ones], 1))
        mixed = (mixed[:, :LANES] / mixed[:, LANES:]).astype(BF16)
        for h in range(2 * local_heads):
            u_s[rows, h * LANES : (h + 1) * LANES] = mixed[h * BLOCK : (h + 1) * BLOCK]
    attended = []
    for pair in range(2 * pairs):
        attended.append(nn(u_s[:, pair * 2 * LANES : (pair + 1) * 2 * LANES], vmap[pair]))
    attended = jnp.concatenate(attended, 1).astype(BF16)
    l_eo0.wait()
    l_eo1.wait()
    own_mesh = mesh_v[pl.ds(pl.multiple_of(core * half, half), half), :].astype(F32)
    latent = (own_mesh + nn(attended, eo_v[...])).astype(BF16)
    lat[core] = latent
    to_sibling = remote(lat.at[core], lat.at[core], ls_sem.at[0], lr_sem.at[0], mesh_id(band, other))
    to_sibling.start()
    nx[1 + core] = normalize(latent.astype(F32))

    third = half * 3 // 8
    tail = pl.ds(2 * third, half - 2 * third)

    def part_of(slot, which):
        return nx.at[slot, pl.ds(pl.multiple_of(which * third, 16), third)]

    sends = [
        remote(
            part_of(1 + core, which), part_of(3 * other, which),
            hs_sem.at[i], hr_sem.at[2 * other], mesh_id(toward, which),
        )
        for i, which in enumerate((core, other))
    ]
    sends += [
        remote(
            nx.at[1 + core, tail], nx.at[3 * other, tail],
            hs_sem.at[2 + i], hr_sem.at[2 * other + 1], mesh_id(toward, which),
        )
        for i, which in enumerate((core, other))
    ]
    when(has_toward, lambda: start_all(sends))
    handed = [
        remote(
            part_of(s, core), part_of(s, core),
            ks_sem.at[d], kr_sem.at[d], mesh_id(band, other),
        )
        for d, s in enumerate((0, 3))
    ]

    def hand(d):
        s = 3 * d
        remote(
            part_of(s, core), part_of(s, core),
            hs_sem.at[0], hr_sem.at[2 * d], mesh_id(toward, core),
        ).wait_recv()
        handed[d].start()

    def all_here(d):
        s = 3 * d
        remote(
            nx.at[s, tail], nx.at[s, tail],
            hs_sem.at[2], hr_sem.at[2 * d + 1], mesh_id(toward, core),
        ).wait_recv()
        handed[d].wait_recv()

    def clear(s):
        nx[s] = jnp.zeros((half, width), BF16)

    when(jnp.logical_not(has_left), lambda: clear(0))
    when(jnp.logical_not(has_right), lambda: clear(3))
    to_sibling.wait_recv()
    nx[2 - core] = normalize(lat[other].astype(F32))
    normed = nx[1:3].reshape(nodes, width)

    l_pq.wait()
    win_query = nn(normed, pq_v[...]).astype(BF16)
    win_query = win_query.astype(F32) * HDIM**-0.5
    first_head = iota((half, LANES), 1) < HDIM
    for i in range(2):
        for pair in range(pairs):
            both = win_query[i * half : (i + 1) * half, pair * LANES : (pair + 1) * LANES]
            q_s[i, pair, 0:half, :] = jnp.where(first_head, both, 0.0).astype(BF16)
            q_s[i, pair, half:nodes, :] = jnp.where(first_head, 0.0, both).astype(BF16)
    l_pk.wait()
    l_pv.wait()

    def keys_values(source, places):
        keys = nn(source, pk_v[...]).astype(BF16)
        values = nn(source, pv_v[...]).astype(BF16)
        for n, rows in enumerate(places):
            have = slice(n * half, (n + 1) * half)
            k_s[rows, :] = keys[have]
            for pair in range(pairs):
                v_s[rows, pair * 2 * LANES : pair * 2 * LANES + LANES] = values[
                    have, pair * LANES : (pair + 1) * LANES
                ]

    keys_values(normed, (slice(half, 2 * half), slice(2 * half, 3 * half)))
    l_gate.wait()
    l_up.wait()
    step = 512
    steps = gate_v.shape[1] // step
    for ch in range(steps):
        columns = slice(ch * step, (ch + 1) * step)
        gated = nn(normed, gate_v[:, columns])
        raised = nn(normed, up_v[:, columns])
        hid[:, columns] = (0.5 * gated * (1.0 + jnp.tanh(0.5 * gated)) * raised).astype(BF16)
    l_down.wait()
    l_po.wait()
    own_keys = slice(half, 3 * half)
    for i in (1, 0):
        held = slice((1 - i) * half, (3 - i) * half)
        for pair in range(pairs):
            if pair % 2 == 0:
                at = ((1 - i) * pairs + pair) // 2 * width // pairs
                columns = slice(at, at + width // pairs)
                part[:, columns] = nn(hid[...], down_v[:, columns])
            columns = slice(pair * LANES, (pair + 1) * LANES)
            scores = nt(q_s[i, pair], k_s[own_keys, columns]) + bd[pair, i, :, held]
            peak = jnp.max(scores, 1, keepdims=True)
            weights = jnp.exp(scores - peak).astype(BF16)
            peaks[i, pair] = jnp.broadcast_to(peak, (nodes, LANES))
            sums[i, pair] = nn(weights, v_s[own_keys, pair * 2 * LANES : (pair + 1) * 2 * LANES])
    when(has_right, lambda: hand(1))
    when(has_left, lambda: hand(0))
    results = [None, None]
    for i in (1, 0):
        when(sides[i], lambda: all_here(i))
        rows = slice(i * half, (i + 1) * half)
        seen = slice(3 * i * half, (3 * i + 1) * half)
        held = slice(2 * i * half, (2 * i + 1) * half)
        keys_values(nx[3 * i], (seen,))
        for pair in range(pairs):
            columns = slice(pair * LANES, (pair + 1) * LANES)
            scores = nt(q_s[i, pair], k_s[seen, columns]) + bd[pair, i, :, held]
            before = peaks[i, pair]
            peak = jnp.maximum(before, jnp.max(scores, 1, keepdims=True))
            weights = jnp.exp(scores - peak).astype(BF16)
            mixed = nn(weights, v_s[seen, pair * 2 * LANES : (pair + 1) * 2 * LANES])
            shrink = jnp.exp(before - peak)
            upper = sums[i, pair, :, 0:LANES] * shrink + mixed[:, :LANES]
            lower = sums[i, pair, :, LANES : 2 * LANES] * shrink + mixed[:, LANES:]
            mixed = upper / lower
            wo[rows, columns] = jnp.where(first_head, mixed[:half], mixed[half:]).astype(BF16)
        psend[i] = (part[rows, :] + nn(wo[rows, :], po_v[...])).astype(BF16)
        result = remote(
            psend.at[i], precv.at[i], ps_sem.at[i], pr_sem.at[i], mesh_id(band, other)
        )
        result.start()
        results[i] = result
    for i in (1, 0):
        results[i].wait_recv()
        summed = psend[i].astype(F32) + precv[i].astype(F32)
        node = iota((half, width), 0) + i * half
        scale = (node < own_count).astype(F32)
        out[i * half : (i + 1) * half, :] = ((lat[i].astype(F32) + summed) * scale).astype(BF16)

    def sent(copies):
        for copy in copies:
            copy.wait_send()

    when(has_right, lambda: sent(halo[0::2] + direct[0::2] + passed[1::2] + handed[1:]))
    when(has_left, lambda: sent(halo[1::2] + direct[1::2] + passed[0::2] + handed[:1]))
    when(has_toward, lambda: sent(sends))
    sent([to_sibling] + results)


def local(
    grid_in, mesh_in, counts, enc_edges, enc_bias, proc_bias, w_embed, enc_query, enc_key,
    enc_value, enc_out, proc_query, proc_key, proc_value, proc_out, mlp_gate, mlp_up, mlp_down,
):
    grid_rows, channels = grid_in.shape
    nodes, width = mesh_in.shape
    local_width = enc_query.shape[1]
    heads = local_width // HDIM
    hidden = mlp_gate.shape[1]
    half = nodes // 2
    edges = enc_edges.shape[0]
    enc_bias = enc_bias.reshape(edges * heads, nodes)
    proc_bias = proc_bias.reshape(-1, nodes)
    anywhere = pl.BlockSpec(memory_space=pl.ANY)
    in_scalar = pl.BlockSpec(memory_space=pltpu.SMEM)
    dma = pltpu.SemaphoreType.DMA
    vmem = pltpu.VMEM
    scratch = [
        pltpu.SMEM((edges, half), jnp.int32),
        vmem((RING * grid_rows, channels), BF16),
        vmem((RING * grid_rows, channels), F32),
        vmem((nodes, width), BF16),
        vmem((channels, width), BF16),
        vmem((width, local_width), BF16),
        vmem((width, local_width), BF16),
        vmem((width, local_width), BF16),
        vmem((width, width), BF16),
        vmem((width, local_width), BF16),
        vmem((width, local_width), BF16),
        vmem((width, local_width), BF16),
        vmem((local_width, width), BF16),
        vmem((width, hidden), BF16),
        vmem((width, hidden), BF16),
        vmem((hidden, width), BF16),
        vmem((2, 16 * heads, half), F32),
        vmem((2, proc_bias.shape[0], half), F32),
        vmem((heads // 2, 2, 2 * half, 3 * half), F32),
        vmem((3, heads, half, 2 * LANES), BF16),
        vmem((heads, 2 * LANES, LANES), BF16),
        vmem((16 * BLOCK, 16 * BLOCK), F32),
        vmem((16 * BLOCK, LANES), BF16),
        vmem((half * 16, channels), F32),
        vmem((half, 2 * heads * channels), BF16),
        vmem((2, half, width), BF16),
        vmem((4, half, width), BF16),
        vmem((2, heads // 2, nodes, LANES), BF16),
        vmem((2 * nodes, local_width), BF16),
        vmem((2 * nodes, 2 * local_width), BF16),
        vmem((nodes, hidden), BF16),
        vmem((nodes, width), F32),
        vmem((2, heads // 2, nodes, LANES), F32),
        vmem((2, heads // 2, nodes, 2 * LANES), F32),
        vmem((nodes, local_width), BF16),
        vmem((2, half, width), BF16),
        vmem((2, half, width), BF16),
        dma((20,)),
        dma((2 * CHUNKS,)),
        dma((2 * CHUNKS,)),
        dma((2 * CHUNKS,)),
        dma((2 * CHUNKS,)),
        dma((4,)),
        dma((4,)),
        dma((2,)),
        dma((2,)),
        dma((1,)),
        dma((1,)),
        dma((4,)),
        dma((4,)),
        dma((2,)),
        dma((2,)),
        dma((2,)),
        dma((2,)),
    ]
    return pl.pallas_call(
        kernel,
        out_shape=pltpu.VMEM((nodes, width), BF16),
        in_specs=[in_scalar] + [anywhere] * 17,
        out_specs=pl.BlockSpec(memory_space=pltpu.VMEM),
        scratch_shapes=scratch,
        compiler_params=pltpu.CompilerParams(
            collective_id=0, has_side_effects=True, vmem_limit_bytes=VMEM_BYTES
        ),
        name="encoder_processor",
    )(
        counts, enc_edges, grid_in, mesh_in, enc_bias, proc_bias, w_embed, enc_query, enc_key,
        enc_value, enc_out, proc_query, proc_key, proc_value, proc_out, mlp_gate, mlp_up, mlp_down,
    )


def solution(mesh):
    heads = P(None, "head")
    in_specs = (
        P("band", None), P("band", None), P(), P(None, "band"), P(None, "head", "band"),
        P(None, "head", "band"), P(), heads, heads, heads, P(), heads, heads, heads,
        P("head", None), heads, heads, P("head", None),
    )
    return jax.shard_map(
        local, mesh=mesh, in_specs=in_specs, out_specs=P("band", None), check_vma=False
    )
```

```python
import jax
import jax.numpy as jnp
from jax import lax
from jax.experimental import pallas as pl
from jax.experimental.pallas import tpu as pltpu
from jax.sharding import PartitionSpec as P

HDIM = 64
EPSILON = 1e-05
NEGATIVE = -1e30
F32 = jnp.float32
BF16 = jnp.bfloat16
LANES = 128
BLOCK = 16
CHUNKS = 8
RING = 4
VMEM_BYTES = 60 * 1024 * 1024


def nn(left, right):
    return lax.dot_general(left, right, (((1,), (0,)), ((), ())), preferred_element_type=F32)


def nt(left, right):
    return lax.dot_general(left, right, (((1,), (1,)), ((), ())), preferred_element_type=F32)


def iota(shape, dim):
    return lax.broadcasted_iota(jnp.int32, shape, dim)


def normalize(rows):
    centred = rows - jnp.mean(rows, -1, keepdims=True)
    variance = jnp.mean(centred * centred, -1, keepdims=True)
    return (centred * lax.rsqrt(variance + EPSILON)).astype(BF16)


def kernel(
    counts, enc_edges, grid, mesh_in, enc_bias, proc_bias, w_embed,
    enc_query, enc_key, enc_value, enc_out,
    proc_query, proc_key, proc_value, proc_out, mlp_gate, mlp_up, mlp_down,
    out,
    count_s, edge_s, ext, extf, mesh_v, we_v, eq_v, ek_v, ev_v, eo_v, pq_v, pk_v, pv_v, po_v,
    gate_v, up_v, down_v, eb_v, pb_v, bd, qk, vmap, apart, marks, g, u_s, lat, nx, q_s, k_s, v_s,
    hid, part, peaks, sums, wo, psend, precv,
    load_sem, gs_sem, gr_sem, fs_sem, fr_sem, ds_sem, dr_sem, xs_sem, xr_sem, ls_sem, lr_sem,
    hs_sem, hr_sem, ks_sem, kr_sem, ps_sem, pr_sem,
):
    band, core = lax.axis_index("band"), lax.axis_index("head")
    bands = lax.axis_size("band")
    other = 1 - core
    has_left, has_right = band > 0, band < bands - 1
    left, right = jnp.maximum(band - 1, 0), jnp.minimum(band + 1, bands - 1)
    toward = jnp.where(core == 1, right, left)
    has_toward = band != toward
    grid_rows = grid.shape[0]
    nodes = mesh_in.shape[0]
    half = nodes // 2
    width = mesh_in.shape[1]
    local_width = enc_query.shape[1]
    local_heads = local_width // HDIM
    pairs = local_heads // 2
    edges = edge_s.shape[0]

    def when(condition, action):
        pl.when(condition)(action)

    def mesh_id(b, h):
        return {"band": b, "head": h}

    def ring_rows(b, start, size):
        first = lax.rem(b, RING) * grid_rows + start
        return pl.ds(pl.multiple_of(first, LANES), size)

    own = pl.ds(pl.multiple_of(core * local_width, LANES), local_width)
    theirs = pl.ds(pl.multiple_of(other * local_width, LANES), local_width)
    bias_rows = enc_bias.shape[0]
    sources = [
        (mesh_in, mesh_v),
        (enc_edges.at[:, pl.ds(pl.multiple_of(core * half, LANES), half)], edge_s),
        (counts, count_s),
        (enc_query, eq_v),
        (w_embed, we_v),
        (enc_key, ek_v),
        (enc_value, ev_v),
        (enc_bias.at[:, pl.ds(0, half)], eb_v.at[0, pl.ds(0, bias_rows)]),
        (enc_bias.at[:, pl.ds(half, half)], eb_v.at[1, pl.ds(0, bias_rows)]),
        (proc_bias.at[:, pl.ds(0, half)], pb_v.at[0]),
        (proc_bias.at[:, pl.ds(half, half)], pb_v.at[1]),
        (grid, ext.at[ring_rows(band, 0, grid_rows)]),
        (enc_out.at[own], eo_v.at[pl.ds(0, local_width)]),
        (enc_out.at[theirs], eo_v.at[pl.ds(local_width, local_width)]),
        (mlp_gate, gate_v),
        (mlp_up, up_v),
        (proc_query, pq_v),
        (proc_key, pk_v),
        (proc_value, pv_v),
        (mlp_down, down_v),
        (proc_out, po_v),
    ]
    loads = [
        pltpu.make_async_copy(src, dst, load_sem.at[i]) for i, (src, dst) in enumerate(sources)
    ]
    (
        l_mesh, l_edge, l_count, l_eq, l_we, l_ek, l_ev, l_eb0, l_eb1, l_pb0, l_pb1, l_grid, l_eo0, l_eo1,
        l_gate, l_up, l_pq, l_pk, l_pv, l_down, l_po,
    ) = loads
    barrier = pltpu.get_barrier_semaphore()
    def greet(device):
        pl.semaphore_signal(barrier, inc=1, device_id=device, device_id_type=pl.DeviceIdType.MESH)

    greet(mesh_id(band, other))

    def greet_band(b):
        greet(mesh_id(b, core))
        greet(mesh_id(b, other))

    when(has_left, lambda: greet_band(left))
    when(has_right, lambda: greet_band(right))
    for load in loads[:11]:
        load.start()
    pl.semaphore_wait(barrier, 1 + jnp.where(has_left, 2, 0) + jnp.where(has_right, 2, 0))

    def remote(src, dst, send, recv, device):
        return pltpu.make_async_remote_copy(
            src_ref=src, dst_ref=dst, send_sem=send, recv_sem=recv,
            device_id=device, device_id_type=pl.DeviceIdType.MESH,
        )

    piece = grid_rows // 2 // CHUNKS
    last_piece = piece // 2
    sizes = [piece] * (CHUNKS - 1) + [piece - last_piece]
    halo = []
    passed = []
    direct = []
    landing = []
    for k, size in enumerate(sizes):
        start = core * (grid_rows // 2) + k * piece
        for d, (target, source) in enumerate(((right, left), (left, right))):
            slot = d * CHUNKS + k
            halo.append(
                remote(
                    grid.at[pl.ds(pl.multiple_of(start, LANES), size)],
                    ext.at[ring_rows(band, start, size)],
                    gs_sem.at[slot], gr_sem.at[slot], mesh_id(target, core),
                )
            )
            here = ext.at[ring_rows(source, start, size)]
            passed.append(
                remote(here, here, fs_sem.at[slot], fr_sem.at[slot], mesh_id(band, other))
            )

    def direct_start(which):
        return which * (grid_rows // 2) + grid_rows // 2 - last_piece

    for n, peer in enumerate((core, other)):
        for d, (target, source) in enumerate(((right, left), (left, right))):
            mine = pl.ds(pl.multiple_of(direct_start(core), LANES), last_piece)
            direct.append(
                remote(
                    grid.at[mine], ext.at[ring_rows(band, direct_start(core), last_piece)],
                    ds_sem.at[2 * n + d], dr_sem.at[2 * n + d], mesh_id(target, peer),
                )
            )
            here = ext.at[ring_rows(source, direct_start(peer), last_piece)]
            landing.append(
                remote(
                    here, here, ds_sem.at[2 * n + d], dr_sem.at[2 * n + d], mesh_id(target, peer)
                )
            )
    sides = (has_left, has_right)

    def start_all(copies):
        for copy in copies:
            copy.start()

    when(has_right, halo[0].start)
    when(has_left, halo[1].start)
    when(has_right, lambda: start_all(halo[2::2] + direct[0::2]))
    when(has_left, lambda: start_all(halo[3::2] + direct[1::2]))
    for load in loads[11:]:
        load.start()

    padding = eb_v.shape[1] - bias_rows
    eb_v[:, pl.ds(bias_rows, padding), :] = jnp.zeros((2, padding, half), F32)
    l_mesh.wait()
    normed_mesh = normalize(mesh_v[...].astype(F32))
    l_eq.wait()
    queries = nn(normed_mesh, eq_v[...]).astype(BF16)
    queries = (queries.astype(F32) * HDIM**-0.5).astype(BF16)
    l_we.wait()
    l_ek.wait()
    key_map = nn(we_v[...], ek_v[...]).astype(BF16)
    l_ev.wait()
    value_map = nn(we_v[...], ev_v[...])
    low_lanes = iota((LANES, LANES), 1) < HDIM
    for pair in range(pairs):
        both = value_map[:, pair * LANES : (pair + 1) * LANES]
        vmap[pair, 0:LANES, :] = jnp.where(low_lanes, both, 0.0).astype(BF16)
        vmap[pair, LANES : 2 * LANES, :] = jnp.where(low_lanes, 0.0, both).astype(BF16)
    l_eb0.wait()
    l_eb1.wait()
    low_half = iota((nodes, LANES), 1) < HDIM
    for h in range(local_heads):
        columns = slice(h // 2 * LANES, (h // 2 + 1) * LANES)
        keep = low_half if h % 2 == 0 else jnp.logical_not(low_half)
        masked = jnp.where(keep, queries[:, columns].astype(F32), 0.0).astype(BF16)
        mapped = nt(masked, key_map[:, columns]).astype(BF16)
        for n in range(2):
            bias = eb_v[n, pl.ds(h, 16, stride=local_heads), :]
            high = bias.astype(BF16).astype(F32)
            middle = (bias - high).astype(BF16).astype(F32)
            low = (bias - high) - middle
            lanes = jnp.concatenate([high, middle, low, jnp.zeros((LANES - 48, half), F32)], 0)
            slot = lax.rem(core + n, 2)
            qk[slot, h, :, 0:LANES] = mapped[n * half : (n + 1) * half]
            qk[slot, h, :, LANES : 2 * LANES] = lanes.T.astype(BF16)
    exchange = [
        remote(qk.at[1], qk.at[2], xs_sem.at[0], xr_sem.at[0], mesh_id(band, other)),
        remote(vmap.at[0:pairs], vmap.at[pairs : 2 * pairs], xs_sem.at[1], xr_sem.at[1], mesh_id(band, other)),
    ]
    for copy in exchange:
        copy.start()

    reach = half
    span = nodes + 2 * reach
    window = 3 * half
    l_count.wait()
    own_count = count_s[band]
    lower_count = jnp.where(has_left, count_s[left], 0)
    upper_count = jnp.where(has_right, count_s[right], 0)
    key_slot = iota((1, span), 1)
    before, after = key_slot < reach, key_slot >= reach + nodes
    limit = jnp.where(before, lower_count, jnp.where(after, upper_count, own_count))
    place = key_slot - jnp.where(before, reach - nodes, jnp.where(after, reach + nodes, reach))
    live = jnp.where(place < limit, 1, 0)
    offset = iota((half, window), 1) - iota((half, window), 0)
    in_window = (offset >= 0) & (offset <= 2 * reach)
    l_pb0.wait()
    l_pb1.wait()
    last = [pb_v[i, pl.ds(2 * reach * local_heads, local_heads), :].T for i in range(2)]

    def window_bias(h):
        for i in range(2):
            turned = pb_v[i, pl.ds(h, 2 * reach, stride=local_heads), :].T
            wide = jnp.concatenate([turned, jnp.zeros((half, window - 2 * reach), F32)], 1)
            skewed = pltpu.roll(wide, 0, 1, stride=1, stride_axis=0)
            final = last[i][:, h : h + 1]
            skewed = jnp.where(offset == 2 * reach, final, skewed)
            usable = in_window & (
                (live[:, i * half : i * half + window] > 0) | (offset == reach)
            )
            bd[h // 2, i, h % 2 * half : (h % 2 + 1) * half] = jnp.where(usable, skewed, NEGATIVE)

    def widen(rows):
        extf[rows, :] = ext[rows, :].astype(F32)

    def arrive(k, d):
        halo[2 * k + d].wait_recv()
        passed[2 * k + d].start()
        widen(ring_rows((left, right)[d], core * (grid_rows // 2) + k * piece, sizes[k]))

    def arrive_passed(k, d):
        passed[2 * k + d].wait_recv()
        widen(ring_rows((left, right)[d], other * (grid_rows // 2) + k * piece, sizes[k]))

    def arrive_direct(d):
        for n, peer in enumerate((core, other)):
            landing[2 * n + d].wait_recv()
            widen(ring_rows((left, right)[d], direct_start(peer), last_piece))

    blocks = half // BLOCK
    block_rows = 16 * BLOCK
    row = iota((block_rows, block_rows), 0)
    column = iota((block_rows, block_rows), 1)
    same = ((row & (BLOCK - 1)) == (column & (BLOCK - 1))) & (column < edges * BLOCK)
    apart[...] = jnp.where(same, 0.0, NEGATIVE)
    lane = iota((block_rows, LANES), 1)
    edge_of_row = iota((block_rows, LANES), 0) >> 4
    mark = (lane < 48) & ((lane & 15) == edge_of_row)
    marks[...] = jnp.where(mark, 1.0, 0.0).astype(BF16)
    v_s[...] = jnp.ones(v_s.shape, BF16)
    for block in range(blocks):
        unused = slice(block * block_rows + edges * BLOCK, (block + 1) * block_rows)
        g[unused, :] = jnp.zeros((block_rows - edges * BLOCK, LANES), F32)
    l_edge.wait()
    l_grid.wait()
    for h in range(local_heads):
        window_bias(h)
    for k in range(CHUNKS):
        widen(ring_rows(band, 2 * k * piece, 2 * piece))
        for d in range(2):
            when(sides[d], lambda k=k, d=d: arrive(k, d))
        if k > 0:
            for d in range(2):
                when(sides[d], lambda k=k, d=d: arrive_passed(k - 1, d))
    for copy in exchange:
        copy.wait()
    for d in range(2):
        when(sides[d], lambda d=d: arrive_direct(d))
    for d in range(2):
        when(sides[d], lambda d=d: arrive_passed(CHUNKS - 1, d))

    def gather(block):
        for edge in range(edges):
            found = []
            for n in range(BLOCK):
                row = edge_s[edge, block * BLOCK + n] & (RING * grid_rows - 1)
                found.append(extf[pl.ds(row, 1), :])
            for n in range(BLOCK):
                g[pl.ds(block * block_rows + edge * BLOCK + n, 1), :] = found[n]

    ones = jnp.ones((block_rows, LANES), BF16)
    quarter = half // 2
    eighth = quarter // 2
    sixteenth = eighth // 2
    parts = (
        lambda which: pl.ds(pl.multiple_of(which * eighth, 16), eighth),
        lambda which: pl.ds(pl.multiple_of(quarter + which * sixteenth, 16), sixteenth),
        lambda which: pl.ds(quarter + eighth, eighth),
    )

    def window_copy(section, which, n):
        rows = parts[section](which)
        return remote(
            nx.at[1 + core, rows], nx.at[3 * other, rows],
            hs_sem.at[2 * section + n], hr_sem.at[3 * other + section], mesh_id(toward, which),
        )

    sends = [
        window_copy(section, which, n) for section in range(3) for n, which in enumerate((core, other))
    ]
    to_sibling = [
        remote(
            lat.at[core, pl.ds(n * quarter, quarter)], lat.at[core, pl.ds(n * quarter, quarter)],
            ls_sem.at[n], lr_sem.at[n], mesh_id(band, other),
        )
        for n in range(2)
    ]
    from_sibling = [
        remote(
            lat.at[other, pl.ds(n * quarter, quarter)], lat.at[other, pl.ds(n * quarter, quarter)],
            ls_sem.at[n], lr_sem.at[n], mesh_id(band, other),
        )
        for n in range(2)
    ]
    handed = []
    for d in range(2):
        for section in range(2):
            here = nx.at[3 * d, parts[section](core)]
            handed.append(
                remote(
                    here, here, ks_sem.at[2 * d + section], kr_sem.at[2 * d + section],
                    mesh_id(band, other),
                )
            )

    def landed(d, section):
        here = nx.at[3 * d, parts[section](core)]
        remote(
            here, here, hs_sem.at[2 * section], hr_sem.at[3 * d + section], mesh_id(toward, core)
        ).wait_recv()

    def hand(d):
        for section in range(2):
            landed(d, section)
            handed[2 * d + section].start()

    def all_here(d):
        landed(d, 2)
        for section in range(2):
            handed[2 * d + section].wait_recv()

    def attend(block):
        rows = slice(block * BLOCK, (block + 1) * BLOCK)
        near = g[block * block_rows : (block + 1) * block_rows, :].astype(BF16)
        asked = jnp.concatenate(
            [qk[s, :, rows, :].reshape(local_heads * BLOCK, 2 * LANES) for s in (0, 2)], 0
        )
        scores = nt(asked, jnp.concatenate([near, marks[...]], 1)) + apart[...]
        peak = jnp.max(scores, 1, keepdims=True)
        weights = jnp.exp(scores - peak).astype(BF16)
        mixed = nn(weights, jnp.concatenate([near, ones], 1))
        mixed = (mixed[:, :LANES] / mixed[:, LANES:]).astype(BF16)
        for h in range(2 * local_heads):
            u_s[rows, h * LANES : (h + 1) * LANES] = mixed[h * BLOCK : (h + 1) * BLOCK]

    l_eo0.wait()
    l_eo1.wait()
    gather(0)
    for n in range(2):
        for block in range(n * blocks // 2, (n + 1) * blocks // 2):
            if block + 1 < blocks:
                gather(block + 1)
            attend(block)
        rows = slice(n * quarter, (n + 1) * quarter)
        attended = jnp.concatenate(
            [
                nn(u_s[rows, pair * 2 * LANES : (pair + 1) * 2 * LANES], vmap[pair])
                for pair in range(2 * pairs)
            ],
            1,
        ).astype(BF16)
        start = pl.multiple_of(core * half + n * quarter, quarter)
        own_mesh = mesh_v[pl.ds(start, quarter), :].astype(F32)
        latent = (own_mesh + nn(attended, eo_v[...])).astype(BF16)
        lat[core, rows] = latent
        to_sibling[n].start()
        nx[1 + core, rows] = normalize(latent.astype(F32))
        when(has_toward, lambda n=n: start_all(sends[:2] if n == 0 else sends[2:]))

    def clear(s):
        nx[s] = jnp.zeros((half, width), BF16)

    when(jnp.logical_not(has_left), lambda: clear(0))
    when(jnp.logical_not(has_right), lambda: clear(3))
    first_head = iota((half, LANES), 1) < HDIM
    step = 512
    steps = gate_v.shape[1] // step

    def keys_values(source, start):
        rows = pl.ds(pl.multiple_of(start, half), half)
        k_s[rows, :] = nn(source, pk_v[...]).astype(BF16)
        values = nn(source, pv_v[...]).astype(BF16)
        for pair in range(pairs):
            v_s[rows, pair * 2 * LANES : pair * 2 * LANES + LANES] = values[
                :, pair * LANES : (pair + 1) * LANES
            ]

    def project(which):
        source = nx[1 + which]
        win_query = nn(source, pq_v[...]).astype(BF16)
        win_query = win_query.astype(F32) * HDIM**-0.5
        for pair in range(pairs):
            both = win_query[:, pair * LANES : (pair + 1) * LANES]
            q_s[which, pair, 0:half, :] = jnp.where(first_head, both, 0.0).astype(BF16)
            q_s[which, pair, half:nodes, :] = jnp.where(first_head, 0.0, both).astype(BF16)
        keys_values(source, (1 + which) * half)
        rows = pl.ds(pl.multiple_of(which * half, half), half)
        for ch in range(steps):
            columns = slice(ch * step, (ch + 1) * step)
            gated = nn(source, gate_v[:, columns])
            raised = nn(source, up_v[:, columns])
            activated = 0.5 * gated * (1.0 + jnp.tanh(0.5 * gated)) * raised
            hid[rows, columns] = activated.astype(BF16)

    for load in (l_pq, l_pk, l_pv, l_gate, l_up, l_down, l_po):
        load.wait()
    project(core)
    for copy in from_sibling:
        copy.wait_recv()
    nx[2 - core] = normalize(lat[other].astype(F32))
    project(other)

    own_keys = slice(half, 3 * half)
    for i in (1, 0):
        held = slice((1 - i) * half, (3 - i) * half)
        for pair in range(pairs):
            if pair % 2 == 0:
                at = ((1 - i) * pairs + pair) // 2 * width // pairs
                columns = slice(at, at + width // pairs)
                part[:, columns] = nn(hid[...], down_v[:, columns])
            columns = slice(pair * LANES, (pair + 1) * LANES)
            scores = nt(q_s[i, pair], k_s[own_keys, columns]) + bd[pair, i, :, held]
            peak = jnp.max(scores, 1, keepdims=True)
            weights = jnp.exp(scores - peak).astype(BF16)
            peaks[i, pair] = jnp.broadcast_to(peak, (nodes, LANES))
            sums[i, pair] = nn(weights, v_s[own_keys, pair * 2 * LANES : (pair + 1) * 2 * LANES])
    when(has_right, lambda: hand(1))
    when(has_left, lambda: hand(0))
    results = [None] * 4
    for i in (1, 0):
        when(sides[i], lambda: all_here(i))
        rows = slice(i * half, (i + 1) * half)
        seen = slice(3 * i * half, (3 * i + 1) * half)
        held = slice(2 * i * half, (2 * i + 1) * half)
        keys_values(nx[3 * i], 3 * i * half)
        for pair in range(pairs):
            columns = slice(pair * LANES, (pair + 1) * LANES)
            scores = nt(q_s[i, pair], k_s[seen, columns]) + bd[pair, i, :, held]
            before = peaks[i, pair]
            peak = jnp.maximum(before, jnp.max(scores, 1, keepdims=True))
            weights = jnp.exp(scores - peak).astype(BF16)
            mixed = nn(weights, v_s[seen, pair * 2 * LANES : (pair + 1) * 2 * LANES])
            shrink = jnp.exp(before - peak)
            upper = sums[i, pair, :, 0:LANES] * shrink + mixed[:, :LANES]
            lower = sums[i, pair, :, LANES : 2 * LANES] * shrink + mixed[:, LANES:]
            mixed = upper / lower
            wo[rows, columns] = jnp.where(first_head, mixed[:half], mixed[half:]).astype(BF16)
        for n in range(2):
            columns = slice(n * width // 2, (n + 1) * width // 2)
            psend[i, n] = (part[rows, columns] + nn(wo[rows, :], po_v[:, columns])).astype(BF16)
            at = 2 * i + n
            results[at] = remote(
                psend.at[i, n], precv.at[i, n], ps_sem.at[at], pr_sem.at[at], mesh_id(band, other)
            )
            results[at].start()
    for i in (1, 0):
        node = iota((half, width // 2), 0) + i * half
        scale = (node < own_count).astype(F32)
        for n in range(2):
            results[2 * i + n].wait_recv()
            columns = slice(n * width // 2, (n + 1) * width // 2)
            summed = psend[i, n].astype(F32) + precv[i, n].astype(F32)
            total = lat[i, :, columns].astype(F32) + summed
            out[i * half : (i + 1) * half, columns] = (total * scale).astype(BF16)

    def sent(copies):
        for copy in copies:
            copy.wait_send()

    when(has_right, lambda: sent(halo[0::2] + direct[0::2] + passed[1::2] + handed[2:]))
    when(has_left, lambda: sent(halo[1::2] + direct[1::2] + passed[0::2] + handed[:2]))
    when(has_toward, lambda: sent(sends))
    sent(to_sibling + results)


def local(
    grid_in, mesh_in, counts, enc_edges, enc_bias, proc_bias, w_embed, enc_query, enc_key,
    enc_value, enc_out, proc_query, proc_key, proc_value, proc_out, mlp_gate, mlp_up, mlp_down,
):
    grid_rows, channels = grid_in.shape
    nodes, width = mesh_in.shape
    local_width = enc_query.shape[1]
    heads = local_width // HDIM
    hidden = mlp_gate.shape[1]
    half = nodes // 2
    edges = enc_edges.shape[0]
    enc_bias = enc_bias.reshape(edges * heads, nodes)
    proc_bias = proc_bias.reshape(-1, nodes)
    anywhere = pl.BlockSpec(memory_space=pl.ANY)
    dma = pltpu.SemaphoreType.DMA
    vmem = pltpu.VMEM
    scratch = [
        pltpu.SMEM(counts.shape, jnp.int32),
        pltpu.SMEM((edges, half), jnp.int32),
        vmem((RING * grid_rows, channels), BF16),
        vmem((RING * grid_rows, channels), F32),
        vmem((nodes, width), BF16),
        vmem((channels, width), BF16),
        vmem((width, local_width), BF16),
        vmem((width, local_width), BF16),
        vmem((width, local_width), BF16),
        vmem((width, width), BF16),
        vmem((width, local_width), BF16),
        vmem((width, local_width), BF16),
        vmem((width, local_width), BF16),
        vmem((local_width, width), BF16),
        vmem((width, hidden), BF16),
        vmem((width, hidden), BF16),
        vmem((hidden, width), BF16),
        vmem((2, 16 * heads, half), F32),
        vmem((2, proc_bias.shape[0], half), F32),
        vmem((heads // 2, 2, 2 * half, 3 * half), F32),
        vmem((3, heads, half, 2 * LANES), BF16),
        vmem((heads, 2 * LANES, LANES), BF16),
        vmem((16 * BLOCK, 16 * BLOCK), F32),
        vmem((16 * BLOCK, LANES), BF16),
        vmem((half * 16, channels), F32),
        vmem((half, 2 * heads * channels), BF16),
        vmem((2, half, width), BF16),
        vmem((4, half, width), BF16),
        vmem((2, heads // 2, nodes, LANES), BF16),
        vmem((2 * nodes, local_width), BF16),
        vmem((2 * nodes, 2 * local_width), BF16),
        vmem((nodes, hidden), BF16),
        vmem((nodes, width), F32),
        vmem((2, heads // 2, nodes, LANES), F32),
        vmem((2, heads // 2, nodes, 2 * LANES), F32),
        vmem((nodes, local_width), BF16),
        vmem((2, 2, half, width // 2), BF16),
        vmem((2, 2, half, width // 2), BF16),
        dma((21,)),
        dma((2 * CHUNKS,)),
        dma((2 * CHUNKS,)),
        dma((2 * CHUNKS,)),
        dma((2 * CHUNKS,)),
        dma((4,)),
        dma((4,)),
        dma((2,)),
        dma((2,)),
        dma((2,)),
        dma((2,)),
        dma((6,)),
        dma((6,)),
        dma((4,)),
        dma((4,)),
        dma((4,)),
        dma((4,)),
    ]
    return pl.pallas_call(
        kernel,
        out_shape=pltpu.VMEM((nodes, width), BF16),
        in_specs=[anywhere] * 18,
        out_specs=pl.BlockSpec(memory_space=pltpu.VMEM),
        scratch_shapes=scratch,
        compiler_params=pltpu.CompilerParams(
            collective_id=0, has_side_effects=True, vmem_limit_bytes=VMEM_BYTES
        ),
        name="encoder_processor",
    )(
        counts, enc_edges, grid_in, mesh_in, enc_bias, proc_bias, w_embed, enc_query, enc_key,
        enc_value, enc_out, proc_query, proc_key, proc_value, proc_out, mlp_gate, mlp_up, mlp_down,
    )


def solution(mesh):
    heads = P(None, "head")
    in_specs = (
        P("band", None), P("band", None), P(), P(None, "band"), P(None, "head", "band"),
        P(None, "head", "band"), P(), heads, heads, heads, P(), heads, heads, heads,
        P("head", None), heads, heads, P("head", None),
    )
    return jax.shard_map(
        local, mesh=mesh, in_specs=in_specs, out_specs=P("band", None), check_vma=False
    )
```

```python
import jax
import jax.numpy as jnp
from jax import lax
from jax.experimental import pallas as pl
from jax.experimental.pallas import tpu as pltpu
from jax.sharding import PartitionSpec as P

HDIM = 64
EPSILON = 1e-05
NEGATIVE = -1e30
F32 = jnp.float32
BF16 = jnp.bfloat16
LANES = 128
BLOCK = 16
SHARES = (4, 4, 4, 3)
CHUNKS = len(SHARES)
RING = 4
VMEM_BYTES = 60 * 1024 * 1024


def nn(left, right):
    return lax.dot_general(left, right, (((1,), (0,)), ((), ())), preferred_element_type=F32)


def nt(left, right):
    return lax.dot_general(left, right, (((1,), (1,)), ((), ())), preferred_element_type=F32)


def inverse(values):
    guess = pl.reciprocal(values, approx=True)
    return guess * (2.0 - values * guess)


def iota(shape, dim):
    return lax.broadcasted_iota(jnp.int32, shape, dim)


def normalize(rows):
    centred = rows - jnp.mean(rows, -1, keepdims=True)
    variance = jnp.mean(centred * centred, -1, keepdims=True)
    return (centred * lax.rsqrt(variance + EPSILON)).astype(BF16)


def kernel(
    counts, enc_edges, grid, mesh_in, enc_bias, proc_bias, w_embed,
    enc_query, enc_key, enc_value, enc_out,
    proc_query, proc_key, proc_value, proc_out, mlp_gate, mlp_up, mlp_down,
    out,
    count_s, edge_s, ext, extf, mesh_v, we_v, eq_v, ek_v, ev_v, eo_v, pq_v, pk_v, pv_v, po_v,
    gate_v, up_v, down_v, eb_v, pb_v, bd, qk, vmap, apart, marks, g, u_s, lat, nx, q_s, k_s, v_s,
    hid, part, peaks, sums, wo, psend, precv,
    load_sem, gs_sem, gr_sem, fs_sem, fr_sem, ds_sem, dr_sem, xs_sem, xr_sem, ls_sem, lr_sem,
    hs_sem, hr_sem, ks_sem, kr_sem, ps_sem, pr_sem,
):
    band, core = lax.axis_index("band"), lax.axis_index("head")
    bands = lax.axis_size("band")
    other = 1 - core
    has_left, has_right = band > 0, band < bands - 1
    left, right = jnp.maximum(band - 1, 0), jnp.minimum(band + 1, bands - 1)
    toward = jnp.where(core == 1, right, left)
    has_toward = band != toward
    grid_rows = grid.shape[0]
    nodes = mesh_in.shape[0]
    half = nodes // 2
    width = mesh_in.shape[1]
    local_width = enc_query.shape[1]
    local_heads = local_width // HDIM
    pairs = local_heads // 2
    edges = edge_s.shape[0]

    def when(condition, action):
        pl.when(condition)(action)

    def mesh_id(b, h):
        return {"band": b, "head": h}

    def ring_rows(b, start, size):
        first = lax.rem(b, RING) * grid_rows + start
        return pl.ds(pl.multiple_of(first, LANES), size)

    own = pl.ds(pl.multiple_of(core * local_width, LANES), local_width)
    theirs = pl.ds(pl.multiple_of(other * local_width, LANES), local_width)
    bias_rows = enc_bias.shape[0]
    sources = [
        (grid, ext.at[ring_rows(band, 0, grid_rows)]),
        (mesh_in, mesh_v),
        (enc_edges.at[:, pl.ds(pl.multiple_of(core * half, LANES), half)], edge_s),
        (counts, count_s),
        (enc_query, eq_v),
        (w_embed, we_v),
        (enc_key, ek_v),
        (enc_value, ev_v),
        (enc_bias.at[:, pl.ds(0, half)], eb_v.at[0, pl.ds(0, bias_rows)]),
        (enc_bias.at[:, pl.ds(half, half)], eb_v.at[1, pl.ds(0, bias_rows)]),
        (proc_bias.at[:, pl.ds(0, half)], pb_v.at[0]),
        (proc_bias.at[:, pl.ds(half, half)], pb_v.at[1]),
        (enc_out.at[own], eo_v.at[pl.ds(0, local_width)]),
        (enc_out.at[theirs], eo_v.at[pl.ds(local_width, local_width)]),
        (mlp_gate, gate_v),
        (mlp_up, up_v),
        (proc_query, pq_v),
        (proc_key, pk_v),
        (proc_value, pv_v),
        (mlp_down, down_v),
        (proc_out, po_v),
    ]
    loads = [
        pltpu.make_async_copy(src, dst, load_sem.at[i]) for i, (src, dst) in enumerate(sources)
    ]
    (
        l_grid, l_mesh, l_edge, l_count, l_eq, l_we, l_ek, l_ev, l_eb0, l_eb1, l_pb0, l_pb1, l_eo0, l_eo1,
        l_gate, l_up, l_pq, l_pk, l_pv, l_down, l_po,
    ) = loads
    barrier = pltpu.get_barrier_semaphore()
    def greet(device):
        pl.semaphore_signal(barrier, inc=1, device_id=device, device_id_type=pl.DeviceIdType.MESH)

    def greet_band(b):
        greet(mesh_id(b, core))
        greet(mesh_id(b, other))

    when(has_right, lambda: greet_band(right))
    when(has_left, lambda: greet_band(left))
    greet(mesh_id(band, other))
    for load in loads[:8]:
        load.start()
    pl.semaphore_wait(barrier, 1 + jnp.where(has_left, 2, 0) + jnp.where(has_right, 2, 0))

    def remote(src, dst, send, recv, device):
        return pltpu.make_async_remote_copy(
            src_ref=src, dst_ref=dst, send_sem=send, recv_sem=recv,
            device_id=device, device_id_type=pl.DeviceIdType.MESH,
        )

    unit = grid_rows // 2 // 16
    sizes = [share * unit for share in SHARES]
    starts = [sum(sizes[:k]) for k in range(CHUNKS)]
    last_piece = grid_rows // 2 - sum(sizes)
    halo = []
    passed = []
    direct = []
    landing = []
    for k, size in enumerate(sizes):
        start = core * (grid_rows // 2) + starts[k]
        for d, (target, source) in enumerate(((right, left), (left, right))):
            slot = d * CHUNKS + k
            halo.append(
                remote(
                    ext.at[ring_rows(band, start, size)],
                    ext.at[ring_rows(band, start, size)],
                    gs_sem.at[slot], gr_sem.at[slot], mesh_id(target, core),
                )
            )
            here = ext.at[ring_rows(source, start, size)]
            passed.append(
                remote(here, here, fs_sem.at[slot], fr_sem.at[slot], mesh_id(band, other))
            )

    def direct_start(which):
        return which * (grid_rows // 2) + grid_rows // 2 - last_piece

    for n, peer in enumerate((core, other)):
        for d, (target, source) in enumerate(((right, left), (left, right))):
            mine = ring_rows(band, direct_start(core), last_piece)
            direct.append(
                remote(
                    ext.at[mine], ext.at[mine],
                    ds_sem.at[2 * n + d], dr_sem.at[2 * n + d], mesh_id(target, peer),
                )
            )
            here = ext.at[ring_rows(source, direct_start(peer), last_piece)]
            landing.append(
                remote(
                    here, here, ds_sem.at[2 * n + d], dr_sem.at[2 * n + d], mesh_id(target, peer)
                )
            )
    sides = (has_left, has_right)

    def start_all(copies):
        for copy in copies:
            copy.start()

    l_grid.wait()
    when(has_left, halo[1].start)
    when(has_right, halo[0].start)
    when(has_left, lambda: start_all(halo[3::2] + direct[1::2]))
    when(has_right, lambda: start_all(halo[2::2] + direct[0::2]))
    for load in loads[8:]:
        load.start()

    padding = eb_v.shape[1] - bias_rows
    eb_v[:, pl.ds(bias_rows, padding), :] = jnp.zeros((2, padding, half), F32)
    l_mesh.wait()
    normed_mesh = normalize(mesh_v[...].astype(F32))
    l_eq.wait()
    queries = nn(normed_mesh, eq_v[...]).astype(BF16)
    queries = (queries.astype(F32) * HDIM**-0.5).astype(BF16)
    l_we.wait()
    l_ek.wait()
    key_map = nn(we_v[...], ek_v[...]).astype(BF16)
    l_ev.wait()
    value_map = nn(we_v[...], ev_v[...])
    low_lanes = iota((LANES, LANES), 1) < HDIM
    for pair in range(pairs):
        both = value_map[:, pair * LANES : (pair + 1) * LANES]
        vmap[pair, 0:LANES, :] = jnp.where(low_lanes, both, 0.0).astype(BF16)
        vmap[pair, LANES : 2 * LANES, :] = jnp.where(low_lanes, 0.0, both).astype(BF16)
    l_eb0.wait()
    l_eb1.wait()
    low_half = iota((nodes, LANES), 1) < HDIM
    for h in range(local_heads):
        columns = slice(h // 2 * LANES, (h // 2 + 1) * LANES)
        keep = low_half if h % 2 == 0 else jnp.logical_not(low_half)
        masked = jnp.where(keep, queries[:, columns].astype(F32), 0.0).astype(BF16)
        mapped = nt(masked, key_map[:, columns]).astype(BF16)
        for n in range(2):
            bias = eb_v[n, pl.ds(h, 16, stride=local_heads), :]
            high = bias.astype(BF16).astype(F32)
            middle = (bias - high).astype(BF16).astype(F32)
            low = (bias - high) - middle
            lanes = jnp.concatenate([high, middle, low, jnp.zeros((LANES - 48, half), F32)], 0)
            slot = lax.rem(core + n, 2)
            qk[slot, h, :, 0:LANES] = mapped[n * half : (n + 1) * half]
            qk[slot, h, :, LANES : 2 * LANES] = lanes.T.astype(BF16)
    exchange = [
        remote(qk.at[1], qk.at[2], xs_sem.at[0], xr_sem.at[0], mesh_id(band, other)),
        remote(vmap.at[0:pairs], vmap.at[pairs : 2 * pairs], xs_sem.at[1], xr_sem.at[1], mesh_id(band, other)),
    ]
    for copy in exchange:
        copy.start()

    reach = half
    span = nodes + 2 * reach
    window = 3 * half
    l_count.wait()
    own_count = count_s[band]
    lower_count = jnp.where(has_left, count_s[left], 0)
    upper_count = jnp.where(has_right, count_s[right], 0)
    key_slot = iota((1, span), 1)
    before, after = key_slot < reach, key_slot >= reach + nodes
    limit = jnp.where(before, lower_count, jnp.where(after, upper_count, own_count))
    place = key_slot - jnp.where(before, reach - nodes, jnp.where(after, reach + nodes, reach))
    live = jnp.where(place < limit, 1, 0)
    offset = iota((half, window), 1) - iota((half, window), 0)
    in_window = (offset >= 0) & (offset <= 2 * reach)
    l_pb0.wait()
    l_pb1.wait()
    last = [pb_v[i, pl.ds(2 * reach * local_heads, local_heads), :].T for i in range(2)]

    def window_bias(h):
        for i in range(2):
            turned = pb_v[i, pl.ds(h, 2 * reach, stride=local_heads), :].T
            wide = jnp.concatenate([turned, jnp.zeros((half, window - 2 * reach), F32)], 1)
            skewed = pltpu.roll(wide, 0, 1, stride=1, stride_axis=0)
            final = last[i][:, h : h + 1]
            skewed = jnp.where(offset == 2 * reach, final, skewed)
            usable = in_window & (
                (live[:, i * half : i * half + window] > 0) | (offset == reach)
            )
            bd[h // 2, i, h % 2 * half : (h % 2 + 1) * half] = jnp.where(usable, skewed, NEGATIVE)

    def widen(rows):
        extf[rows, :] = ext[rows, :].astype(F32)

    def arrive(k, d):
        halo[2 * k + d].wait_recv()
        passed[2 * k + d].start()
        widen(ring_rows((left, right)[d], core * (grid_rows // 2) + starts[k], sizes[k]))

    def arrive_passed(k, d):
        passed[2 * k + d].wait_recv()
        widen(ring_rows((left, right)[d], other * (grid_rows // 2) + starts[k], sizes[k]))

    def arrive_direct(d):
        for n, peer in enumerate((core, other)):
            landing[2 * n + d].wait_recv()
            widen(ring_rows((left, right)[d], direct_start(peer), last_piece))

    blocks = half // BLOCK
    block_rows = 16 * BLOCK
    row = iota((block_rows, block_rows), 0)
    column = iota((block_rows, block_rows), 1)
    same = ((row & (BLOCK - 1)) == (column & (BLOCK - 1))) & (column < edges * BLOCK)
    apart[...] = jnp.where(same, 0.0, NEGATIVE)
    lane = iota((block_rows, LANES), 1)
    edge_of_row = iota((block_rows, LANES), 0) >> 4
    mark = (lane < 48) & ((lane & 15) == edge_of_row)
    marks[...] = jnp.where(mark, 1.0, 0.0).astype(BF16)
    v_s[...] = jnp.ones(v_s.shape, BF16)
    for block in range(blocks):
        unused = slice(block * block_rows + edges * BLOCK, (block + 1) * block_rows)
        g[unused, :] = jnp.zeros((block_rows - edges * BLOCK, LANES), F32)
    l_edge.wait()
    for h in range(local_heads):
        window_bias(h)
    for k in range(CHUNKS):
        widen(ring_rows(band, 2 * starts[k], 2 * sizes[k]))
        for d in range(2):
            when(sides[d], lambda k=k, d=d: arrive(k, d))
        if k > 0:
            for d in range(2):
                when(sides[d], lambda k=k, d=d: arrive_passed(k - 1, d))
    widen(ring_rows(band, grid_rows - 2 * last_piece, 2 * last_piece))
    for copy in exchange:
        copy.wait()
    for d in range(2):
        when(sides[d], lambda d=d: arrive_direct(d))
    for d in range(2):
        when(sides[d], lambda d=d: arrive_passed(CHUNKS - 1, d))

    def gather(block):
        for edge in range(edges):
            found = []
            for n in range(BLOCK):
                row = edge_s[edge, block * BLOCK + n] & (RING * grid_rows - 1)
                found.append(extf[pl.ds(row, 1), :])
            for n in range(BLOCK):
                g[pl.ds(block * block_rows + edge * BLOCK + n, 1), :] = found[n]

    ones = jnp.ones((block_rows, LANES), BF16)
    quarter = half // 2
    eighth = quarter // 2
    sixteenth = eighth // 2
    parts = (
        lambda which: pl.ds(pl.multiple_of(which * eighth, 16), eighth),
        lambda which: pl.ds(pl.multiple_of(quarter + which * sixteenth, 16), sixteenth),
        lambda which: pl.ds(quarter + eighth, eighth),
    )

    def window_copy(section, which, n):
        rows = parts[section](which)
        return remote(
            nx.at[1 + core, rows], nx.at[3 * other, rows],
            hs_sem.at[2 * section + n], hr_sem.at[3 * other + section], mesh_id(toward, which),
        )

    sends = [
        window_copy(section, which, n) for section in range(3) for n, which in enumerate((core, other))
    ]
    to_sibling = [
        remote(
            lat.at[core, pl.ds(n * quarter, quarter)], lat.at[core, pl.ds(n * quarter, quarter)],
            ls_sem.at[n], lr_sem.at[n], mesh_id(band, other),
        )
        for n in range(2)
    ]
    from_sibling = [
        remote(
            lat.at[other, pl.ds(n * quarter, quarter)], lat.at[other, pl.ds(n * quarter, quarter)],
            ls_sem.at[n], lr_sem.at[n], mesh_id(band, other),
        )
        for n in range(2)
    ]
    handed = []
    for d in range(2):
        for section in range(2):
            here = nx.at[3 * d, parts[section](core)]
            handed.append(
                remote(
                    here, here, ks_sem.at[2 * d + section], kr_sem.at[2 * d + section],
                    mesh_id(band, other),
                )
            )

    def landed(d, section):
        here = nx.at[3 * d, parts[section](core)]
        remote(
            here, here, hs_sem.at[2 * section], hr_sem.at[3 * d + section], mesh_id(toward, core)
        ).wait_recv()

    def hand(d):
        for section in range(2):
            landed(d, section)
            handed[2 * d + section].start()

    def all_here(d):
        landed(d, 2)
        for section in range(2):
            handed[2 * d + section].wait_recv()

    def attend(block):
        rows = slice(block * BLOCK, (block + 1) * BLOCK)
        near = g[block * block_rows : (block + 1) * block_rows, :].astype(BF16)
        asked = jnp.concatenate(
            [qk[s, :, rows, :].reshape(local_heads * BLOCK, 2 * LANES) for s in (0, 2)], 0
        )
        scores = nt(asked, jnp.concatenate([near, marks[...]], 1)) + apart[...]
        peak = jnp.max(scores, 1, keepdims=True)
        weights = jnp.exp(scores - peak).astype(BF16)
        mixed = nn(weights, jnp.concatenate([near, ones], 1))
        mixed = (mixed[:, :LANES] * inverse(mixed[:, LANES:])).astype(BF16)
        for h in range(2 * local_heads):
            u_s[rows, h * LANES : (h + 1) * LANES] = mixed[h * BLOCK : (h + 1) * BLOCK]

    l_eo0.wait()
    l_eo1.wait()
    gather(0)
    for block in range(blocks):
        if block + 1 < blocks:
            gather(block + 1)
        attend(block)
    attended = jnp.concatenate(
        [
            nn(u_s[:, pair * 2 * LANES : (pair + 1) * 2 * LANES], vmap[pair])
            for pair in range(2 * pairs)
        ],
        1,
    ).astype(BF16)
    own_mesh = mesh_v[pl.ds(pl.multiple_of(core * half, half), half), :].astype(F32)
    latent = (own_mesh + nn(attended, eo_v[...])).astype(BF16)
    lat[core] = latent
    nx[1 + core] = normalize(latent.astype(F32))
    when(has_toward, lambda: start_all(sends))
    start_all(to_sibling)

    def clear(s):
        nx[s] = jnp.zeros((half, width), BF16)

    when(jnp.logical_not(has_left), lambda: clear(0))
    when(jnp.logical_not(has_right), lambda: clear(3))
    first_head = iota((half, LANES), 1) < HDIM
    step = 512
    steps = gate_v.shape[1] // step

    def keys_values(source, start):
        rows = pl.ds(pl.multiple_of(start, half), half)
        k_s[rows, :] = nn(source, pk_v[...]).astype(BF16)
        values = nn(source, pv_v[...]).astype(BF16)
        for pair in range(pairs):
            v_s[rows, pair * 2 * LANES : pair * 2 * LANES + LANES] = values[
                :, pair * LANES : (pair + 1) * LANES
            ]

    def project(which):
        source = nx[1 + which]
        win_query = nn(source, pq_v[...]).astype(BF16)
        win_query = win_query.astype(F32) * HDIM**-0.5
        for pair in range(pairs):
            both = win_query[:, pair * LANES : (pair + 1) * LANES]
            q_s[which, pair, 0:half, :] = jnp.where(first_head, both, 0.0).astype(BF16)
            q_s[which, pair, half:nodes, :] = jnp.where(first_head, 0.0, both).astype(BF16)
        keys_values(source, (1 + which) * half)
        rows = pl.ds(pl.multiple_of(which * half, half), half)
        for ch in range(steps):
            columns = slice(ch * step, (ch + 1) * step)
            gated = nn(source, gate_v[:, columns])
            raised = nn(source, up_v[:, columns])
            activated = 0.5 * gated * (1.0 + jnp.tanh(0.5 * gated)) * raised
            hid[rows, columns] = activated.astype(BF16)

    for load in (l_pq, l_pk, l_pv, l_gate, l_up, l_down, l_po):
        load.wait()
    project(core)
    for copy in from_sibling:
        copy.wait_recv()
    nx[2 - core] = normalize(lat[other].astype(F32))
    project(other)

    when(has_right, lambda: hand(1))
    own_keys = slice(half, 3 * half)
    for i in (1, 0):
        held = slice((1 - i) * half, (3 - i) * half)
        for pair in range(pairs):
            if pair % 2 == 0:
                at = ((1 - i) * pairs + pair) // 2 * width // pairs
                columns = slice(at, at + width // pairs)
                part[:, columns] = nn(hid[...], down_v[:, columns])
            columns = slice(pair * LANES, (pair + 1) * LANES)
            scores = nt(q_s[i, pair], k_s[own_keys, columns]) + bd[pair, i, :, held]
            peak = jnp.max(scores, 1, keepdims=True)
            weights = jnp.exp(scores - peak).astype(BF16)
            peaks[i, pair] = jnp.broadcast_to(peak, (nodes, LANES))
            sums[i, pair] = nn(weights, v_s[own_keys, pair * 2 * LANES : (pair + 1) * 2 * LANES])
    when(has_left, lambda: hand(0))
    results = [None] * 4
    for i in (1, 0):
        when(sides[i], lambda: all_here(i))
        rows = slice(i * half, (i + 1) * half)
        seen = slice(3 * i * half, (3 * i + 1) * half)
        held = slice(2 * i * half, (2 * i + 1) * half)
        keys_values(nx[3 * i], 3 * i * half)
        for pair in range(pairs):
            columns = slice(pair * LANES, (pair + 1) * LANES)
            scores = nt(q_s[i, pair], k_s[seen, columns]) + bd[pair, i, :, held]
            before = peaks[i, pair]
            peak = jnp.maximum(before, jnp.max(scores, 1, keepdims=True))
            weights = jnp.exp(scores - peak).astype(BF16)
            mixed = nn(weights, v_s[seen, pair * 2 * LANES : (pair + 1) * 2 * LANES])
            shrink = jnp.exp(before - peak)
            upper = sums[i, pair, :, 0:LANES] * shrink + mixed[:, :LANES]
            lower = sums[i, pair, :, LANES : 2 * LANES] * shrink + mixed[:, LANES:]
            mixed = upper * inverse(lower)
            wo[rows, columns] = jnp.where(first_head, mixed[:half], mixed[half:]).astype(BF16)
        for n in range(2):
            columns = slice(n * width // 2, (n + 1) * width // 2)
            psend[i, n] = (part[rows, columns] + nn(wo[rows, :], po_v[:, columns])).astype(BF16)
            at = 2 * i + n
            results[at] = remote(
                psend.at[i, n], precv.at[i, n], ps_sem.at[at], pr_sem.at[at], mesh_id(band, other)
            )
            results[at].start()
    for i in (1, 0):
        node = iota((half, width // 2), 0) + i * half
        scale = (node < own_count).astype(F32)
        for n in range(2):
            results[2 * i + n].wait_recv()
            columns = slice(n * width // 2, (n + 1) * width // 2)
            summed = psend[i, n].astype(F32) + precv[i, n].astype(F32)
            total = lat[i, :, columns].astype(F32) + summed
            out[i * half : (i + 1) * half, columns] = (total * scale).astype(BF16)

    def sent(copies):
        for copy in copies:
            copy.wait_send()

    when(has_right, lambda: sent(halo[0::2] + direct[0::2] + passed[1::2] + handed[2:]))
    when(has_left, lambda: sent(halo[1::2] + direct[1::2] + passed[0::2] + handed[:2]))
    when(has_toward, lambda: sent(sends))
    sent(to_sibling + results)


def local(
    grid_in, mesh_in, counts, enc_edges, enc_bias, proc_bias, w_embed, enc_query, enc_key,
    enc_value, enc_out, proc_query, proc_key, proc_value, proc_out, mlp_gate, mlp_up, mlp_down,
):
    grid_rows, channels = grid_in.shape
    nodes, width = mesh_in.shape
    local_width = enc_query.shape[1]
    heads = local_width // HDIM
    hidden = mlp_gate.shape[1]
    half = nodes // 2
    edges = enc_edges.shape[0]
    enc_bias = enc_bias.reshape(edges * heads, nodes)
    proc_bias = proc_bias.reshape(-1, nodes)
    anywhere = pl.BlockSpec(memory_space=pl.ANY)
    dma = pltpu.SemaphoreType.DMA
    vmem = pltpu.VMEM
    scratch = [
        pltpu.SMEM(counts.shape, jnp.int32),
        pltpu.SMEM((edges, half), jnp.int32),
        vmem((RING * grid_rows, channels), BF16),
        vmem((RING * grid_rows, channels), F32),
        vmem((nodes, width), BF16),
        vmem((channels, width), BF16),
        vmem((width, local_width), BF16),
        vmem((width, local_width), BF16),
        vmem((width, local_width), BF16),
        vmem((width, width), BF16),
        vmem((width, local_width), BF16),
        vmem((width, local_width), BF16),
        vmem((width, local_width), BF16),
        vmem((local_width, width), BF16),
        vmem((width, hidden), BF16),
        vmem((width, hidden), BF16),
        vmem((hidden, width), BF16),
        vmem((2, 16 * heads, half), F32),
        vmem((2, proc_bias.shape[0], half), F32),
        vmem((heads // 2, 2, 2 * half, 3 * half), F32),
        vmem((3, heads, half, 2 * LANES), BF16),
        vmem((heads, 2 * LANES, LANES), BF16),
        vmem((16 * BLOCK, 16 * BLOCK), F32),
        vmem((16 * BLOCK, LANES), BF16),
        vmem((half * 16, channels), F32),
        vmem((half, 2 * heads * channels), BF16),
        vmem((2, half, width), BF16),
        vmem((4, half, width), BF16),
        vmem((2, heads // 2, nodes, LANES), BF16),
        vmem((2 * nodes, local_width), BF16),
        vmem((2 * nodes, 2 * local_width), BF16),
        vmem((nodes, hidden), BF16),
        vmem((nodes, width), F32),
        vmem((2, heads // 2, nodes, LANES), F32),
        vmem((2, heads // 2, nodes, 2 * LANES), F32),
        vmem((nodes, local_width), BF16),
        vmem((2, 2, half, width // 2), BF16),
        vmem((2, 2, half, width // 2), BF16),
        dma((21,)),
        dma((2 * CHUNKS,)),
        dma((2 * CHUNKS,)),
        dma((2 * CHUNKS,)),
        dma((2 * CHUNKS,)),
        dma((4,)),
        dma((4,)),
        dma((2,)),
        dma((2,)),
        dma((2,)),
        dma((2,)),
        dma((6,)),
        dma((6,)),
        dma((4,)),
        dma((4,)),
        dma((4,)),
        dma((4,)),
    ]
    return pl.pallas_call(
        kernel,
        out_shape=pltpu.VMEM((nodes, width), BF16),
        in_specs=[anywhere] * 18,
        out_specs=pl.BlockSpec(memory_space=pltpu.VMEM),
        scratch_shapes=scratch,
        compiler_params=pltpu.CompilerParams(
            collective_id=0, has_side_effects=True, vmem_limit_bytes=VMEM_BYTES
        ),
        name="encoder_processor",
    )(
        counts, enc_edges, grid_in, mesh_in, enc_bias, proc_bias, w_embed, enc_query, enc_key,
        enc_value, enc_out, proc_query, proc_key, proc_value, proc_out, mlp_gate, mlp_up, mlp_down,
    )


def solution(mesh):
    heads = P(None, "head")
    in_specs = (
        P("band", None), P("band", None), P(), P(None, "band"), P(None, "head", "band"),
        P(None, "head", "band"), P(), heads, heads, heads, P(), heads, heads, heads,
        P("head", None), heads, heads, P("head", None),
    )
    return jax.shard_map(
        local, mesh=mesh, in_specs=in_specs, out_specs=P("band", None), check_vma=False
    )
```

```python
import jax
import jax.numpy as jnp
from jax import lax
from jax.experimental import pallas as pl
from jax.experimental.pallas import tpu as pltpu
from jax.sharding import PartitionSpec as P

HDIM = 64
EPSILON = 1e-05
NEGATIVE = -1e30
F32 = jnp.float32
BF16 = jnp.bfloat16
LANES = 128
BLOCK = 16
SHARES = (4, 4, 4, 3, 1)
CHUNKS = len(SHARES)
RING = 4
VMEM_BYTES = 60 * 1024 * 1024


def nn(left, right):
    return lax.dot_general(left, right, (((1,), (0,)), ((), ())), preferred_element_type=F32)


def nt(left, right):
    return lax.dot_general(left, right, (((1,), (1,)), ((), ())), preferred_element_type=F32)


def inverse(values):
    guess = pl.reciprocal(values, approx=True)
    return guess * (2.0 - values * guess)


def iota(shape, dim):
    return lax.broadcasted_iota(jnp.int32, shape, dim)


def normalize(rows):
    centred = rows - jnp.mean(rows, -1, keepdims=True)
    variance = jnp.mean(centred * centred, -1, keepdims=True)
    return (centred * lax.rsqrt(variance + EPSILON)).astype(BF16)


def kernel(
    counts, enc_edges, grid, mesh_in, enc_bias, proc_bias, w_embed,
    enc_query, enc_key, enc_value, enc_out,
    proc_query, proc_key, proc_value, proc_out, mlp_gate, mlp_up, mlp_down,
    out,
    count_s, edge_s, ext, extf, mesh_v, we_v, eq_v, ek_v, ev_v, eo_v, pq_v, pk_v, pv_v, po_v,
    gate_v, up_v, down_v, eb_v, pb_v, bd, qk, vmap, apart, marks, g, u_s, lat, nx, q_s, k_s, v_s,
    hid, part, peaks, sums, wo, psend, precv,
    load_sem, gs_sem, gr_sem, fs_sem, fr_sem, xs_sem, xr_sem, ls_sem, lr_sem,
    hs_sem, hr_sem, ks_sem, kr_sem, ps_sem, pr_sem,
):
    band, core = lax.axis_index("band"), lax.axis_index("head")
    bands = lax.axis_size("band")
    other = 1 - core
    has_left, has_right = band > 0, band < bands - 1
    left, right = jnp.maximum(band - 1, 0), jnp.minimum(band + 1, bands - 1)
    toward = jnp.where(core == 1, right, left)
    has_toward = band != toward
    beyond = jnp.where(core == 1, left, right)
    has_beyond = band != beyond
    grid_rows = grid.shape[0]
    nodes = mesh_in.shape[0]
    half = nodes // 2
    width = mesh_in.shape[1]
    local_width = enc_query.shape[1]
    local_heads = local_width // HDIM
    pairs = local_heads // 2
    edges = edge_s.shape[0]

    def when(condition, action):
        pl.when(condition)(action)

    def mesh_id(b, h):
        return {"band": b, "head": h}

    def ring_rows(b, start, size):
        first = lax.rem(b, RING) * grid_rows + start
        return pl.ds(pl.multiple_of(first, LANES), size)

    own = pl.ds(pl.multiple_of(core * local_width, LANES), local_width)
    theirs = pl.ds(pl.multiple_of(other * local_width, LANES), local_width)
    bias_rows = enc_bias.shape[0]
    sources = [
        (grid, ext.at[ring_rows(band, 0, grid_rows)]),
        (mesh_in, mesh_v),
        (enc_edges.at[:, pl.ds(pl.multiple_of(core * half, LANES), half)], edge_s),
        (counts, count_s),
        (enc_query, eq_v),
        (w_embed, we_v),
        (enc_key, ek_v),
        (enc_value, ev_v),
        (enc_bias.at[:, pl.ds(0, half)], eb_v.at[0, pl.ds(0, bias_rows)]),
        (enc_bias.at[:, pl.ds(half, half)], eb_v.at[1, pl.ds(0, bias_rows)]),
        (proc_bias.at[:, pl.ds(0, half)], pb_v.at[0]),
        (proc_bias.at[:, pl.ds(half, half)], pb_v.at[1]),
        (enc_out.at[own], eo_v.at[pl.ds(0, local_width)]),
        (enc_out.at[theirs], eo_v.at[pl.ds(local_width, local_width)]),
        (mlp_gate, gate_v),
        (mlp_up, up_v),
        (proc_query, pq_v),
        (proc_key, pk_v),
        (proc_value, pv_v),
        (mlp_down, down_v),
        (proc_out, po_v),
    ]
    loads = [
        pltpu.make_async_copy(src, dst, load_sem.at[i]) for i, (src, dst) in enumerate(sources)
    ]
    (
        l_grid, l_mesh, l_edge, l_count, l_eq, l_we, l_ek, l_ev, l_eb0, l_eb1, l_pb0, l_pb1, l_eo0, l_eo1,
        l_gate, l_up, l_pq, l_pk, l_pv, l_down, l_po,
    ) = loads
    barrier = pltpu.get_barrier_semaphore()
    def greet(device):
        pl.semaphore_signal(barrier, inc=1, device_id=device, device_id_type=pl.DeviceIdType.MESH)

    def greet_band(b):
        greet(mesh_id(b, core))
        greet(mesh_id(b, other))

    when(has_right, lambda: greet_band(right))
    when(has_left, lambda: greet_band(left))
    greet(mesh_id(band, other))
    for load in loads[:8]:
        load.start()
    pl.semaphore_wait(barrier, 1 + jnp.where(has_left, 2, 0) + jnp.where(has_right, 2, 0))

    def remote(src, dst, send, recv, device):
        return pltpu.make_async_remote_copy(
            src_ref=src, dst_ref=dst, send_sem=send, recv_sem=recv,
            device_id=device, device_id_type=pl.DeviceIdType.MESH,
        )

    unit = grid_rows // 2 // 16
    sizes = [share * unit for share in SHARES]
    starts = [sum(sizes[:k]) for k in range(CHUNKS)]

    def piece_of(b, which, k):
        return ext.at[ring_rows(b, which * (grid_rows // 2) + starts[k], sizes[k])]

    to_right, to_left, halo, passed, passing = [], [], [], [], []
    for k in range(CHUNKS):
        mine = piece_of(band, core, k)
        for d, (copies, device) in enumerate(
            ((to_right, mesh_id(right, 0)), (to_left, mesh_id(left, 1)))
        ):
            copies.append(
                remote(
                    mine, mine, gs_sem.at[d * CHUNKS + k], gr_sem.at[core * CHUNKS + k], device
                )
            )
        for which in range(2):
            slot = which * CHUNKS + k
            near, far = piece_of(toward, which, k), piece_of(beyond, which, k)
            halo.append(
                remote(near, near, gs_sem.at[slot], gr_sem.at[slot], mesh_id(toward, other))
            )
            passing.append(
                remote(near, near, fs_sem.at[slot], fr_sem.at[slot], mesh_id(band, other))
            )
            passed.append(
                remote(far, far, fs_sem.at[slot], fr_sem.at[slot], mesh_id(band, other))
            )
    sides = (has_left, has_right)

    def start_all(copies):
        for copy in copies:
            copy.start()

    l_grid.wait()
    when(has_left, to_left[0].start)
    when(has_right, to_right[0].start)
    when(has_left, lambda: start_all(to_left[1:]))
    when(has_right, lambda: start_all(to_right[1:]))
    for load in loads[8:]:
        load.start()

    padding = eb_v.shape[1] - bias_rows
    eb_v[:, pl.ds(bias_rows, padding), :] = jnp.zeros((2, padding, half), F32)
    l_mesh.wait()
    normed_mesh = normalize(mesh_v[...].astype(F32))
    l_eq.wait()
    queries = nn(normed_mesh, eq_v[...]).astype(BF16)
    queries = (queries.astype(F32) * HDIM**-0.5).astype(BF16)
    l_we.wait()
    l_ek.wait()
    key_map = nn(we_v[...], ek_v[...]).astype(BF16)
    l_ev.wait()
    value_map = nn(we_v[...], ev_v[...])
    low_lanes = iota((LANES, LANES), 1) < HDIM
    for pair in range(pairs):
        both = value_map[:, pair * LANES : (pair + 1) * LANES]
        vmap[pair, 0:LANES, :] = jnp.where(low_lanes, both, 0.0).astype(BF16)
        vmap[pair, LANES : 2 * LANES, :] = jnp.where(low_lanes, 0.0, both).astype(BF16)
    l_eb0.wait()
    l_eb1.wait()
    low_half = iota((nodes, LANES), 1) < HDIM
    for h in range(local_heads):
        columns = slice(h // 2 * LANES, (h // 2 + 1) * LANES)
        keep = low_half if h % 2 == 0 else jnp.logical_not(low_half)
        masked = jnp.where(keep, queries[:, columns].astype(F32), 0.0).astype(BF16)
        mapped = nt(masked, key_map[:, columns]).astype(BF16)
        for n in range(2):
            bias = eb_v[n, pl.ds(h, 16, stride=local_heads), :]
            high = bias.astype(BF16).astype(F32)
            middle = (bias - high).astype(BF16).astype(F32)
            low = (bias - high) - middle
            lanes = jnp.concatenate([high, middle, low, jnp.zeros((LANES - 48, half), F32)], 0)
            slot = lax.rem(core + n, 2)
            qk[slot, h, :, 0:LANES] = mapped[n * half : (n + 1) * half]
            qk[slot, h, :, LANES : 2 * LANES] = lanes.T.astype(BF16)
    exchange = [
        remote(qk.at[1], qk.at[2], xs_sem.at[0], xr_sem.at[0], mesh_id(band, other)),
        remote(vmap.at[0:pairs], vmap.at[pairs : 2 * pairs], xs_sem.at[1], xr_sem.at[1], mesh_id(band, other)),
    ]
    for copy in exchange:
        copy.start()

    reach = half
    span = nodes + 2 * reach
    window = 3 * half
    l_count.wait()
    own_count = count_s[band]
    lower_count = jnp.where(has_left, count_s[left], 0)
    upper_count = jnp.where(has_right, count_s[right], 0)
    key_slot = iota((1, span), 1)
    before, after = key_slot < reach, key_slot >= reach + nodes
    limit = jnp.where(before, lower_count, jnp.where(after, upper_count, own_count))
    place = key_slot - jnp.where(before, reach - nodes, jnp.where(after, reach + nodes, reach))
    live = jnp.where(place < limit, 1, 0)
    offset = iota((half, window), 1) - iota((half, window), 0)
    in_window = (offset >= 0) & (offset <= 2 * reach)
    l_pb0.wait()
    l_pb1.wait()
    last = [pb_v[i, pl.ds(2 * reach * local_heads, local_heads), :].T for i in range(2)]

    def window_bias(h):
        for i in range(2):
            turned = pb_v[i, pl.ds(h, 2 * reach, stride=local_heads), :].T
            wide = jnp.concatenate([turned, jnp.zeros((half, window - 2 * reach), F32)], 1)
            skewed = pltpu.roll(wide, 0, 1, stride=1, stride_axis=0)
            final = last[i][:, h : h + 1]
            skewed = jnp.where(offset == 2 * reach, final, skewed)
            usable = in_window & (
                (live[:, i * half : i * half + window] > 0) | (offset == reach)
            )
            bd[h // 2, i, h % 2 * half : (h % 2 + 1) * half] = jnp.where(usable, skewed, NEGATIVE)

    def widen(rows):
        extf[rows, :] = ext[rows, :].astype(F32)

    def arrive(k):
        for which in range(2):
            halo[2 * k + which].wait_recv()
            passing[2 * k + which].start()
        for which in range(2):
            widen(ring_rows(toward, which * (grid_rows // 2) + starts[k], sizes[k]))

    def arrive_passed(k):
        for which in range(2):
            passed[2 * k + which].wait_recv()
            widen(ring_rows(beyond, which * (grid_rows // 2) + starts[k], sizes[k]))

    blocks = half // BLOCK
    block_rows = 16 * BLOCK
    row = iota((block_rows, block_rows), 0)
    column = iota((block_rows, block_rows), 1)
    same = ((row & (BLOCK - 1)) == (column & (BLOCK - 1))) & (column < edges * BLOCK)
    apart[...] = jnp.where(same, 0.0, NEGATIVE)
    lane = iota((block_rows, LANES), 1)
    edge_of_row = iota((block_rows, LANES), 0) >> 4
    mark = (lane < 48) & ((lane & 15) == edge_of_row)
    marks[...] = jnp.where(mark, 1.0, 0.0).astype(BF16)
    v_s[...] = jnp.ones(v_s.shape, BF16)
    for block in range(blocks):
        unused = slice(block * block_rows + edges * BLOCK, (block + 1) * block_rows)
        g[unused, :] = jnp.zeros((block_rows - edges * BLOCK, LANES), F32)
    l_edge.wait()
    for h in range(local_heads):
        window_bias(h)
    for k in range(CHUNKS):
        widen(ring_rows(band, 2 * starts[k], 2 * sizes[k]))
        when(has_toward, lambda k=k: arrive(k))
        if k > 0:
            when(has_beyond, lambda k=k: arrive_passed(k - 1))
    for copy in exchange:
        copy.wait()
    when(has_beyond, lambda: arrive_passed(CHUNKS - 1))

    def gather(block):
        for edge in range(edges):
            found = []
            for n in range(BLOCK):
                row = edge_s[edge, block * BLOCK + n] & (RING * grid_rows - 1)
                found.append(extf[pl.ds(row, 1), :])
            for n in range(BLOCK):
                g[pl.ds(block * block_rows + edge * BLOCK + n, 1), :] = found[n]

    ones = jnp.ones((block_rows, LANES), BF16)
    quarter = half // 2
    eighth = quarter // 2
    sixteenth = eighth // 2
    parts = (
        lambda which: pl.ds(pl.multiple_of(which * eighth, 16), eighth),
        lambda which: pl.ds(pl.multiple_of(quarter + which * sixteenth, 16), sixteenth),
        lambda which: pl.ds(quarter + eighth, eighth),
    )

    def window_copy(section, which, n):
        rows = parts[section](which)
        return remote(
            nx.at[1 + core, rows], nx.at[3 * other, rows],
            hs_sem.at[2 * section + n], hr_sem.at[3 * other + section], mesh_id(toward, which),
        )

    sends = [
        window_copy(section, which, n) for section in range(3) for n, which in enumerate((core, other))
    ]
    to_sibling = [
        remote(
            lat.at[core, pl.ds(n * quarter, quarter)], lat.at[core, pl.ds(n * quarter, quarter)],
            ls_sem.at[n], lr_sem.at[n], mesh_id(band, other),
        )
        for n in range(2)
    ]
    from_sibling = [
        remote(
            lat.at[other, pl.ds(n * quarter, quarter)], lat.at[other, pl.ds(n * quarter, quarter)],
            ls_sem.at[n], lr_sem.at[n], mesh_id(band, other),
        )
        for n in range(2)
    ]
    handed = []
    for d in range(2):
        for section in range(2):
            here = nx.at[3 * d, parts[section](core)]
            handed.append(
                remote(
                    here, here, ks_sem.at[2 * d + section], kr_sem.at[2 * d + section],
                    mesh_id(band, other),
                )
            )

    def landed(d, section):
        here = nx.at[3 * d, parts[section](core)]
        remote(
            here, here, hs_sem.at[2 * section], hr_sem.at[3 * d + section], mesh_id(toward, core)
        ).wait_recv()

    def hand(d):
        for section in range(2):
            landed(d, section)
            handed[2 * d + section].start()

    def all_here(d):
        landed(d, 2)
        for section in range(2):
            handed[2 * d + section].wait_recv()

    def attend(block):
        rows = slice(block * BLOCK, (block + 1) * BLOCK)
        near = g[block * block_rows : (block + 1) * block_rows, :].astype(BF16)
        asked = jnp.concatenate(
            [qk[s, :, rows, :].reshape(local_heads * BLOCK, 2 * LANES) for s in (0, 2)], 0
        )
        scores = nt(asked, jnp.concatenate([near, marks[...]], 1)) + apart[...]
        peak = jnp.max(scores, 1, keepdims=True)
        weights = jnp.exp(scores - peak).astype(BF16)
        mixed = nn(weights, jnp.concatenate([near, ones], 1))
        mixed = (mixed[:, :LANES] * inverse(mixed[:, LANES:])).astype(BF16)
        for h in range(2 * local_heads):
            u_s[rows, h * LANES : (h + 1) * LANES] = mixed[h * BLOCK : (h + 1) * BLOCK]

    l_eo0.wait()
    l_eo1.wait()
    gather(0)
    for block in range(blocks):
        if block + 1 < blocks:
            gather(block + 1)
        attend(block)
    attended = jnp.concatenate(
        [
            nn(u_s[:, pair * 2 * LANES : (pair + 1) * 2 * LANES], vmap[pair])
            for pair in range(2 * pairs)
        ],
        1,
    ).astype(BF16)
    own_mesh = mesh_v[pl.ds(pl.multiple_of(core * half, half), half), :].astype(F32)
    latent = (own_mesh + nn(attended, eo_v[...])).astype(BF16)
    lat[core] = latent
    nx[1 + core] = normalize(latent.astype(F32))
    when(has_toward, lambda: start_all(sends))
    start_all(to_sibling)

    def clear(s):
        nx[s] = jnp.zeros((half, width), BF16)

    when(jnp.logical_not(has_left), lambda: clear(0))
    when(jnp.logical_not(has_right), lambda: clear(3))
    first_head = iota((half, LANES), 1) < HDIM
    step = 512
    steps = gate_v.shape[1] // step

    def keys_values(source, start):
        rows = pl.ds(pl.multiple_of(start, half), half)
        k_s[rows, :] = nn(source, pk_v[...]).astype(BF16)
        values = nn(source, pv_v[...]).astype(BF16)
        for pair in range(pairs):
            v_s[rows, pair * 2 * LANES : pair * 2 * LANES + LANES] = values[
                :, pair * LANES : (pair + 1) * LANES
            ]

    def project(which):
        source = nx[1 + which]
        win_query = nn(source, pq_v[...]).astype(BF16)
        win_query = win_query.astype(F32) * HDIM**-0.5
        for pair in range(pairs):
            both = win_query[:, pair * LANES : (pair + 1) * LANES]
            q_s[which, pair, 0:half, :] = jnp.where(first_head, both, 0.0).astype(BF16)
            q_s[which, pair, half:nodes, :] = jnp.where(first_head, 0.0, both).astype(BF16)
        keys_values(source, (1 + which) * half)
        rows = pl.ds(pl.multiple_of(which * half, half), half)
        for ch in range(steps):
            columns = slice(ch * step, (ch + 1) * step)
            gated = nn(source, gate_v[:, columns])
            raised = nn(source, up_v[:, columns])
            activated = 0.5 * gated * (1.0 + jnp.tanh(0.5 * gated)) * raised
            hid[rows, columns] = activated.astype(BF16)

    for load in (l_pq, l_pk, l_pv, l_gate, l_up, l_down, l_po):
        load.wait()
    project(core)
    for copy in from_sibling:
        copy.wait_recv()
    nx[2 - core] = normalize(lat[other].astype(F32))
    project(other)

    when(has_right, lambda: hand(1))
    own_keys = slice(half, 3 * half)
    for i in (1, 0):
        held = slice((1 - i) * half, (3 - i) * half)
        for pair in range(pairs):
            if pair % 2 == 0:
                at = ((1 - i) * pairs + pair) // 2 * width // pairs
                columns = slice(at, at + width // pairs)
                part[:, columns] = nn(hid[...], down_v[:, columns])
            columns = slice(pair * LANES, (pair + 1) * LANES)
            scores = nt(q_s[i, pair], k_s[own_keys, columns]) + bd[pair, i, :, held]
            peak = jnp.max(scores, 1, keepdims=True)
            weights = jnp.exp(scores - peak).astype(BF16)
            peaks[i, pair] = jnp.broadcast_to(peak, (nodes, LANES))
            sums[i, pair] = nn(weights, v_s[own_keys, pair * 2 * LANES : (pair + 1) * 2 * LANES])
    when(has_left, lambda: hand(0))
    results = [None] * 4
    for i in (1, 0):
        when(sides[i], lambda: all_here(i))
        rows = slice(i * half, (i + 1) * half)
        seen = slice(3 * i * half, (3 * i + 1) * half)
        held = slice(2 * i * half, (2 * i + 1) * half)
        keys_values(nx[3 * i], 3 * i * half)
        for pair in range(pairs):
            columns = slice(pair * LANES, (pair + 1) * LANES)
            scores = nt(q_s[i, pair], k_s[seen, columns]) + bd[pair, i, :, held]
            before = peaks[i, pair]
            peak = jnp.maximum(before, jnp.max(scores, 1, keepdims=True))
            weights = jnp.exp(scores - peak).astype(BF16)
            mixed = nn(weights, v_s[seen, pair * 2 * LANES : (pair + 1) * 2 * LANES])
            shrink = jnp.exp(before - peak)
            upper = sums[i, pair, :, 0:LANES] * shrink + mixed[:, :LANES]
            lower = sums[i, pair, :, LANES : 2 * LANES] * shrink + mixed[:, LANES:]
            mixed = upper * inverse(lower)
            wo[rows, columns] = jnp.where(first_head, mixed[:half], mixed[half:]).astype(BF16)
        for n in range(2):
            columns = slice(n * width // 2, (n + 1) * width // 2)
            psend[i, n] = (part[rows, columns] + nn(wo[rows, :], po_v[:, columns])).astype(BF16)
            at = 2 * i + n
            results[at] = remote(
                psend.at[i, n], precv.at[i, n], ps_sem.at[at], pr_sem.at[at], mesh_id(band, other)
            )
            results[at].start()
    for i in (1, 0):
        node = iota((half, width // 2), 0) + i * half
        scale = (node < own_count).astype(F32)
        for n in range(2):
            results[2 * i + n].wait_recv()
            columns = slice(n * width // 2, (n + 1) * width // 2)
            summed = psend[i, n].astype(F32) + precv[i, n].astype(F32)
            total = lat[i, :, columns].astype(F32) + summed
            out[i * half : (i + 1) * half, columns] = (total * scale).astype(BF16)

    def sent(copies):
        for copy in copies:
            copy.wait_send()

    when(has_right, lambda: sent(to_right + handed[2:]))
    when(has_left, lambda: sent(to_left + handed[:2]))
    when(has_toward, lambda: sent(sends + passing))
    sent(to_sibling + results)


def local(
    grid_in, mesh_in, counts, enc_edges, enc_bias, proc_bias, w_embed, enc_query, enc_key,
    enc_value, enc_out, proc_query, proc_key, proc_value, proc_out, mlp_gate, mlp_up, mlp_down,
):
    grid_rows, channels = grid_in.shape
    nodes, width = mesh_in.shape
    local_width = enc_query.shape[1]
    heads = local_width // HDIM
    hidden = mlp_gate.shape[1]
    half = nodes // 2
    edges = enc_edges.shape[0]
    enc_bias = enc_bias.reshape(edges * heads, nodes)
    proc_bias = proc_bias.reshape(-1, nodes)
    anywhere = pl.BlockSpec(memory_space=pl.ANY)
    dma = pltpu.SemaphoreType.DMA
    vmem = pltpu.VMEM
    scratch = [
        pltpu.SMEM(counts.shape, jnp.int32),
        pltpu.SMEM((edges, half), jnp.int32),
        vmem((RING * grid_rows, channels), BF16),
        vmem((RING * grid_rows, channels), F32),
        vmem((nodes, width), BF16),
        vmem((channels, width), BF16),
        vmem((width, local_width), BF16),
        vmem((width, local_width), BF16),
        vmem((width, local_width), BF16),
        vmem((width, width), BF16),
        vmem((width, local_width), BF16),
        vmem((width, local_width), BF16),
        vmem((width, local_width), BF16),
        vmem((local_width, width), BF16),
        vmem((width, hidden), BF16),
        vmem((width, hidden), BF16),
        vmem((hidden, width), BF16),
        vmem((2, 16 * heads, half), F32),
        vmem((2, proc_bias.shape[0], half), F32),
        vmem((heads // 2, 2, 2 * half, 3 * half), F32),
        vmem((3, heads, half, 2 * LANES), BF16),
        vmem((heads, 2 * LANES, LANES), BF16),
        vmem((16 * BLOCK, 16 * BLOCK), F32),
        vmem((16 * BLOCK, LANES), BF16),
        vmem((half * 16, channels), F32),
        vmem((half, 2 * heads * channels), BF16),
        vmem((2, half, width), BF16),
        vmem((4, half, width), BF16),
        vmem((2, heads // 2, nodes, LANES), BF16),
        vmem((2 * nodes, local_width), BF16),
        vmem((2 * nodes, 2 * local_width), BF16),
        vmem((nodes, hidden), BF16),
        vmem((nodes, width), F32),
        vmem((2, heads // 2, nodes, LANES), F32),
        vmem((2, heads // 2, nodes, 2 * LANES), F32),
        vmem((nodes, local_width), BF16),
        vmem((2, 2, half, width // 2), BF16),
        vmem((2, 2, half, width // 2), BF16),
        dma((21,)),
        dma((2 * CHUNKS,)),
        dma((2 * CHUNKS,)),
        dma((2 * CHUNKS,)),
        dma((2 * CHUNKS,)),
        dma((2,)),
        dma((2,)),
        dma((2,)),
        dma((2,)),
        dma((6,)),
        dma((6,)),
        dma((4,)),
        dma((4,)),
        dma((4,)),
        dma((4,)),
    ]
    return pl.pallas_call(
        kernel,
        out_shape=pltpu.VMEM((nodes, width), BF16),
        in_specs=[anywhere] * 18,
        out_specs=pl.BlockSpec(memory_space=pltpu.VMEM),
        scratch_shapes=scratch,
        compiler_params=pltpu.CompilerParams(
            collective_id=0, has_side_effects=True, vmem_limit_bytes=VMEM_BYTES
        ),
        name="encoder_processor",
    )(
        counts, enc_edges, grid_in, mesh_in, enc_bias, proc_bias, w_embed, enc_query, enc_key,
        enc_value, enc_out, proc_query, proc_key, proc_value, proc_out, mlp_gate, mlp_up, mlp_down,
    )


def solution(mesh):
    heads = P(None, "head")
    in_specs = (
        P("band", None), P("band", None), P(), P(None, "band"), P(None, "head", "band"),
        P(None, "head", "band"), P(), heads, heads, heads, P(), heads, heads, heads,
        P("head", None), heads, heads, P("head", None),
    )
    return jax.shard_map(
        local, mesh=mesh, in_specs=in_specs, out_specs=P("band", None), check_vma=False
    )
```

```python
import jax
import jax.numpy as jnp
from jax import lax
from jax.experimental import pallas as pl
from jax.experimental.pallas import tpu as pltpu
from jax.sharding import PartitionSpec as P

HDIM = 64
EPSILON = 1e-05
NEGATIVE = -1e30
F32 = jnp.float32
BF16 = jnp.bfloat16
LANES = 128
BLOCK = 16
SHARES = (4, 4, 4, 3, 1)
CHUNKS = len(SHARES)
RING = 4
VMEM_BYTES = 60 * 1024 * 1024


def nn(left, right):
    return lax.dot_general(left, right, (((1,), (0,)), ((), ())), preferred_element_type=F32)


def nt(left, right):
    return lax.dot_general(left, right, (((1,), (1,)), ((), ())), preferred_element_type=F32)


def inverse(values):
    guess = pl.reciprocal(values, approx=True)
    return guess * (2.0 - values * guess)


def iota(shape, dim):
    return lax.broadcasted_iota(jnp.int32, shape, dim)


def normalize(rows):
    centred = rows - jnp.mean(rows, -1, keepdims=True)
    variance = jnp.mean(centred * centred, -1, keepdims=True)
    return (centred * lax.rsqrt(variance + EPSILON)).astype(BF16)


def kernel(
    counts, enc_edges, grid, mesh_in, enc_bias, proc_bias, w_embed,
    enc_query, enc_key, enc_value, enc_out,
    proc_query, proc_key, proc_value, proc_out, mlp_gate, mlp_up, mlp_down,
    out,
    count_s, edge_s, ext, extf, mesh_v, we_v, eq_v, ek_v, ev_v, eo_v, pq_v, pk_v, pv_v, po_v,
    gate_v, up_v, down_v, eb_v, pb_v, bd, qk, vmap, apart, marks, g, u_s, lat, nx, q_s, k_s, v_s,
    hid, part, peaks, sums, wo, psend, precv,
    load_sem, gs_sem, gr_sem, fs_sem, fr_sem, xs_sem, xr_sem, ls_sem, lr_sem,
    hs_sem, hr_sem, ks_sem, kr_sem, ps_sem, pr_sem,
):
    band, core = lax.axis_index("band"), lax.axis_index("head")
    bands = lax.axis_size("band")
    other = 1 - core
    has_left, has_right = band > 0, band < bands - 1
    left, right = jnp.maximum(band - 1, 0), jnp.minimum(band + 1, bands - 1)
    toward = jnp.where(core == 1, right, left)
    has_toward = band != toward
    beyond = jnp.where(core == 1, left, right)
    has_beyond = band != beyond
    grid_rows = grid.shape[0]
    nodes = mesh_in.shape[0]
    half = nodes // 2
    width = mesh_in.shape[1]
    local_width = enc_query.shape[1]
    local_heads = local_width // HDIM
    pairs = local_heads // 2
    edges = edge_s.shape[0]

    def when(condition, action):
        pl.when(condition)(action)

    def mesh_id(b, h):
        return {"band": b, "head": h}

    def ring_rows(b, start, size):
        first = lax.rem(b, RING) * grid_rows + start
        return pl.ds(pl.multiple_of(first, LANES), size)

    own = pl.ds(pl.multiple_of(core * local_width, LANES), local_width)
    theirs = pl.ds(pl.multiple_of(other * local_width, LANES), local_width)
    bias_rows = enc_bias.shape[0]
    sources = [
        (grid, ext.at[ring_rows(band, 0, grid_rows)]),
        (mesh_in, mesh_v),
        (enc_edges.at[:, pl.ds(pl.multiple_of(core * half, LANES), half)], edge_s),
        (counts, count_s),
        (enc_query, eq_v),
        (w_embed, we_v),
        (enc_key, ek_v),
        (enc_value, ev_v),
        (enc_bias.at[:, pl.ds(0, half)], eb_v.at[0, pl.ds(0, bias_rows)]),
        (enc_bias.at[:, pl.ds(half, half)], eb_v.at[1, pl.ds(0, bias_rows)]),
        (proc_bias.at[:, pl.ds(0, half)], pb_v.at[0]),
        (proc_bias.at[:, pl.ds(half, half)], pb_v.at[1]),
        (enc_out.at[own], eo_v.at[pl.ds(0, local_width)]),
        (enc_out.at[theirs], eo_v.at[pl.ds(local_width, local_width)]),
        (mlp_gate, gate_v),
        (mlp_up, up_v),
        (proc_query, pq_v),
        (proc_key, pk_v),
        (proc_value, pv_v),
        (mlp_down, down_v),
        (proc_out, po_v),
    ]
    loads = [
        pltpu.make_async_copy(src, dst, load_sem.at[i]) for i, (src, dst) in enumerate(sources)
    ]
    (
        l_grid, l_mesh, l_edge, l_count, l_eq, l_we, l_ek, l_ev, l_eb0, l_eb1, l_pb0, l_pb1, l_eo0, l_eo1,
        l_gate, l_up, l_pq, l_pk, l_pv, l_down, l_po,
    ) = loads
    barrier = pltpu.get_barrier_semaphore()
    def greet(device):
        pl.semaphore_signal(barrier, inc=1, device_id=device, device_id_type=pl.DeviceIdType.MESH)

    def greet_band(b):
        greet(mesh_id(b, core))
        greet(mesh_id(b, other))

    when(has_right, lambda: greet_band(right))
    when(has_left, lambda: greet_band(left))
    greet(mesh_id(band, other))
    for load in loads[:8]:
        load.start()
    pl.semaphore_wait(barrier, 1 + jnp.where(has_left, 2, 0) + jnp.where(has_right, 2, 0))

    def remote(src, dst, send, recv, device):
        return pltpu.make_async_remote_copy(
            src_ref=src, dst_ref=dst, send_sem=send, recv_sem=recv,
            device_id=device, device_id_type=pl.DeviceIdType.MESH,
        )

    unit = grid_rows // 2 // 16
    sizes = [share * unit for share in SHARES]
    starts = [sum(sizes[:k]) for k in range(CHUNKS)]

    def piece_of(b, which, k):
        return ext.at[ring_rows(b, which * (grid_rows // 2) + starts[k], sizes[k])]

    to_right, to_left, halo, passed, passing = [], [], [], [], []
    for k in range(CHUNKS):
        mine = piece_of(band, core, k)
        for d, (copies, device) in enumerate(
            ((to_right, mesh_id(right, 0)), (to_left, mesh_id(left, 1)))
        ):
            copies.append(
                remote(
                    mine, mine, gs_sem.at[d * CHUNKS + k], gr_sem.at[core * CHUNKS + k], device
                )
            )
        for which in range(2):
            slot = which * CHUNKS + k
            near, far = piece_of(toward, which, k), piece_of(beyond, which, k)
            halo.append(
                remote(near, near, gs_sem.at[slot], gr_sem.at[slot], mesh_id(toward, other))
            )
            passing.append(
                remote(near, near, fs_sem.at[slot], fr_sem.at[slot], mesh_id(band, other))
            )
            passed.append(
                remote(far, far, fs_sem.at[slot], fr_sem.at[slot], mesh_id(band, other))
            )
    sides = (has_left, has_right)

    def start_all(copies):
        for copy in copies:
            copy.start()

    l_grid.wait()
    when(has_left, to_left[0].start)
    when(has_right, to_right[0].start)
    when(has_left, lambda: start_all(to_left[1:]))
    when(has_right, lambda: start_all(to_right[1:]))
    for load in loads[8:]:
        load.start()

    padding = eb_v.shape[1] - bias_rows
    eb_v[:, pl.ds(bias_rows, padding), :] = jnp.zeros((2, padding, half), F32)
    l_mesh.wait()
    normed_mesh = normalize(mesh_v[...].astype(F32))
    l_eq.wait()
    queries = nn(normed_mesh, eq_v[...]).astype(BF16)
    queries = (queries.astype(F32) * HDIM**-0.5).astype(BF16)
    l_we.wait()
    l_ek.wait()
    key_map = nn(we_v[...], ek_v[...]).astype(BF16)
    l_ev.wait()
    value_map = nn(we_v[...], ev_v[...])
    low_lanes = iota((LANES, LANES), 1) < HDIM
    for pair in range(pairs):
        both = value_map[:, pair * LANES : (pair + 1) * LANES]
        vmap[pair, 0:LANES, :] = jnp.where(low_lanes, both, 0.0).astype(BF16)
        vmap[pair, LANES : 2 * LANES, :] = jnp.where(low_lanes, 0.0, both).astype(BF16)
    l_eb0.wait()
    l_eb1.wait()
    low_half = iota((nodes, LANES), 1) < HDIM
    for h in range(local_heads):
        columns = slice(h // 2 * LANES, (h // 2 + 1) * LANES)
        keep = low_half if h % 2 == 0 else jnp.logical_not(low_half)
        masked = jnp.where(keep, queries[:, columns].astype(F32), 0.0).astype(BF16)
        mapped = nt(masked, key_map[:, columns]).astype(BF16)
        for n in range(2):
            bias = eb_v[n, pl.ds(h, 16, stride=local_heads), :]
            high = bias.astype(BF16).astype(F32)
            middle = (bias - high).astype(BF16).astype(F32)
            low = (bias - high) - middle
            lanes = jnp.concatenate([high, middle, low, jnp.zeros((LANES - 48, half), F32)], 0)
            slot = lax.rem(core + n, 2)
            qk[slot, h, :, 0:LANES] = mapped[n * half : (n + 1) * half]
            qk[slot, h, :, LANES : 2 * LANES] = lanes.T.astype(BF16)
    exchange = [
        remote(qk.at[1], qk.at[2], xs_sem.at[0], xr_sem.at[0], mesh_id(band, other)),
        remote(vmap.at[0:pairs], vmap.at[pairs : 2 * pairs], xs_sem.at[1], xr_sem.at[1], mesh_id(band, other)),
    ]
    for copy in exchange:
        copy.start()

    reach = half
    span = nodes + 2 * reach
    window = 3 * half
    l_count.wait()
    own_count = count_s[band]
    lower_count = jnp.where(has_left, count_s[left], 0)
    upper_count = jnp.where(has_right, count_s[right], 0)
    key_slot = iota((1, span), 1)
    before, after = key_slot < reach, key_slot >= reach + nodes
    limit = jnp.where(before, lower_count, jnp.where(after, upper_count, own_count))
    place = key_slot - jnp.where(before, reach - nodes, jnp.where(after, reach + nodes, reach))
    live = jnp.where(place < limit, 1, 0)
    offset = iota((half, window), 1) - iota((half, window), 0)
    in_window = (offset >= 0) & (offset <= 2 * reach)
    l_pb0.wait()
    l_pb1.wait()
    last = [pb_v[i, pl.ds(2 * reach * local_heads, local_heads), :].T for i in range(2)]

    def window_bias(h):
        for i in range(2):
            turned = pb_v[i, pl.ds(h, 2 * reach, stride=local_heads), :].T
            wide = jnp.concatenate([turned, jnp.zeros((half, window - 2 * reach), F32)], 1)
            skewed = pltpu.roll(wide, 0, 1, stride=1, stride_axis=0)
            final = last[i][:, h : h + 1]
            skewed = jnp.where(offset == 2 * reach, final, skewed)
            usable = in_window & (
                (live[:, i * half : i * half + window] > 0) | (offset == reach)
            )
            bd[h // 2, i, h % 2 * half : (h % 2 + 1) * half] = jnp.where(usable, skewed, NEGATIVE)

    def widen(rows):
        extf[rows, :] = ext[rows, :].astype(F32)

    def arrive(k):
        for which in range(2):
            halo[2 * k + which].wait_recv()
            passing[2 * k + which].start()
        for which in range(2):
            widen(ring_rows(toward, which * (grid_rows // 2) + starts[k], sizes[k]))

    def arrive_passed(k):
        for which in range(2):
            passed[2 * k + which].wait_recv()
            widen(ring_rows(beyond, which * (grid_rows // 2) + starts[k], sizes[k]))

    blocks = half // BLOCK
    block_rows = 16 * BLOCK
    row = iota((block_rows, block_rows), 0)
    column = iota((block_rows, block_rows), 1)
    same = ((row & (BLOCK - 1)) == (column & (BLOCK - 1))) & (column < edges * BLOCK)
    apart[...] = jnp.where(same, 0.0, NEGATIVE)
    lane = iota((block_rows, LANES), 1)
    edge_of_row = iota((block_rows, LANES), 0) >> 4
    mark = (lane < 48) & ((lane & 15) == edge_of_row)
    marks[...] = jnp.where(mark, 1.0, 0.0).astype(BF16)
    v_s[...] = jnp.ones(v_s.shape, BF16)
    for block in range(blocks):
        unused = slice(block * block_rows + edges * BLOCK, (block + 1) * block_rows)
        g[unused, :] = jnp.zeros((block_rows - edges * BLOCK, LANES), F32)
    l_edge.wait()
    for h in range(local_heads):
        window_bias(h)
    for k in range(CHUNKS):
        widen(ring_rows(band, 2 * starts[k], 2 * sizes[k]))
        when(has_toward, lambda k=k: arrive(k))
        if k > 0:
            when(has_beyond, lambda k=k: arrive_passed(k - 1))
    for copy in exchange:
        copy.wait()
    when(has_beyond, lambda: arrive_passed(CHUNKS - 1))

    def gather(block):
        for edge in range(edges):
            found = []
            for n in range(BLOCK):
                row = edge_s[edge, block * BLOCK + n] & (RING * grid_rows - 1)
                found.append(extf[pl.ds(row, 1), :])
            for n in range(BLOCK):
                g[pl.ds(block * block_rows + edge * BLOCK + n, 1), :] = found[n]

    ones = jnp.ones((block_rows, LANES), BF16)
    quarter = half // 2
    eighth = quarter // 2
    sixteenth = eighth // 2
    parts = (
        lambda which: pl.ds(pl.multiple_of(which * eighth, 16), eighth),
        lambda which: pl.ds(pl.multiple_of(quarter + which * sixteenth, 16), sixteenth),
        lambda which: pl.ds(quarter + eighth, eighth),
    )

    def window_copy(section, which, n):
        rows = parts[section](which)
        return remote(
            nx.at[1 + core, rows], nx.at[3 * other, rows],
            hs_sem.at[2 * section + n], hr_sem.at[3 * other + section], mesh_id(toward, which),
        )

    sends = [
        window_copy(section, which, n) for section in range(3) for n, which in enumerate((core, other))
    ]
    to_sibling = [
        remote(
            lat.at[core, pl.ds(n * quarter, quarter)], lat.at[core, pl.ds(n * quarter, quarter)],
            ls_sem.at[n], lr_sem.at[n], mesh_id(band, other),
        )
        for n in range(2)
    ]
    from_sibling = [
        remote(
            lat.at[other, pl.ds(n * quarter, quarter)], lat.at[other, pl.ds(n * quarter, quarter)],
            ls_sem.at[n], lr_sem.at[n], mesh_id(band, other),
        )
        for n in range(2)
    ]
    handed = []
    for d in range(2):
        for section in range(2):
            here = nx.at[3 * d, parts[section](core)]
            handed.append(
                remote(
                    here, here, ks_sem.at[2 * d + section], kr_sem.at[2 * d + section],
                    mesh_id(band, other),
                )
            )

    def landed(d, section):
        here = nx.at[3 * d, parts[section](core)]
        remote(
            here, here, hs_sem.at[2 * section], hr_sem.at[3 * d + section], mesh_id(toward, core)
        ).wait_recv()

    def hand(d):
        for section in range(2):
            landed(d, section)
            handed[2 * d + section].start()

    def all_here(d):
        landed(d, 2)
        for section in range(2):
            handed[2 * d + section].wait_recv()

    def attend(block):
        rows = slice(block * BLOCK, (block + 1) * BLOCK)
        near = g[block * block_rows : (block + 1) * block_rows, :].astype(BF16)
        asked = jnp.concatenate(
            [qk[s, :, rows, :].reshape(local_heads * BLOCK, 2 * LANES) for s in (0, 2)], 0
        )
        scores = nt(asked, jnp.concatenate([near, marks[...]], 1)) + apart[...]
        peak = jnp.max(scores, 1, keepdims=True)
        weights = jnp.exp(scores - peak).astype(BF16)
        mixed = nn(weights, jnp.concatenate([near, ones], 1))
        mixed = (mixed[:, :LANES] * inverse(mixed[:, LANES:])).astype(BF16)
        for h in range(2 * local_heads):
            u_s[rows, h * LANES : (h + 1) * LANES] = mixed[h * BLOCK : (h + 1) * BLOCK]

    l_eo0.wait()
    l_eo1.wait()
    gather(0)
    for block in range(blocks):
        if block + 1 < blocks:
            gather(block + 1)
        attend(block)
    attended = jnp.concatenate(
        [
            nn(u_s[:, pair * 2 * LANES : (pair + 1) * 2 * LANES], vmap[pair])
            for pair in range(2 * pairs)
        ],
        1,
    ).astype(BF16)
    own_mesh = mesh_v[pl.ds(pl.multiple_of(core * half, half), half), :].astype(F32)
    latent = (own_mesh + nn(attended, eo_v[...])).astype(BF16)
    lat[core] = latent
    nx[1 + core] = normalize(latent.astype(F32))
    when(has_toward, lambda: start_all(sends))
    start_all(to_sibling)

    def clear(s):
        nx[s] = jnp.zeros((half, width), BF16)

    when(jnp.logical_not(has_left), lambda: clear(0))
    when(jnp.logical_not(has_right), lambda: clear(3))
    first_head = iota((half, LANES), 1) < HDIM
    step = 512
    steps = gate_v.shape[1] // step

    def keys_values(source, start):
        rows = pl.ds(pl.multiple_of(start, half), half)
        k_s[rows, :] = nn(source, pk_v[...]).astype(BF16)
        values = nn(source, pv_v[...]).astype(BF16)
        for pair in range(pairs):
            v_s[rows, pair * 2 * LANES : pair * 2 * LANES + LANES] = values[
                :, pair * LANES : (pair + 1) * LANES
            ]

    def project(which):
        source = nx[1 + which]
        win_query = nn(source, pq_v[...]).astype(BF16)
        win_query = win_query.astype(F32) * HDIM**-0.5
        for pair in range(pairs):
            both = win_query[:, pair * LANES : (pair + 1) * LANES]
            q_s[which, pair, 0:half, :] = jnp.where(first_head, both, 0.0).astype(BF16)
            q_s[which, pair, half:nodes, :] = jnp.where(first_head, 0.0, both).astype(BF16)
        keys_values(source, (1 + which) * half)
        rows = pl.ds(pl.multiple_of(which * half, half), half)
        for ch in range(steps):
            columns = slice(ch * step, (ch + 1) * step)
            gated = nn(source, gate_v[:, columns])
            raised = nn(source, up_v[:, columns])
            activated = 0.5 * gated * (1.0 + jnp.tanh(0.5 * gated)) * raised
            hid[rows, columns] = activated.astype(BF16)

    for load in (l_pq, l_pk, l_pv, l_gate, l_up, l_down, l_po):
        load.wait()
    project(core)
    for copy in from_sibling:
        copy.wait_recv()
    nx[2 - core] = normalize(lat[other].astype(F32))
    project(other)

    own_keys = slice(half, 3 * half)
    for i in (1, 0):
        if i == 0:
            when(has_right, lambda: hand(1))
        held = slice((1 - i) * half, (3 - i) * half)
        for pair in range(pairs):
            if pair % 2 == 0:
                at = ((1 - i) * pairs + pair) // 2 * width // pairs
                columns = slice(at, at + width // pairs)
                part[:, columns] = nn(hid[...], down_v[:, columns])
            columns = slice(pair * LANES, (pair + 1) * LANES)
            scores = nt(q_s[i, pair], k_s[own_keys, columns]) + bd[pair, i, :, held]
            peak = jnp.max(scores, 1, keepdims=True)
            weights = jnp.exp(scores - peak).astype(BF16)
            peaks[i, pair] = jnp.broadcast_to(peak, (nodes, LANES))
            sums[i, pair] = nn(weights, v_s[own_keys, pair * 2 * LANES : (pair + 1) * 2 * LANES])
    when(has_left, lambda: hand(0))
    results = [None] * 4
    for i in (1, 0):
        when(sides[i], lambda: all_here(i))
        rows = slice(i * half, (i + 1) * half)
        seen = slice(3 * i * half, (3 * i + 1) * half)
        held = slice(2 * i * half, (2 * i + 1) * half)
        keys_values(nx[3 * i], 3 * i * half)
        for pair in range(pairs):
            columns = slice(pair * LANES, (pair + 1) * LANES)
            scores = nt(q_s[i, pair], k_s[seen, columns]) + bd[pair, i, :, held]
            before = peaks[i, pair]
            peak = jnp.maximum(before, jnp.max(scores, 1, keepdims=True))
            weights = jnp.exp(scores - peak).astype(BF16)
            mixed = nn(weights, v_s[seen, pair * 2 * LANES : (pair + 1) * 2 * LANES])
            shrink = jnp.exp(before - peak)
            upper = sums[i, pair, :, 0:LANES] * shrink + mixed[:, :LANES]
            lower = sums[i, pair, :, LANES : 2 * LANES] * shrink + mixed[:, LANES:]
            mixed = upper * inverse(lower)
            wo[rows, columns] = jnp.where(first_head, mixed[:half], mixed[half:]).astype(BF16)
        for n in range(2):
            columns = slice(n * width // 2, (n + 1) * width // 2)
            psend[i, n] = (part[rows, columns] + nn(wo[rows, :], po_v[:, columns])).astype(BF16)
            at = 2 * i + n
            results[at] = remote(
                psend.at[i, n], precv.at[i, n], ps_sem.at[at], pr_sem.at[at], mesh_id(band, other)
            )
            results[at].start()
    for i in (1, 0):
        node = iota((half, width // 2), 0) + i * half
        scale = (node < own_count).astype(F32)
        for n in range(2):
            results[2 * i + n].wait_recv()
            columns = slice(n * width // 2, (n + 1) * width // 2)
            summed = psend[i, n].astype(F32) + precv[i, n].astype(F32)
            total = lat[i, :, columns].astype(F32) + summed
            out[i * half : (i + 1) * half, columns] = (total * scale).astype(BF16)

    def sent(copies):
        for copy in copies:
            copy.wait_send()

    when(has_right, lambda: sent(to_right + handed[2:]))
    when(has_left, lambda: sent(to_left + handed[:2]))
    when(has_toward, lambda: sent(sends + passing))
    sent(to_sibling + results)


def local(
    grid_in, mesh_in, counts, enc_edges, enc_bias, proc_bias, w_embed, enc_query, enc_key,
    enc_value, enc_out, proc_query, proc_key, proc_value, proc_out, mlp_gate, mlp_up, mlp_down,
):
    grid_rows, channels = grid_in.shape
    nodes, width = mesh_in.shape
    local_width = enc_query.shape[1]
    heads = local_width // HDIM
    hidden = mlp_gate.shape[1]
    half = nodes // 2
    edges = enc_edges.shape[0]
    enc_bias = enc_bias.reshape(edges * heads, nodes)
    proc_bias = proc_bias.reshape(-1, nodes)
    anywhere = pl.BlockSpec(memory_space=pl.ANY)
    dma = pltpu.SemaphoreType.DMA
    vmem = pltpu.VMEM
    scratch = [
        pltpu.SMEM(counts.shape, jnp.int32),
        pltpu.SMEM((edges, half), jnp.int32),
        vmem((RING * grid_rows, channels), BF16),
        vmem((RING * grid_rows, channels), F32),
        vmem((nodes, width), BF16),
        vmem((channels, width), BF16),
        vmem((width, local_width), BF16),
        vmem((width, local_width), BF16),
        vmem((width, local_width), BF16),
        vmem((width, width), BF16),
        vmem((width, local_width), BF16),
        vmem((width, local_width), BF16),
        vmem((width, local_width), BF16),
        vmem((local_width, width), BF16),
        vmem((width, hidden), BF16),
        vmem((width, hidden), BF16),
        vmem((hidden, width), BF16),
        vmem((2, 16 * heads, half), F32),
        vmem((2, proc_bias.shape[0], half), F32),
        vmem((heads // 2, 2, 2 * half, 3 * half), F32),
        vmem((3, heads, half, 2 * LANES), BF16),
        vmem((heads, 2 * LANES, LANES), BF16),
        vmem((16 * BLOCK, 16 * BLOCK), F32),
        vmem((16 * BLOCK, LANES), BF16),
        vmem((half * 16, channels), F32),
        vmem((half, 2 * heads * channels), BF16),
        vmem((2, half, width), BF16),
        vmem((4, half, width), BF16),
        vmem((2, heads // 2, nodes, LANES), BF16),
        vmem((2 * nodes, local_width), BF16),
        vmem((2 * nodes, 2 * local_width), BF16),
        vmem((nodes, hidden), BF16),
        vmem((nodes, width), F32),
        vmem((2, heads // 2, nodes, LANES), F32),
        vmem((2, heads // 2, nodes, 2 * LANES), F32),
        vmem((nodes, local_width), BF16),
        vmem((2, 2, half, width // 2), BF16),
        vmem((2, 2, half, width // 2), BF16),
        dma((21,)),
        dma((2 * CHUNKS,)),
        dma((2 * CHUNKS,)),
        dma((2 * CHUNKS,)),
        dma((2 * CHUNKS,)),
        dma((2,)),
        dma((2,)),
        dma((2,)),
        dma((2,)),
        dma((6,)),
        dma((6,)),
        dma((4,)),
        dma((4,)),
        dma((4,)),
        dma((4,)),
    ]
    return pl.pallas_call(
        kernel,
        out_shape=pltpu.VMEM((nodes, width), BF16),
        in_specs=[anywhere] * 18,
        out_specs=pl.BlockSpec(memory_space=pltpu.VMEM),
        scratch_shapes=scratch,
        compiler_params=pltpu.CompilerParams(
            collective_id=0, has_side_effects=True, vmem_limit_bytes=VMEM_BYTES
        ),
        name="encoder_processor",
    )(
        counts, enc_edges, grid_in, mesh_in, enc_bias, proc_bias, w_embed, enc_query, enc_key,
        enc_value, enc_out, proc_query, proc_key, proc_value, proc_out, mlp_gate, mlp_up, mlp_down,
    )


def solution(mesh):
    heads = P(None, "head")
    in_specs = (
        P("band", None), P("band", None), P(), P(None, "band"), P(None, "head", "band"),
        P(None, "head", "band"), P(), heads, heads, heads, P(), heads, heads, heads,
        P("head", None), heads, heads, P("head", None),
    )
    return jax.shard_map(
        local, mesh=mesh, in_specs=in_specs, out_specs=P("band", None), check_vma=False
    )
```
